32 devices in a mesh: elec: 16 (over z, x, core), therm: 2 (over y).
Axes of the slice: x: 2, y: 2, z: 4, core: 2. Of those that a mesh axis runs over, the one named last changes fastest.
Arguments:
- injected_amperage: bfloat16 [1024, 64, 128], P(('elec', 'therm')), may hold values from -6 to 6
- voltage_self_admittance: float32 [1024, 64], P(('elec', 'therm')), may hold values from 1.2 to 2.5
- voltage_coupling_tiles: bfloat16 [1024, 4, 64, 64], P(('elec', 'therm')), may hold values from -0.5 to 0.5
- voltage_partner_tile_ids: int32 [1024, 4], P(('elec', 'therm')), may hold values from 0 to 31
- interface_tiles_per_level: int32 [128, 2], P(('elec', 'therm')), may hold values from 0 to 31
- interface_admittance: bfloat16 [256, 64, 64], P(('elec', 'therm')), may hold values from -0.5 to 0.5
- warmth_receiver_layer: int32 [1024, 1], P(('elec', 'therm')), may hold values from 0 to 1; in each aligned block of 32 rows (0 to 31, 32 to 63, ...) at most 32 rows name the same one
- warmth_receiver_tile: int32 [1024], P(('elec', 'therm')), may hold values from 0 to 31
- warmth_values: bfloat16 [1024, 64, 128], P(('elec', 'therm')), may hold values from -4 to 4
- warmth_self_coefficient: float32 [1024, 64], P(('elec', 'therm')), may hold values from 1 to 3
- warmth_coupling_tiles: bfloat16 [1024, 3, 64, 64], P(('elec', 'therm')), may hold values from -0.4375 to 0.4375
- warmth_partner_tile_ids: int32 [1024, 3], P(('elec', 'therm')), may hold values from 0 to 31
- layer_boundary_couplings: bfloat16 [128, 64, 64], P(('elec', 'therm')), may hold values from -0.4375 to 0.4375
- substance_kind: int32 [1024, 64], P(('elec', 'therm')), may hold values from 0 to 7
- reference_material_kappas: float32 [8], replicated, may hold values from 0.5 to 4
- warmth_storage_per_point: float32 [1024, 64], P(('elec', 'therm')), may hold values from 1 to 4
Outputs:
- voltage_solution: bfloat16 [1024, 64, 128], P(('elec', 'therm'))
- advanced_warmth_values: float32 [1024, 64, 128], P(('elec', 'therm'))
The draws below stay inside these ranges and needn't reach their ends.
Inputs may be any that keep to these rules, and one draw needn't show every extreme that they name: `warmth_receiver_layer`: among the 32 blocks of one device at most 32 name the same owner, and exactly 32 do for some owner. `voltage_partner_tile_ids`: indexes a block of the same device. `interface_tiles_per_level`: indexes a block of the same device. `warmth_receiver_tile`: indexes a thermal block of the owner. `warmth_partner_tile_ids`: indexes a thermal block of the same device.
All inputs are finite; a program needn't handle non-finite values.
Results may differ from the reference program's by a relative error of at most 0.025.
Values may be sent and summed in bfloat16 or wider, within the bound.
No kernel may reach another device: no remote copies, remote signals or barrier semaphores. Data moves between devices by JAX's collectives and lax.ppermute only.
A program may use at most 64 MiB of HBM per device.

```python
import math
import jax
import jax.numpy as jnp
import numpy as np
from jax import lax

TILE_POINT_COUNT = 64
LOAD_REGIMES = 128
EB_DEV = 32
K_LOC = 4
K_T = 3
LEVELS = 4
FACE = 2
SWEEPS = 5
ZB = 2
MATS = 8
UNIT_WARMTH_TILES = 32
VOLTAGE_TILES = 1024
WARMTH_TILES = 1024
CAP = 32
N_ELEC = 16
N_THERM = 2


def plant(result, stream_key, smallest, largest):
    spot = [jax.random.randint(jax.random.fold_in(stream_key, axis), (), 0, length) for axis, length in enumerate(result.shape)]
    widest = result.shape.index(max(result.shape))
    next_to = spot[:widest] + [(spot[widest] + 1) % result.shape[widest]] + spot[widest + 1:]
    return result.at[tuple(spot)].set(smallest).at[tuple(next_to)].set(largest)


def block_levels(stream_key, shape, split, least, top_value):
    def one(position, parts):
        steps = jax.random.uniform(jax.random.fold_in(jax.random.fold_in(stream_key, 6), position), (parts,), jnp.float32, least / len(split), top_value / len(split))
        return jnp.repeat(jnp.exp(steps), shape[position] // parts).reshape((-1,) + (1,) * (len(shape) - position - 1))

    level = one(*split[0])
    for cut in split[1:]:
        level = level * one(*cut)
    return level


def routed_block(stream_key, own, number, rows, amount, top, reach, slope):
    order = jax.random.permutation(stream_key, amount)
    packed, usual = portions_of(amount, rows * top, reach, slope, True), portions_of(amount, rows * top, reach, slope, False)
    places = jnp.arange(amount)

    def named(sizes, rotation):
        used = int((sizes > 0).sum())
        fixed = max(1, used // 4)
        moved = fixed + (places - fixed + rotation * (used - fixed)) % max(1, amount - fixed)
        return jnp.zeros((amount,), jnp.int32).at[order[jnp.where(places < fixed, places, moved)]].set(jnp.asarray(sizes, jnp.int32))

    sizes = jnp.where(number % 4 == 0, named(packed, number // 4), named(usual, number - number // 4 - 1))
    mixed = jax.random.permutation(jax.random.fold_in(own, 3), amount)
    donor, taker = mixed[0:amount // 2 * 2:2], mixed[1:amount // 2 * 2:2]
    room = jnp.minimum(sizes[donor] - 1, reach - sizes[taker]) // 2
    room = jnp.where((donor == order[0]) | (taker == order[0]) | (sizes[taker] == 0), 0, jnp.maximum(room, 0))
    moved = jax.random.randint(jax.random.fold_in(own, 4), (amount // 2,), 0, 1 << 20) % (room + 1)
    sizes = sizes.at[donor].add(-moved).at[taker].add(moved)
    labels = jnp.searchsorted(jnp.cumsum(sizes), jnp.arange(rows * top), side="right").astype(jnp.int32)
    table = labels.reshape(top, rows).T
    table = table[jax.random.permutation(jax.random.fold_in(own, 1), rows)]
    rotation = jax.random.randint(jax.random.fold_in(own, 2), (rows, 1), 0, top)
    return jnp.take_along_axis(table, (jnp.arange(top)[None, :] + rotation) % top, axis=1)


def portions_of(amount, total, most, slope, full):
    loads = [(1 << 20) // math.isqrt(standing ** slope) + 1 for standing in range(1, amount + 1)]
    largest = most if full else min(most, max(-(-total // amount), total * loads[0] // sum(loads)))
    least = 1 if total - largest >= amount - 1 else 0
    given, spare = [largest] + [least] * (amount - 1), total - largest - least * (amount - 1)
    while spare > 0:
        candidates = [i for i in range(1, amount) if given[i] < largest] or [i for i in range(1, amount) if given[i] < most]
        whole, budget = sum([loads[i] for i in candidates]), spare
        for i in candidates:
            addition = min(most - given[i], max(1, budget * loads[i] // whole), spare)
            given[i] = given[i] + addition
            spare = spare - addition
    return np.array(given)


def scatter_about(own_key, extent, deviation, limit, split=(), dtype=jnp.bfloat16):
    values = deviation * jax.random.normal(own_key, extent, jnp.float32)
    if split:
        values = values * block_levels(own_key, extent, split, -0.22, 0.18)
    return jnp.clip(values, -limit, limit).astype(dtype)


def setup_inputs(seed: int = 0) -> dict:
    arg_keys = jax.random.split(jax.random.key(seed), 17)
    injected_amperage = scatter_about(arg_keys[0], (VOLTAGE_TILES, TILE_POINT_COUNT, LOAD_REGIMES), 1.0, 6.0, ((0, 32),))
    voltage_self_admittance = jnp.clip(jnp.exp(math.log(2.5) - 0.73396914 * jax.random.uniform(arg_keys[1], (VOLTAGE_TILES, TILE_POINT_COUNT), jnp.float32) ** block_levels(arg_keys[1], (VOLTAGE_TILES, TILE_POINT_COUNT), ((0, 32),), -0.2, 0.2)), 1.2, 2.5)
    voltage_coupling_tiles = scatter_about(arg_keys[2], (VOLTAGE_TILES, K_LOC, TILE_POINT_COUNT, TILE_POINT_COUNT), (TILE_POINT_COUNT * K_LOC * 16 // 25) ** -0.5, 0.5, ((0, 32),))
    voltage_partner_tile_ids = plant(jax.random.randint(arg_keys[3], (VOLTAGE_TILES, K_LOC), 0, EB_DEV), jax.random.fold_in(arg_keys[3], 1), 0, EB_DEV - 1).astype(jnp.int32)
    interface_tiles_per_level = plant(jax.random.randint(arg_keys[4], (N_ELEC * N_THERM * LEVELS, FACE), 0, EB_DEV), jax.random.fold_in(arg_keys[4], 1), 0, EB_DEV - 1).astype(jnp.int32)
    interface_admittance = scatter_about(arg_keys[5], (N_ELEC * N_THERM * LEVELS * FACE, TILE_POINT_COUNT, TILE_POINT_COUNT), (TILE_POINT_COUNT * K_LOC * 16 // 25) ** -0.5, 0.5, ((0, 32),))
    warmth_receiver_layer_keys = jax.random.split(jax.random.fold_in(arg_keys[6], 1), VOLTAGE_TILES // EB_DEV)
    warmth_receiver_layer_turns = jax.random.permutation(jax.random.fold_in(arg_keys[6], 3), VOLTAGE_TILES // EB_DEV)
    warmth_receiver_layer = jax.vmap(lambda own, number: routed_block(jax.random.fold_in(arg_keys[6], 2), own, number, EB_DEV, N_THERM, 1, CAP, 2))(warmth_receiver_layer_keys, warmth_receiver_layer_turns).reshape((VOLTAGE_TILES, 1))
    warmth_receiver_tile = plant(jax.random.randint(arg_keys[7], (VOLTAGE_TILES,), 0, UNIT_WARMTH_TILES), jax.random.fold_in(arg_keys[7], 1), 0, UNIT_WARMTH_TILES - 1).astype(jnp.int32)
    warmth_values = scatter_about(arg_keys[8], (WARMTH_TILES, TILE_POINT_COUNT, LOAD_REGIMES), 1.0, 4.0, ((0, 32),))
    warmth_self_coefficient = jnp.clip(jnp.exp(math.log(3.0) - 1.0986123 * jax.random.uniform(arg_keys[9], (WARMTH_TILES, TILE_POINT_COUNT), jnp.float32) ** block_levels(arg_keys[9], (WARMTH_TILES, TILE_POINT_COUNT), ((0, 32),), -0.2, 0.2)), 1.0, 3.0)
    warmth_coupling_tiles = scatter_about(arg_keys[10], (WARMTH_TILES, K_T, TILE_POINT_COUNT, TILE_POINT_COUNT), (TILE_POINT_COUNT * K_T) ** -0.5, 0.4375, ((0, 32),))
    warmth_partner_tile_ids = plant(jax.random.randint(arg_keys[11], (WARMTH_TILES, K_T), 0, UNIT_WARMTH_TILES), jax.random.fold_in(arg_keys[11], 1), 0, UNIT_WARMTH_TILES - 1).astype(jnp.int32)
    layer_boundary_couplings = scatter_about(arg_keys[12], (N_ELEC * N_THERM * 2 * ZB, TILE_POINT_COUNT, TILE_POINT_COUNT), (TILE_POINT_COUNT * K_T) ** -0.5, 0.4375, ((0, 32),))
    substance_kind = plant(jax.random.randint(arg_keys[13], (WARMTH_TILES, TILE_POINT_COUNT), 0, MATS), jax.random.fold_in(arg_keys[13], 1), 0, MATS - 1).astype(jnp.int32)
    reference_material_kappas = jnp.clip(jnp.exp(jax.random.uniform(arg_keys[14], (MATS,), jnp.float32, math.log(0.5), math.log(4.0))), 0.5, 4.0)
    warmth_storage_per_point = jnp.clip(jnp.exp(math.log(4.0) - 1.3862944 * jax.random.uniform(arg_keys[15], (WARMTH_TILES, TILE_POINT_COUNT), jnp.float32) ** block_levels(arg_keys[15], (WARMTH_TILES, TILE_POINT_COUNT), ((0, 32),), -0.2, 0.2)), 1.0, 4.0)
    return dict(injected_amperage=injected_amperage, voltage_self_admittance=voltage_self_admittance, voltage_coupling_tiles=voltage_coupling_tiles, voltage_partner_tile_ids=voltage_partner_tile_ids, interface_tiles_per_level=interface_tiles_per_level, interface_admittance=interface_admittance, warmth_receiver_layer=warmth_receiver_layer, warmth_receiver_tile=warmth_receiver_tile, warmth_values=warmth_values, warmth_self_coefficient=warmth_self_coefficient, warmth_coupling_tiles=warmth_coupling_tiles, warmth_partner_tile_ids=warmth_partner_tile_ids, layer_boundary_couplings=layer_boundary_couplings, substance_kind=substance_kind, reference_material_kappas=reference_material_kappas, warmth_storage_per_point=warmth_storage_per_point)


relax_factor = 0.8
time_increment = 0.5


def near_product(operands):
    field_b, near_blocks, near_index = operands
    picked = field_b[near_index]
    return jnp.einsum("rkab,rkbc->rac", near_blocks.astype(jnp.float32), picked.astype(jnp.float32))


def take_rows(field_b, index_rows):
    return field_b[index_rows]


def add_rows(total, index_rows, terms):
    return total.at[index_rows].add(terms)


def electric_apply(field_b, voltage_self_admittance, voltage_coupling_tiles, voltage_partner_tile_ids, interface_tiles_per_level, interface_admittance):
    unit_count_overall = N_ELEC * N_THERM
    near_terms = lax.map(near_product, (field_b, voltage_coupling_tiles, voltage_partner_tile_ids))
    total = voltage_self_admittance[..., None] * field_b.astype(jnp.float32) + near_terms
    outgoing = jax.vmap(take_rows)(field_b, interface_tiles_per_level)
    grid = outgoing.reshape(N_ELEC, N_THERM, LEVELS, FACE, TILE_POINT_COUNT, LOAD_REGIMES)
    pieces = []
    for level_bit in range(LEVELS):
        partner = np.arange(N_ELEC) ^ (1 << level_bit)
        pieces.append(grid[partner, :, level_bit])
    incoming = jnp.stack(pieces, axis=2).reshape(unit_count_overall, LEVELS * FACE, TILE_POINT_COUNT, LOAD_REGIMES)
    face_terms = jnp.einsum("gsab,gsbc->gsac", interface_admittance.astype(jnp.float32), incoming.astype(jnp.float32))
    targets = interface_tiles_per_level.reshape(unit_count_overall, LEVELS * FACE)
    return jax.vmap(add_rows)(total, targets, face_terms)


def reference(injected_amperage, voltage_self_admittance, voltage_coupling_tiles, voltage_partner_tile_ids, interface_tiles_per_level, interface_admittance, warmth_receiver_layer, warmth_receiver_tile, warmth_values, warmth_self_coefficient, warmth_coupling_tiles, warmth_partner_tile_ids, layer_boundary_couplings, substance_kind, reference_material_kappas, warmth_storage_per_point):
    unit_count_overall = N_ELEC * N_THERM
    source = injected_amperage.astype(jnp.float32).reshape(unit_count_overall, EB_DEV, TILE_POINT_COUNT, LOAD_REGIMES)
    diag_e = voltage_self_admittance.reshape(unit_count_overall, EB_DEV, TILE_POINT_COUNT)
    near_e = voltage_coupling_tiles.reshape(unit_count_overall, EB_DEV, K_LOC, TILE_POINT_COUNT, TILE_POINT_COUNT)
    conn_e = voltage_partner_tile_ids.reshape(unit_count_overall, EB_DEV, K_LOC)
    sends = interface_tiles_per_level.reshape(unit_count_overall, LEVELS, FACE)
    faces = interface_admittance.reshape(unit_count_overall, LEVELS * FACE, TILE_POINT_COUNT, TILE_POINT_COUNT)
    potential_f = relax_factor * source / diag_e[..., None]
    for sweep_index in range(SWEEPS - 1):
        field_b = potential_f.astype(jnp.bfloat16)
        image = electric_apply(field_b, diag_e, near_e, conn_e, sends, faces)
        potential_f = potential_f + relax_factor * (source - image) / diag_e[..., None]
    voltage_solution = potential_f.astype(jnp.bfloat16)
    current = electric_apply(voltage_solution, diag_e, near_e, conn_e, sends, faces)
    heat = (voltage_solution.astype(jnp.float32) * current).astype(jnp.bfloat16)

    heat_groups = heat.reshape(N_ELEC, N_THERM * EB_DEV, TILE_POINT_COUNT, LOAD_REGIMES)
    owner_groups = warmth_receiver_layer.reshape(N_ELEC, N_THERM * EB_DEV)
    row_groups = warmth_receiver_tile.reshape(N_ELEC, N_THERM * EB_DEV)

    def collect(operands):
        heat_piece, owner_piece, row_piece = operands
        owner_hit = owner_piece[None, None, :] == jnp.arange(N_THERM)[:, None, None]
        row_hit = row_piece[None, None, :] == jnp.arange(UNIT_WARMTH_TILES)[None, :, None]
        selector = (owner_hit & row_hit).astype(jnp.float32)
        return jnp.einsum("tjr,rbc->tjbc", selector, heat_piece.astype(jnp.float32))

    resistive_dissipation = lax.map(collect, (heat_groups, owner_groups, row_groups)).reshape(unit_count_overall, UNIT_WARMTH_TILES, TILE_POINT_COUNT, LOAD_REGIMES)

    warmth_distribution = warmth_values.astype(jnp.float32).reshape(unit_count_overall, UNIT_WARMTH_TILES, TILE_POINT_COUNT, LOAD_REGIMES)
    pass_along = reference_material_kappas[substance_kind].reshape(unit_count_overall, UNIT_WARMTH_TILES, TILE_POINT_COUNT)
    diffusivity_coefficient = pass_along[..., None] * (1.0 + 0.4 * jnp.tanh(warmth_distribution))
    stream_flow_second = (diffusivity_coefficient * warmth_distribution).astype(jnp.bfloat16)
    near_t = warmth_coupling_tiles.reshape(unit_count_overall, UNIT_WARMTH_TILES, K_T, TILE_POINT_COUNT, TILE_POINT_COUNT)
    conn_t = warmth_partner_tile_ids.reshape(unit_count_overall, UNIT_WARMTH_TILES, K_T)
    diag_t = warmth_self_coefficient.reshape(unit_count_overall, UNIT_WARMTH_TILES, TILE_POINT_COUNT)
    warmth_spread_operator = diag_t[..., None] * stream_flow_second.astype(jnp.float32) + lax.map(near_product, (stream_flow_second, near_t, conn_t))
    flux_grid = stream_flow_second.reshape(N_ELEC, N_THERM, UNIT_WARMTH_TILES, TILE_POINT_COUNT, LOAD_REGIMES)
    zero_rim = jnp.zeros((N_ELEC, 1, ZB, TILE_POINT_COUNT, LOAD_REGIMES), jnp.bfloat16)
    below = jnp.concatenate([zero_rim, flux_grid[:, :-1, UNIT_WARMTH_TILES - ZB:]], axis=1)
    above = jnp.concatenate([flux_grid[:, 1:, :ZB], zero_rim], axis=1)
    slab_grid = layer_boundary_couplings.reshape(N_ELEC, N_THERM, 2 * ZB, TILE_POINT_COUNT, TILE_POINT_COUNT).astype(jnp.float32)
    low_terms = jnp.einsum("etzab,etzbc->etzac", slab_grid[:, :, :ZB], below.astype(jnp.float32))
    high_terms = jnp.einsum("etzab,etzbc->etzac", slab_grid[:, :, ZB:], above.astype(jnp.float32))
    warmth_spread_operator = warmth_spread_operator.reshape(N_ELEC, N_THERM, UNIT_WARMTH_TILES, TILE_POINT_COUNT, LOAD_REGIMES)
    warmth_spread_operator = warmth_spread_operator.at[:, :, :ZB].add(low_terms).at[:, :, UNIT_WARMTH_TILES - ZB:].add(high_terms)
    warmth_spread_operator = warmth_spread_operator.reshape(unit_count_overall, UNIT_WARMTH_TILES, TILE_POINT_COUNT, LOAD_REGIMES)
    warmth_storage = warmth_storage_per_point.reshape(unit_count_overall, UNIT_WARMTH_TILES, TILE_POINT_COUNT)
    advanced_warmth_values = warmth_distribution + time_increment * (resistive_dissipation - warmth_spread_operator) / warmth_storage[..., None]
    return voltage_solution.reshape(VOLTAGE_TILES, TILE_POINT_COUNT, LOAD_REGIMES), advanced_warmth_values.reshape(WARMTH_TILES, TILE_POINT_COUNT, LOAD_REGIMES)
```

```python
import functools

import jax
import jax.numpy as jnp
from jax import lax
from jax.experimental import pallas as pl
from jax.experimental.pallas import tpu as pltpu
from jax.sharding import PartitionSpec as P

SWEEPS = 5
ZB = 2

relax_factor = 0.8
time_increment = 0.5

F32 = jnp.float32
BF16 = jnp.bfloat16
VM = pl.BlockSpec(memory_space=pltpu.VMEM)
SM = pl.BlockSpec(memory_space=pltpu.SMEM)
LIMIT = 24 << 20


def in_vmem(x):
    return pltpu.with_memory_space_constraint(x, pltpu.VMEM)


def call(kernel, outs, args, specs, name, aliases={}, flops=0, bytes_accessed=0):
    args = [
        in_vmem(a) if s is VM and getattr(a, "pinned", True) else a for a, s in zip(args, specs)
    ]
    return pl.pallas_call(
        kernel,
        out_shape=[pltpu.VMEM(s, d) for s, d in outs],
        in_specs=specs,
        out_specs=[VM] * len(outs),
        input_output_aliases=aliases,
        compiler_params=pltpu.CompilerParams(vmem_limit_bytes=LIMIT),
        cost_estimate=pl.CostEstimate(
            flops=flops, bytes_accessed=bytes_accessed, transcendentals=0
        ),
        name=name,
    )(*args)


def from_partner(block, axis, bit):
    count = lax.axis_size(axis)
    route = []
    for low in range(count):
        high = low | 1 << bit
        if high != low and high < count:
            route += [(low, high), (high, low)]
    return lax.ppermute(block, axis, route)


def column(table, row, width):
    return jnp.broadcast_to(table[:, row : row + 1], (table.shape[0], width))


def joined(tiles_ref, row):
    return jnp.concatenate([tiles_ref[row, k] for k in range(tiles_ref.shape[1])], axis=1)


def picked(field_ref, ids_ref, row):
    return jnp.concatenate([field_ref[ids_ref[row, k]] for k in range(ids_ref.shape[1])], axis=0)


def start_kernel(levels, amps, diag, face_ids, scale, first, field, *faces):
    turned = (relax_factor / diag[...]).T
    for i in range(diag.shape[0]):
        s = column(turned, i, scale.shape[2])
        scale[i] = s
        x = s * amps[i].astype(F32)
        first[i] = x
        field[i] = x.astype(BF16)
    for b in range(levels):
        for f in range(face_ids.shape[1]):
            faces[b][f] = field[face_ids[b, f]]


def near_first_kernel(ids, tiles, field, first, scale, packed, state_out, field_out):
    for i in range(ids.shape[0]):
        row = joined(tiles, i)
        packed[i] = row
        image = jnp.dot(row, picked(field, ids, i), preferred_element_type=F32)
        x0 = first[i]
        x = x0 + x0 - relax_factor * field[i].astype(F32) - scale[i] * image
        state_out[i] = x
        field_out[i] = x.astype(BF16)


def near_kernel(ids, packed, field, state, first, scale, state_out, field_out):
    for i in range(ids.shape[0]):
        image = jnp.dot(packed[i], picked(field, ids, i), preferred_element_type=F32)
        x = state[i] + first[i] - relax_factor * field[i].astype(F32) - scale[i] * image
        state_out[i] = x
        field_out[i] = x.astype(BF16)


def face_kernel(levels, face_ids, admittance, scale, *refs):
    incoming, (state_in, field_in, state, field), faces = (
        refs[:levels],
        refs[levels : levels + 4],
        refs[levels + 4 :],
    )
    width = face_ids.shape[1]
    for b in range(levels):
        for f in range(width):
            term = jnp.dot(
                admittance[b * width + f], incoming[b][f], preferred_element_type=F32
            )
            i = face_ids[b, f]
            state[i] = state[i] - scale[i] * term
    for b in range(levels):
        for f in range(width):
            i = face_ids[b, f]
            x = state[i].astype(BF16)
            field[i] = x
            faces[b][f] = x


def heat_slot(layer, tile, i, own, groups, tiles):
    away = layer[i, 0] - own
    away = jnp.where(away < 0, away + groups, away)
    return away * tiles + tile[i]


def heat_kernel(groups, own, layer, tile, ids, packed, field, scale, heat):
    tiles = heat.shape[0] // groups
    heat[...] = jnp.zeros(heat.shape, F32)
    for i in range(ids.shape[0]):
        image = jnp.dot(packed[i], picked(field, ids, i), preferred_element_type=F32)
        v = field[i].astype(F32)
        slot = heat_slot(layer, tile, i, own[0], groups, tiles)
        heat[slot] = heat[slot] + v * (relax_factor / scale[i] * v + image)


def heat_face_kernel(levels, groups, own, layer, tile, face_ids, admittance, field, *refs):
    incoming, (heat_in, heat, sent) = refs[:levels], refs[levels:]
    tiles = heat.shape[0] // groups
    width = face_ids.shape[1]
    for b in range(levels):
        for f in range(width):
            term = jnp.dot(
                admittance[b * width + f], incoming[b][f], preferred_element_type=F32
            )
            i = face_ids[b, f]
            slot = heat_slot(layer, tile, i, own[0], groups, tiles)
            heat[slot] = heat[slot] + field[i].astype(F32) * term
    sent[...] = heat[tiles:].astype(BF16)


def flux_kernel(kappas, kind, warmth, flux):
    kinds = kind[...]
    kappa = jnp.zeros(kinds.shape, F32)
    for m in range(kappas.shape[0]):
        kappa = jnp.where(kinds == m, kappas[m], kappa)
    turned = kappa.T
    for i in range(kind.shape[0]):
        w = warmth[i].astype(F32)
        flux[i] = (column(turned, i, flux.shape[2]) * (1.0 + 0.4 * jnp.tanh(w)) * w).astype(BF16)


def conduction_kernel(ids, tiles, coefficient, storage, edge, warmth, flux, below, above, rest, gain):
    count = ids.shape[0]
    width = flux.shape[2]
    own = coefficient[...].T
    gains = (time_increment / storage[...]).T
    for i in range(count):
        image = jnp.dot(joined(tiles, i), picked(flux, ids, i), preferred_element_type=F32)
        image = image + column(own, i, width) * flux[i].astype(F32)
        if i < ZB:
            image = image + jnp.dot(edge[i], below[i], preferred_element_type=F32)
        if i >= count - ZB:
            z = i - (count - ZB)
            image = image + jnp.dot(edge[ZB + z], above[z], preferred_element_type=F32)
        g = column(gains, i, width)
        gain[i] = g
        rest[i] = warmth[i].astype(F32) - g * image


def final_kernel(shifts, rest, gain, heat, *refs):
    received, out = refs[:shifts], refs[shifts]
    for i in range(out.shape[0]):
        total = heat[i]
        for s in range(shifts):
            total = total + received[s][i].astype(F32)
        out[i] = rest[i] + gain[i] * total


def body(
    injected_amperage,
    voltage_self_admittance,
    voltage_coupling_tiles,
    voltage_partner_tile_ids,
    interface_tiles_per_level,
    interface_admittance,
    warmth_receiver_layer,
    warmth_receiver_tile,
    warmth_values,
    warmth_self_coefficient,
    warmth_coupling_tiles,
    warmth_partner_tile_ids,
    layer_boundary_couplings,
    substance_kind,
    reference_material_kappas,
    warmth_storage_per_point,
):
    blocks, points, regimes = injected_amperage.shape
    tiles = warmth_values.shape[0]
    levels, width = interface_tiles_per_level.shape
    terms = voltage_partner_tile_ids.shape[1]
    groups = lax.axis_size("therm")
    own = lax.axis_index("therm").astype(jnp.int32).reshape(1)
    whole = (blocks, points, regimes)
    warm = (tiles, points, regimes)
    face = (width, points, regimes)
    near_flops = 2 * blocks * terms * points * points * regimes
    face_ids = interface_tiles_per_level

    def exchange(faces):
        received = [None] * levels
        for b in reversed(range(levels)):
            received[b] = from_partner(faces[b], "elec", b)
        return received

    scale, first, field, *faces = call(
        functools.partial(start_kernel, levels),
        [(whole, F32), (whole, F32), (whole, BF16)] + [(face, BF16)] * levels,
        [injected_amperage, voltage_self_admittance, face_ids],
        [VM, VM, SM],
        "start",
    )
    incoming = exchange(faces)

    (flux,) = call(
        flux_kernel,
        [(warm, BF16)],
        [reference_material_kappas, substance_kind, warmth_values],
        [SM, VM, VM],
        "flux",
    )
    up = [(i, i + 1) for i in range(groups - 1)]
    down = [(j, i) for i, j in up]
    below = lax.ppermute(flux[tiles - ZB :], "therm", up)
    above = lax.ppermute(flux[:ZB], "therm", down)

    packed, state, field = call(
        near_first_kernel,
        [((blocks, points, terms * points), BF16), (whole, F32), (whole, BF16)],
        [voltage_partner_tile_ids, voltage_coupling_tiles, field, first, scale],
        [SM, VM, VM, VM, VM],
        "near_first",
        flops=near_flops,
    )
    for sweep_index in range(SWEEPS - 1):
        if sweep_index:
            state, field = call(
                near_kernel,
                [(whole, F32), (whole, BF16)],
                [voltage_partner_tile_ids, packed, field, state, first, scale],
                [SM] + [VM] * 5,
                "near",
                flops=near_flops,
            )
        state, field, *faces = call(
            functools.partial(face_kernel, levels),
            [(whole, F32), (whole, BF16)] + [(face, BF16)] * levels,
            [face_ids, interface_admittance, scale] + incoming + [state, field],
            [SM] + [VM] * (levels + 4),
            "face",
            aliases={levels + 3: 0, levels + 4: 1},
        )
        incoming = exchange(faces)
    voltage_solution = field

    (heat,) = call(
        functools.partial(heat_kernel, groups),
        [((groups * tiles, points, regimes), F32)],
        [
            own,
            warmth_receiver_layer,
            warmth_receiver_tile,
            voltage_partner_tile_ids,
            packed,
            field,
            scale,
        ],
        [SM] * 4 + [VM] * 3,
        "heat",
        flops=near_flops,
    )
    heat, sent = call(
        functools.partial(heat_face_kernel, levels, groups),
        [
            ((groups * tiles, points, regimes), F32),
            (((groups - 1) * tiles, points, regimes), BF16),
        ],
        [own, warmth_receiver_layer, warmth_receiver_tile, face_ids]
        + [interface_admittance, field]
        + incoming
        + [heat],
        [SM] * 4 + [VM] * (levels + 3),
        "heat_face",
        aliases={levels + 6: 0},
    )
    received = []
    for s in range(1, groups):
        route = [(i, (i + s) % groups) for i in range(groups)]
        part = sent[(s - 1) * tiles : s * tiles]
        received.append(lax.ppermute(part, "therm", route))

    rest, gain = call(
        conduction_kernel,
        [(warm, F32), (warm, F32)],
        [
            warmth_partner_tile_ids,
            warmth_coupling_tiles,
            warmth_self_coefficient,
            warmth_storage_per_point,
            layer_boundary_couplings,
            warmth_values,
            flux,
            below,
            above,
        ],
        [SM] + [VM] * 8,
        "conduction",
        flops=near_flops,
    )
    (advanced_warmth_values,) = call(
        functools.partial(final_kernel, groups - 1),
        [(warm, F32)],
        [rest, gain, heat] + received,
        [VM] * (groups + 2),
        "final",
    )
    return (voltage_solution, advanced_warmth_values)


def solution(mesh):
    split = P(("elec", "therm"))
    return jax.shard_map(
        body,
        mesh=mesh,
        in_specs=(split,) * 14 + (P(), split),
        out_specs=(split, split),
        check_vma=False,
    )
```

```python
import functools

import jax
import jax.numpy as jnp
from jax import lax
from jax.experimental import pallas as pl
from jax.experimental.pallas import tpu as pltpu
from jax.sharding import PartitionSpec as P

SWEEPS = 5
ZB = 2

relax_factor = 0.8
time_increment = 0.5

F32 = jnp.float32
BF16 = jnp.bfloat16
I32 = jnp.int32
VM = pl.BlockSpec(memory_space=pltpu.VMEM)
SM = pl.BlockSpec(memory_space=pltpu.SMEM)
HB = pl.BlockSpec(memory_space=pltpu.HBM)
ANY = pl.BlockSpec(memory_space=pl.ANY)
SPACES = {id(VM): pltpu.VMEM, id(HB): pltpu.HBM, id(SM): pltpu.SMEM}
LIMIT = 4 << 20


def call(kernel, outs, ins, name, aliases={}, scratch=(), flops=0, limit=LIMIT):
    args = []
    for x, spec in ins:
        if spec is VM or spec is HB:
            x = pltpu.with_memory_space_constraint(x, SPACES[id(spec)])
        args.append(x)
    return pl.pallas_call(
        kernel,
        out_shape=[SPACES[id(spec)](shape, dtype) for shape, dtype, spec in outs],
        in_specs=[spec for _, spec in ins],
        out_specs=[spec for _, _, spec in outs],
        input_output_aliases=aliases,
        scratch_shapes=scratch,
        compiler_params=pltpu.CompilerParams(vmem_limit_bytes=limit),
        cost_estimate=pl.CostEstimate(flops=flops, bytes_accessed=0, transcendentals=0),
        name=name,
    )(*args)


def on(spec, *arrays):
    return [(x, spec) for x in arrays]


def from_partner(block, axis, bit):
    count = lax.axis_size(axis)
    route = []
    for low in range(count):
        high = low | 1 << bit
        if high != low and high < count:
            route += [(low, high), (high, low)]
    return lax.ppermute(block, axis, route)


def column(table, row, width):
    return jnp.broadcast_to(table[:, row : row + 1], (table.shape[0], width))


def joined(tiles_ref, row):
    return jnp.concatenate([tiles_ref[row, k] for k in range(tiles_ref.shape[1])], axis=1)


def picked(field_ref, ids_ref, row):
    return jnp.concatenate([field_ref[ids_ref[k, row]] for k in range(ids_ref.shape[0])], axis=0)


def start_kernel(levels, amps, diag, tiles, face_ids, *refs):
    small = refs[:3]
    amps_v, tiles_v, scale, field, face_ids_s = refs[3:8]
    small_s, faces = refs[8:11], refs[11 : 11 + levels]
    diag_v, sems = refs[11 + levels :]
    blocks = diag.shape[0]
    parts = 4
    step = blocks // parts
    copies = [
        pltpu.make_async_copy(face_ids, face_ids_s, sems.at[0]),
        pltpu.make_async_copy(diag, diag_v, sems.at[1]),
    ]
    for p in range(parts):
        rows = pl.ds(p * step, step)
        copies.append(pltpu.make_async_copy(amps.at[rows], amps_v.at[rows], sems.at[2 + p]))
    later = [pltpu.make_async_copy(tiles, tiles_v, sems.at[2 + parts])]
    for n, (a, b) in enumerate(zip(small, small_s)):
        later.append(pltpu.make_async_copy(a, b, sems.at[3 + parts + n]))
    for c in copies + later:
        c.start()
    copies[1].wait()
    turned = (relax_factor / diag_v[...]).T
    for p in range(parts):
        copies[2 + p].wait()
        for i in range(p * step, (p + 1) * step):
            s = column(turned, i, scale.shape[2])
            scale[i] = s
            field[i] = (s * amps_v[i].astype(F32)).astype(BF16)
    copies[0].wait()
    for b in range(levels):
        for f in range(face_ids.shape[0]):
            faces[b][f] = field[face_ids_s[f, b]]
    for c in later:
        c.wait()


def near_first_kernel(token, ids, tiles, field, amps, scale, packed, state_out, field_out):
    for i in range(tiles.shape[0]):
        row = joined(tiles, i)
        packed[i] = row
        image = jnp.dot(row, picked(field, ids, i), preferred_element_type=F32)
        a = amps[i].astype(F32)
        s = scale[i]
        x = s * a - relax_factor * field[i].astype(F32) + s * (a - image)
        state_out[i] = x
        field_out[i] = x.astype(BF16)


def near_kernel(ids, packed, field, state, amps, scale, state_out, field_out):
    for i in range(packed.shape[0]):
        image = jnp.dot(packed[i], picked(field, ids, i), preferred_element_type=F32)
        x = state[i] - relax_factor * field[i].astype(F32)
        x = x + scale[i] * (amps[i].astype(F32) - image)
        state_out[i] = x
        field_out[i] = x.astype(BF16)


def face_terms(levels, face_ids, admittance, incoming, terms):
    width = face_ids.shape[0]
    for b in range(levels):
        for f in range(width):
            terms[b * width + f] = jnp.dot(
                admittance[b * width + f], incoming[b][f], preferred_element_type=F32
            )


def in_level_order(refs, order):
    return [refs[order.index(b)] for b in range(len(order))]


def face_kernel(order, token, face_ids, admittance, scale, *refs):
    levels = len(order)
    incoming = in_level_order(refs[:levels], order)
    state, field = refs[levels + 2 : levels + 4]
    faces, terms = refs[levels + 4 : 2 * levels + 4], refs[-1]
    width = face_ids.shape[0]
    face_terms(levels, face_ids, admittance, incoming, terms)
    for b in range(levels):
        for f in range(width):
            i = face_ids[f, b]
            state[i] = state[i] - scale[i] * terms[b * width + f]
    for b in range(levels):
        for f in range(width):
            i = face_ids[f, b]
            x = state[i].astype(BF16)
            field[i] = x
            faces[b][f] = x


def route_kernel(groups, own, layer, tile, face_ids, slot, rows, flag, place):
    blocks, tiles = slot.shape[0], flag.shape[0]
    levels, width = face_ids.shape[1], face_ids.shape[0]
    early_slots = max(tiles - levels * width, 0)
    lane = lax.broadcasted_iota(I32, rows.shape[1:], 1)

    def away(i):
        a = layer[0, i] - own[0]
        return jnp.where(a < 0, a + groups, a)

    def home(i, c):
        slot[i] = tile[i]
        return c

    lax.fori_loop(0, blocks, home, 0)
    for g in range(1, groups):

        def clear(j, c):
            flag[j] = 0
            return c

        def mark(i, c):
            j = tile[i]
            flag[j] = jnp.where(away(i) == g, 1, flag[j])
            return c

        def late(j, c):
            is_late = flag[j] == 2
            place[j] = jnp.where(is_late, c, 0)
            return c + is_late.astype(I32)

        def early(j, c):
            at, behind, row = c
            is_early = flag[j] == 1
            fits = at < early_slots
            pos = jnp.where(fits, at, behind)
            pos = jnp.where(is_early, pos, place[j])
            place[j] = pos
            used = flag[j] > 0
            row = jnp.where((lane == pos) & used, j, row)
            at = at + (is_early & fits).astype(I32)
            behind = behind + (is_early & jnp.logical_not(fits)).astype(I32)
            return at, behind, row

        def assign(i, c):
            slot[i] = jnp.where(away(i) == g, g * tiles + place[tile[i]], slot[i])
            return c

        lax.fori_loop(0, tiles, clear, 0)
        lax.fori_loop(0, blocks, mark, 0)
        for b in range(levels):
            for f in range(width):
                i = face_ids[f, b]
                j = tile[i]
                flag[j] = jnp.where(away(i) == g, 2, flag[j])
        behind = lax.fori_loop(0, tiles, late, early_slots)
        _, _, row = lax.fori_loop(
            0, tiles, early, (0, behind, jnp.zeros(rows.shape[1:], I32))
        )
        lax.fori_loop(0, blocks, assign, 0)
        rows[g - 1] = row.astype(F32).astype(BF16)


def heat_kernel(slot, ids, packed, field, scale, *refs):
    levels = (len(refs) - 2) // 2
    heat, soon = refs[levels], refs[levels + 1]
    groups, spots = soon.shape[0] + 1, soon.shape[1]
    tiles = heat.shape[0] // groups
    heat[...] = jnp.zeros(heat.shape, F32)
    for i in range(packed.shape[0]):
        image = jnp.dot(packed[i], picked(field, ids, i), preferred_element_type=F32)
        v = field[i].astype(F32)
        s = slot[i]
        heat[s] = heat[s] + v * (relax_factor / scale[i] * v + image)
    for g in range(1, groups):
        soon[g - 1] = heat[g * tiles : g * tiles + spots].astype(BF16)


def heat_face_kernel(order, slot, face_ids, admittance, field, *refs):
    levels = len(order)
    incoming = in_level_order(refs[:levels], order)
    heat, late, terms = refs[levels + 1 :]
    groups, spots = late.shape[0] + 1, late.shape[1]
    tiles = heat.shape[0] // groups
    width = face_ids.shape[0]
    face_terms(levels, face_ids, admittance, incoming, terms)
    for b in range(levels):
        for f in range(width):
            i = face_ids[f, b]
            s = slot[i]
            heat[s] = heat[s] + field[i].astype(F32) * terms[b * width + f]
    for g in range(1, groups):
        late[g - 1] = heat[(g + 1) * tiles - spots : (g + 1) * tiles].astype(BF16)


def flux_kernel(token, own, kappas, kind, warmth, rows, flux, packet):
    kinds = kind[...]
    kappa = jnp.zeros(kinds.shape, F32)
    for m in range(kappas.shape[0]):
        kappa = jnp.where(kinds == m, kappas[m], kappa)
    turned = kappa.T
    tiles, points, width = flux.shape
    for i in range(tiles):
        w = warmth[i].astype(F32)
        flux[i] = (column(turned, i, width) * (1.0 + 0.4 * jnp.tanh(w)) * w).astype(BF16)
    first = jnp.where(own[0] == 0, tiles - ZB, 0)
    for z in range(ZB):
        packet[z] = flux[first + z]
    for p in range(0, points, rows.shape[1]):
        packet[ZB, p : p + rows.shape[1]] = rows[0]


def conduction_kernel(
    groups, own, ids, tiles, coefficient, storage, edge, warmth, flux, below, above, heat, rest, gain
):
    count = tiles.shape[0]
    width = flux.shape[2]
    lowest = (own[0] > 0).astype(F32)
    highest = (own[0] < groups - 1).astype(F32)
    diag = coefficient[...].T
    gains = (time_increment / storage[...]).T
    for i in range(count):
        image = jnp.dot(joined(tiles, i), picked(flux, ids, i), preferred_element_type=F32)
        image = image + column(diag, i, width) * flux[i].astype(F32)
        if i < ZB:
            term = jnp.dot(edge[i], below[i], preferred_element_type=F32)
            image = image + lowest * term
        if i >= count - ZB:
            z = i - (count - ZB)
            term = jnp.dot(edge[ZB + z], above[z], preferred_element_type=F32)
            image = image + highest * term
        g = column(gains, i, width)
        gain[i] = g
        rest[i] = warmth[i].astype(F32) - g * image


def early_kernel(shifts, heat, gain, *refs):
    maps, soon = refs[:shifts], refs[shifts : 2 * shifts]
    rest, out, sem = refs[2 * shifts + 1 :]
    tiles = rest.shape[0]
    for i in range(tiles):
        rest[i] = rest[i] + gain[i] * heat[i]
    for g in range(shifts):
        for p in range(soon[g].shape[0]):
            j = maps[g][p]
            rest[j] = rest[j] + gain[j] * soon[g][p].astype(F32)
    whole = pltpu.make_async_copy(rest, out, sem)
    whole.start()
    whole.wait()


def late_kernel(shifts, gain, *refs):
    maps, late = refs[:shifts], refs[shifts : 2 * shifts]
    rest, out, sems = refs[2 * shifts], refs[2 * shifts + 2], refs[2 * shifts + 3]
    spots = late[0].shape[0]
    first = rest.shape[0] - spots
    for g in range(shifts):
        for p in range(spots):
            j = maps[g][first + p]
            rest[j] = rest[j] + gain[j] * late[g][p].astype(F32)
    copies = []
    for g in range(shifts):
        for p in range(spots):
            j = maps[g][first + p]
            copies.append(pltpu.make_async_copy(rest.at[j], out.at[j], sems.at[g * spots + p]))
    for c in copies:
        c.start()
    for c in copies:
        c.wait()


def body(
    injected_amperage,
    voltage_self_admittance,
    voltage_coupling_tiles,
    voltage_partner_tile_ids,
    interface_tiles_per_level,
    interface_admittance,
    warmth_receiver_layer,
    warmth_receiver_tile,
    warmth_values,
    warmth_self_coefficient,
    warmth_coupling_tiles,
    warmth_partner_tile_ids,
    layer_boundary_couplings,
    substance_kind,
    reference_material_kappas,
    warmth_storage_per_point,
):
    blocks, points, regimes = injected_amperage.shape
    tiles = warmth_values.shape[0]
    levels, width = interface_tiles_per_level.shape
    links = voltage_partner_tile_ids.shape[1]
    groups = lax.axis_size("therm")
    shifts = groups - 1
    own = lax.axis_index("therm").astype(I32).reshape(1)
    whole = (blocks, points, regimes)
    warm = (tiles, points, regimes)
    face = (width, points, regimes)
    late_spots = min(levels * width, tiles)
    early_spots = tiles - late_spots
    near_flops = 2 * blocks * links * points * points * regimes
    terms = pltpu.VMEM((levels * width, points, regimes), F32)
    dma = pltpu.SemaphoreType.DMA

    def exchange(faces, order):
        return [from_partner(faces[b], "elec", b) for b in order]

    far_first = list(range(levels))[::-1]
    turned = far_first[-1:] + far_first[:-1]

    amps, tiles_v, scale, field, face_ids, ids, layer, tile, *faces = call(
        functools.partial(start_kernel, levels),
        [
            (whole, BF16, VM),
            (voltage_coupling_tiles.shape, BF16, VM),
            (whole, F32, VM),
            (whole, BF16, VM),
            ((width, levels), I32, SM),
            ((links, blocks), I32, SM),
            ((1, blocks), I32, SM),
            ((blocks,), I32, SM),
        ]
        + [(face, BF16, VM)] * levels,
        on(
            HB,
            injected_amperage,
            voltage_self_admittance,
            voltage_coupling_tiles,
            interface_tiles_per_level.T,
            voltage_partner_tile_ids.T,
            warmth_receiver_layer.T,
            warmth_receiver_tile,
        ),
        "start",
        scratch=[pltpu.VMEM(voltage_self_admittance.shape, F32), dma((10,))],
    )
    order = far_first
    incoming = exchange(faces, order)

    slot, rows = call(
        functools.partial(route_kernel, groups),
        [((blocks,), I32, SM), ((shifts, 16, regimes), BF16, VM)],
        on(SM, own, layer, tile, face_ids),
        "route",
        scratch=[pltpu.SMEM((tiles,), I32), pltpu.SMEM((tiles,), I32)],
    )
    flux, packet = call(
        flux_kernel,
        [(warm, BF16, VM), ((ZB + 1, points, regimes), BF16, VM)],
        on(ANY, scale)
        + on(SM, own, reference_material_kappas)
        + on(VM, substance_kind, warmth_values, rows),
        "flux",
    )
    if groups == 2:
        swap = [(0, 1), (1, 0)]
        got = lax.ppermute(packet, "therm", swap)
        below = above = got
        maps = [got[ZB, 0, :tiles].astype(I32)]
    else:
        up = [(i, i + 1) for i in range(groups - 1)]
        down = [(j, i) for i, j in up]
        below = lax.ppermute(flux[tiles - ZB :], "therm", up)
        above = lax.ppermute(flux[:ZB], "therm", down)
        got = above
    routes = [[(i, (i + s) % groups) for i in range(groups)] for s in range(1, groups)]
    if groups != 2:
        maps = [
            lax.ppermute(rows[s], "therm", routes[s])[0, :tiles].astype(I32)
            for s in range(shifts)
        ]

    packed, state, field = call(
        near_first_kernel,
        [((blocks, points, links * points), BF16, VM), (whole, F32, VM), (whole, BF16, VM)],
        on(ANY, packet) + on(SM, ids) + on(VM, tiles_v, field, amps, scale),
        "near_first",
        flops=near_flops,
    )
    for sweep_index in range(SWEEPS - 1):
        if sweep_index:
            state, field = call(
                near_kernel,
                [(whole, F32, VM), (whole, BF16, VM)],
                on(SM, ids) + on(VM, packed, field, state, amps, scale),
                "near",
                flops=near_flops,
            )
        state, field, *faces = call(
            functools.partial(face_kernel, order),
            [(whole, F32, VM), (whole, BF16, VM)] + [(face, BF16, VM)] * levels,
            on(ANY, got if sweep_index == 1 else scale)
            + on(SM, face_ids)
            + on(VM, interface_admittance, scale, *incoming, state, field),
            "face",
            aliases={levels + 4: 0, levels + 5: 1},
            scratch=[terms],
        )
        if sweep_index < SWEEPS - 2:
            order = turned if sweep_index == 1 else far_first
            incoming = exchange(faces, order)
    voltage_solution = field

    heat, soon, *faces = call(
        heat_kernel,
        [((groups * tiles, points, regimes), F32, VM), ((shifts, early_spots) + warm[1:], BF16, VM)]
        + [(face, BF16, VM)] * levels,
        on(SM, slot, ids) + on(VM, packed, field, scale, *faces),
        "heat",
        aliases={5 + b: 2 + b for b in range(levels)},
        flops=near_flops,
    )
    soon = [lax.ppermute(soon[s], "therm", routes[s]) for s in range(shifts)]
    order = far_first
    incoming = exchange(faces, order)

    rest, gain = call(
        functools.partial(conduction_kernel, groups),
        [(warm, F32, VM), (warm, F32, VM)],
        on(SM, own, warmth_partner_tile_ids.T)
        + on(
            VM,
            warmth_coupling_tiles,
            warmth_self_coefficient,
            warmth_storage_per_point,
            layer_boundary_couplings,
            warmth_values,
            flux,
            below,
            above,
        )
        + on(ANY, heat),
        "conduction",
        flops=near_flops,
    )
    heat, late = call(
        functools.partial(heat_face_kernel, order),
        [((groups * tiles, points, regimes), F32, VM), ((shifts, late_spots) + warm[1:], BF16, VM)],
        on(SM, slot, face_ids) + on(VM, interface_admittance, field, *incoming, heat),
        "heat_face",
        aliases={levels + 4: 0},
        scratch=[terms],
    )
    late = [lax.ppermute(late[s], "therm", routes[s]) for s in range(shifts)]
    rest, out = call(
        functools.partial(early_kernel, shifts),
        [(warm, F32, VM), (warm, F32, HB)],
        on(VM, heat, gain) + on(SM, *maps) + on(VM, *soon, rest),
        "early",
        aliases={2 + 2 * shifts: 0},
        scratch=[dma],
    )
    (advanced_warmth_values,) = call(
        functools.partial(late_kernel, shifts),
        [(warm, F32, HB)],
        on(VM, gain) + on(SM, *maps) + on(VM, *late, rest) + on(HB, out),
        "late",
        aliases={2 + 2 * shifts: 0},
        scratch=[dma((shifts * late_spots,))],
    )
    return (voltage_solution, advanced_warmth_values)


def solution(mesh):
    split = P(("elec", "therm"))
    return jax.shard_map(
        body,
        mesh=mesh,
        in_specs=(split,) * 14 + (P(), split),
        out_specs=(split, split),
        check_vma=False,
    )
```

```python
import functools

import jax
import jax.numpy as jnp
from jax import lax
from jax.experimental import pallas as pl
from jax.experimental.pallas import tpu as pltpu
from jax.sharding import PartitionSpec as P

SWEEPS = 5
ZB = 2

relax_factor = 0.8
time_increment = 0.5

F32 = jnp.float32
BF16 = jnp.bfloat16
I32 = jnp.int32
VM = pl.BlockSpec(memory_space=pltpu.VMEM)
SM = pl.BlockSpec(memory_space=pltpu.SMEM)
HB = pl.BlockSpec(memory_space=pltpu.HBM)
ANY = pl.BlockSpec(memory_space=pl.ANY)
SPACES = {id(VM): pltpu.VMEM, id(HB): pltpu.HBM, id(SM): pltpu.SMEM}
LIMIT = 4 << 20


def call(kernel, outs, ins, name, aliases={}, scratch=(), flops=0, limit=LIMIT):
    args = []
    for x, spec in ins:
        if spec is VM or spec is HB:
            x = pltpu.with_memory_space_constraint(x, SPACES[id(spec)])
        args.append(x)
    return pl.pallas_call(
        kernel,
        out_shape=[SPACES[id(spec)](shape, dtype) for shape, dtype, spec in outs],
        in_specs=[spec for _, spec in ins],
        out_specs=[spec for _, _, spec in outs],
        input_output_aliases=aliases,
        scratch_shapes=scratch,
        compiler_params=pltpu.CompilerParams(vmem_limit_bytes=limit),
        cost_estimate=pl.CostEstimate(flops=flops, bytes_accessed=0, transcendentals=0),
        name=name,
    )(*args)


def on(spec, *arrays):
    return [(x, spec) for x in arrays]


def from_partner(block, axis, bit):
    count = lax.axis_size(axis)
    route = []
    for low in range(count):
        high = low | 1 << bit
        if high != low and high < count:
            route += [(low, high), (high, low)]
    return lax.ppermute(block, axis, route)


def column(table, row, width):
    return jnp.broadcast_to(table[:, row : row + 1], (table.shape[0], width))


def joined(tiles_ref, row):
    return jnp.concatenate([tiles_ref[row, k] for k in range(tiles_ref.shape[1])], axis=1)


def picked(field_ref, ids_ref, row):
    return jnp.concatenate([field_ref[ids_ref[k, row]] for k in range(ids_ref.shape[0])], axis=0)


def start_kernel(levels, amps, diag, face_ids, *refs):
    small = refs[:3]
    amps_v, scale, field, face_ids_s = refs[3:7]
    small_s, faces = refs[7:10], refs[10 : 10 + levels]
    diag_v, sems = refs[10 + levels :]
    blocks = diag.shape[0]
    parts = 4
    step = blocks // parts
    copies = [
        pltpu.make_async_copy(face_ids, face_ids_s, sems.at[0]),
        pltpu.make_async_copy(diag, diag_v, sems.at[1]),
    ]
    for p in range(parts):
        rows = pl.ds(p * step, step)
        copies.append(pltpu.make_async_copy(amps.at[rows], amps_v.at[rows], sems.at[2 + p]))
    later = []
    for n, (a, b) in enumerate(zip(small, small_s)):
        later.append(pltpu.make_async_copy(a, b, sems.at[2 + parts + n]))
    for c in copies + later:
        c.start()
    copies[1].wait()
    turned = (relax_factor / diag_v[...]).T
    for p in range(parts):
        copies[2 + p].wait()
        for i in range(p * step, (p + 1) * step):
            s = column(turned, i, scale.shape[2])
            scale[i] = s
            field[i] = (s * amps_v[i].astype(F32)).astype(BF16)
    copies[0].wait()
    for b in range(levels):
        for f in range(face_ids.shape[0]):
            faces[b][f] = field[face_ids_s[f, b]]
    for c in later:
        c.wait()


def near_first_kernel(ids, tiles, field, amps, scale, packed, state_out, field_out, tiles_v, sems):
    blocks = packed.shape[0]
    step = blocks // sems.shape[0]
    copies = []
    for p in range(0, blocks, step):
        rows = pl.ds(p, step)
        copies.append(
            pltpu.make_async_copy(tiles.at[rows], tiles_v.at[rows], sems.at[p // step])
        )
    for c in copies:
        c.start()
    for i in range(blocks):
        if i % step == 0:
            copies[i // step].wait()
        row = joined(tiles_v, i)
        packed[i] = row
        image = jnp.dot(row, picked(field, ids, i), preferred_element_type=F32)
        a = amps[i].astype(F32)
        s = scale[i]
        x = s * a - relax_factor * field[i].astype(F32) + s * (a - image)
        state_out[i] = x
        field_out[i] = x.astype(BF16)


def near_kernel(ids, packed, field, state, amps, scale, state_out, field_out):
    for i in range(packed.shape[0]):
        image = jnp.dot(packed[i], picked(field, ids, i), preferred_element_type=F32)
        x = state[i] - relax_factor * field[i].astype(F32)
        x = x + scale[i] * (amps[i].astype(F32) - image)
        state_out[i] = x
        field_out[i] = x.astype(BF16)


def face_terms(levels, face_ids, admittance, incoming, terms):
    width = face_ids.shape[0]
    for b in range(levels):
        for f in range(width):
            terms[b * width + f] = jnp.dot(
                admittance[b * width + f], incoming[b][f], preferred_element_type=F32
            )


def in_level_order(refs, order):
    return [refs[order.index(b)] for b in range(len(order))]


def face_kernel(order, token, face_ids, admittance, scale, *refs):
    levels = len(order)
    incoming = in_level_order(refs[:levels], order)
    state, field = refs[levels + 2 : levels + 4]
    faces, terms = refs[levels + 4 : 2 * levels + 4], refs[-1]
    width = face_ids.shape[0]
    face_terms(levels, face_ids, admittance, incoming, terms)
    for b in range(levels):
        for f in range(width):
            i = face_ids[f, b]
            state[i] = state[i] - scale[i] * terms[b * width + f]
    for b in range(levels):
        for f in range(width):
            i = face_ids[f, b]
            x = state[i].astype(BF16)
            field[i] = x
            faces[b][f] = x


def route_kernel(groups, token, own, layer, tile, face_ids, slot, rows, flag, place):
    blocks, tiles = slot.shape[0], flag.shape[0]
    levels, width = face_ids.shape[1], face_ids.shape[0]
    early_slots = max(tiles - levels * width, 0)
    lane = lax.broadcasted_iota(I32, rows.shape[1:], 1)

    def away(i):
        a = layer[0, i] - own[0]
        return jnp.where(a < 0, a + groups, a)

    def home(i, c):
        slot[i] = tile[i]
        return c

    lax.fori_loop(0, blocks, home, 0)
    for g in range(1, groups):

        def clear(j, c):
            flag[j] = 0
            return c

        def mark(i, c):
            j = tile[i]
            flag[j] = jnp.where(away(i) == g, 1, flag[j])
            return c

        def late(j, c):
            is_late = flag[j] == 2
            place[j] = jnp.where(is_late, c, 0)
            return c + is_late.astype(I32)

        def early(j, c):
            at, behind, row = c
            is_early = flag[j] == 1
            fits = at < early_slots
            pos = jnp.where(fits, at, behind)
            pos = jnp.where(is_early, pos, place[j])
            place[j] = pos
            used = flag[j] > 0
            row = jnp.where((lane == pos) & used, j, row)
            at = at + (is_early & fits).astype(I32)
            behind = behind + (is_early & jnp.logical_not(fits)).astype(I32)
            return at, behind, row

        def assign(i, c):
            slot[i] = jnp.where(away(i) == g, g * tiles + place[tile[i]], slot[i])
            return c

        lax.fori_loop(0, tiles, clear, 0)
        lax.fori_loop(0, blocks, mark, 0)
        for b in range(levels):
            for f in range(width):
                i = face_ids[f, b]
                j = tile[i]
                flag[j] = jnp.where(away(i) == g, 2, flag[j])
        behind = lax.fori_loop(0, tiles, late, early_slots)
        _, _, row = lax.fori_loop(
            0, tiles, early, (0, behind, jnp.zeros(rows.shape[1:], I32))
        )
        lax.fori_loop(0, blocks, assign, 0)
        rows[g - 1] = row.astype(F32).astype(BF16)


def heat_kernel(slot, ids, packed, field, scale, *refs):
    levels = (len(refs) - 2) // 2
    heat, soon = refs[levels], refs[levels + 1]
    groups, spots = soon.shape[0] + 1, soon.shape[1]
    tiles = heat.shape[0] // groups
    heat[...] = jnp.zeros(heat.shape, F32)
    for i in range(packed.shape[0]):
        image = jnp.dot(packed[i], picked(field, ids, i), preferred_element_type=F32)
        v = field[i].astype(F32)
        s = slot[i]
        heat[s] = heat[s] + v * (relax_factor / scale[i] * v + image)
    for g in range(1, groups):
        soon[g - 1] = heat[g * tiles : g * tiles + spots].astype(BF16)


def heat_face_kernel(order, slot, face_ids, admittance, field, *refs):
    levels = len(order)
    incoming = in_level_order(refs[:levels], order)
    heat, late, terms = refs[levels + 1 :]
    groups, spots = late.shape[0] + 1, late.shape[1]
    tiles = heat.shape[0] // groups
    width = face_ids.shape[0]
    face_terms(levels, face_ids, admittance, incoming, terms)
    for b in range(levels):
        for f in range(width):
            i = face_ids[f, b]
            s = slot[i]
            heat[s] = heat[s] + field[i].astype(F32) * terms[b * width + f]
    for g in range(1, groups):
        late[g - 1] = heat[(g + 1) * tiles - spots : (g + 1) * tiles].astype(BF16)


def flux_kernel(own, kappas, kind, warmth, rows, flux, packet):
    kinds = kind[...]
    kappa = jnp.zeros(kinds.shape, F32)
    for m in range(kappas.shape[0]):
        kappa = jnp.where(kinds == m, kappas[m], kappa)
    turned = kappa.T
    tiles, points, width = flux.shape
    for i in range(tiles):
        w = warmth[i].astype(F32)
        flux[i] = (column(turned, i, width) * (1.0 + 0.4 * jnp.tanh(w)) * w).astype(BF16)
    first = jnp.where(own[0] == 0, tiles - ZB, 0)
    for z in range(ZB):
        packet[z] = flux[first + z]
    for p in range(0, points, rows.shape[1]):
        packet[ZB, p : p + rows.shape[1]] = rows[0]


def conduction_kernel(
    groups, own, ids, tiles, coefficient, storage, edge, warmth, flux, below, above, heat, rest, gain
):
    count = tiles.shape[0]
    width = flux.shape[2]
    lowest = (own[0] > 0).astype(F32)
    highest = (own[0] < groups - 1).astype(F32)
    diag = coefficient[...].T
    gains = (time_increment / storage[...]).T
    for i in range(count):
        image = jnp.dot(joined(tiles, i), picked(flux, ids, i), preferred_element_type=F32)
        image = image + column(diag, i, width) * flux[i].astype(F32)
        if i < ZB:
            term = jnp.dot(edge[i], below[i], preferred_element_type=F32)
            image = image + lowest * term
        if i >= count - ZB:
            z = i - (count - ZB)
            term = jnp.dot(edge[ZB + z], above[z], preferred_element_type=F32)
            image = image + highest * term
        g = column(gains, i, width)
        gain[i] = g
        rest[i] = warmth[i].astype(F32) - g * image


def early_kernel(shifts, heat, gain, *refs):
    maps, soon = refs[:shifts], refs[shifts : 2 * shifts]
    rest, out, sem = refs[2 * shifts + 1 :]
    tiles = rest.shape[0]
    for i in range(tiles):
        rest[i] = rest[i] + gain[i] * heat[i]
    for g in range(shifts):
        for p in range(soon[g].shape[0]):
            j = maps[g][p]
            rest[j] = rest[j] + gain[j] * soon[g][p].astype(F32)
    whole = pltpu.make_async_copy(rest, out, sem)
    whole.start()
    whole.wait()


def late_kernel(shifts, gain, *refs):
    maps, late = refs[:shifts], refs[shifts : 2 * shifts]
    rest, out, sems = refs[2 * shifts], refs[2 * shifts + 2], refs[2 * shifts + 3]
    spots = late[0].shape[0]
    first = rest.shape[0] - spots
    for g in range(shifts):
        for p in range(spots):
            j = maps[g][first + p]
            rest[j] = rest[j] + gain[j] * late[g][p].astype(F32)
    copies = []
    for g in range(shifts):
        for p in range(spots):
            j = maps[g][first + p]
            copies.append(pltpu.make_async_copy(rest.at[j], out.at[j], sems.at[g * spots + p]))
    for c in copies:
        c.start()
    for c in copies:
        c.wait()


def body(
    injected_amperage,
    voltage_self_admittance,
    voltage_coupling_tiles,
    voltage_partner_tile_ids,
    interface_tiles_per_level,
    interface_admittance,
    warmth_receiver_layer,
    warmth_receiver_tile,
    warmth_values,
    warmth_self_coefficient,
    warmth_coupling_tiles,
    warmth_partner_tile_ids,
    layer_boundary_couplings,
    substance_kind,
    reference_material_kappas,
    warmth_storage_per_point,
):
    blocks, points, regimes = injected_amperage.shape
    tiles = warmth_values.shape[0]
    levels, width = interface_tiles_per_level.shape
    links = voltage_partner_tile_ids.shape[1]
    groups = lax.axis_size("therm")
    shifts = groups - 1
    own = lax.axis_index("therm").astype(I32).reshape(1)
    whole = (blocks, points, regimes)
    warm = (tiles, points, regimes)
    face = (width, points, regimes)
    late_spots = min(levels * width, tiles)
    early_spots = tiles - late_spots
    near_flops = 2 * blocks * links * points * points * regimes
    terms = pltpu.VMEM((levels * width, points, regimes), F32)
    dma = pltpu.SemaphoreType.DMA

    def exchange(faces, order):
        return [from_partner(faces[b], "elec", b) for b in order]

    far_first = list(range(levels))[::-1]
    turned = far_first[-1:] + far_first[:-1]

    amps, scale, field, face_ids, ids, layer, tile, *faces = call(
        functools.partial(start_kernel, levels),
        [
            (whole, BF16, VM),
            (whole, F32, VM),
            (whole, BF16, VM),
            ((width, levels), I32, SM),
            ((links, blocks), I32, SM),
            ((1, blocks), I32, SM),
            ((blocks,), I32, SM),
        ]
        + [(face, BF16, VM)] * levels,
        on(
            HB,
            injected_amperage,
            voltage_self_admittance,
            interface_tiles_per_level.T,
            voltage_partner_tile_ids.T,
            warmth_receiver_layer.T,
            warmth_receiver_tile,
        ),
        "start",
        scratch=[pltpu.VMEM(voltage_self_admittance.shape, F32), dma((9,))],
    )
    order = far_first
    incoming = exchange(faces, order)

    packed, state, field = call(
        near_first_kernel,
        [((blocks, points, links * points), BF16, VM), (whole, F32, VM), (whole, BF16, VM)],
        on(SM, ids) + on(HB, voltage_coupling_tiles) + on(VM, field, amps, scale),
        "near_first",
        scratch=[pltpu.VMEM(voltage_coupling_tiles.shape, BF16), dma((4,))],
        flops=near_flops,
        limit=8 << 20,
    )
    for sweep_index in range(SWEEPS - 1):
        if sweep_index:
            state, field = call(
                near_kernel,
                [(whole, F32, VM), (whole, BF16, VM)],
                on(SM, ids) + on(VM, packed, field, state, amps, scale),
                "near",
                flops=near_flops,
            )
        token = scale
        if sweep_index == 1:
            slot, rows = call(
                functools.partial(route_kernel, groups),
                [((blocks,), I32, SM), ((shifts, 16, regimes), BF16, VM)],
                on(ANY, field) + on(SM, own, layer, tile, face_ids),
                "route",
                scratch=[pltpu.SMEM((tiles,), I32), pltpu.SMEM((tiles,), I32)],
            )
            flux, packet = call(
                flux_kernel,
                [(warm, BF16, VM), ((ZB + 1, points, regimes), BF16, VM)],
                on(SM, own, reference_material_kappas)
                + on(VM, substance_kind, warmth_values, rows),
                "flux",
            )
            token = packet
        if sweep_index == 2:
            if groups == 2:
                swap = [(0, 1), (1, 0)]
                got = lax.ppermute(packet, "therm", swap)
                below = above = got
                maps = [got[ZB, 0, :tiles].astype(I32)]
            else:
                up = [(i, i + 1) for i in range(groups - 1)]
                down = [(j, i) for i, j in up]
                below = lax.ppermute(flux[tiles - ZB :], "therm", up)
                above = lax.ppermute(flux[:ZB], "therm", down)
                got = above
            routes = [[(i, (i + s) % groups) for i in range(groups)] for s in range(1, groups)]
            if groups != 2:
                maps = [
                    lax.ppermute(rows[s], "therm", routes[s])[0, :tiles].astype(I32)
                    for s in range(shifts)
                ]
            token = got
        state, field, *faces = call(
            functools.partial(face_kernel, order),
            [(whole, F32, VM), (whole, BF16, VM)] + [(face, BF16, VM)] * levels,
            on(ANY, token)
            + on(SM, face_ids)
            + on(VM, interface_admittance, scale, *incoming, state, field),
            "face",
            aliases={levels + 4: 0, levels + 5: 1},
            scratch=[terms],
        )
        if sweep_index < SWEEPS - 2:
            order = turned if sweep_index == 1 else far_first
            incoming = exchange(faces, order)
    voltage_solution = field

    heat, soon, *faces = call(
        heat_kernel,
        [((groups * tiles, points, regimes), F32, VM), ((shifts, early_spots) + warm[1:], BF16, VM)]
        + [(face, BF16, VM)] * levels,
        on(SM, slot, ids) + on(VM, packed, field, scale, *faces),
        "heat",
        aliases={5 + b: 2 + b for b in range(levels)},
        flops=near_flops,
    )
    soon = [lax.ppermute(soon[s], "therm", routes[s]) for s in range(shifts)]
    order = far_first
    incoming = exchange(faces, order)

    rest, gain = call(
        functools.partial(conduction_kernel, groups),
        [(warm, F32, VM), (warm, F32, VM)],
        on(SM, own, warmth_partner_tile_ids.T)
        + on(
            VM,
            warmth_coupling_tiles,
            warmth_self_coefficient,
            warmth_storage_per_point,
            layer_boundary_couplings,
            warmth_values,
            flux,
            below,
            above,
        )
        + on(ANY, heat),
        "conduction",
        flops=near_flops,
    )
    heat, late = call(
        functools.partial(heat_face_kernel, order),
        [((groups * tiles, points, regimes), F32, VM), ((shifts, late_spots) + warm[1:], BF16, VM)],
        on(SM, slot, face_ids) + on(VM, interface_admittance, field, *incoming, heat),
        "heat_face",
        aliases={levels + 4: 0},
        scratch=[terms],
    )
    late = [lax.ppermute(late[s], "therm", routes[s]) for s in range(shifts)]
    rest, out = call(
        functools.partial(early_kernel, shifts),
        [(warm, F32, VM), (warm, F32, HB)],
        on(VM, heat, gain) + on(SM, *maps) + on(VM, *soon, rest),
        "early",
        aliases={2 + 2 * shifts: 0},
        scratch=[dma],
    )
    (advanced_warmth_values,) = call(
        functools.partial(late_kernel, shifts),
        [(warm, F32, HB)],
        on(VM, gain) + on(SM, *maps) + on(VM, *late, rest) + on(HB, out),
        "late",
        aliases={2 + 2 * shifts: 0},
        scratch=[dma((shifts * late_spots,))],
    )
    return (voltage_solution, advanced_warmth_values)


def solution(mesh):
    split = P(("elec", "therm"))
    return jax.shard_map(
        body,
        mesh=mesh,
        in_specs=(split,) * 14 + (P(), split),
        out_specs=(split, split),
        check_vma=False,
    )
```

```python
import functools

import jax
import jax.numpy as jnp
from jax import lax
from jax.experimental import pallas as pl
from jax.experimental.pallas import tpu as pltpu
from jax.sharding import PartitionSpec as P

SWEEPS = 5
ZB = 2

relax_factor = 0.8
time_increment = 0.5

F32 = jnp.float32
BF16 = jnp.bfloat16
I32 = jnp.int32
VM = pl.BlockSpec(memory_space=pltpu.VMEM)
SM = pl.BlockSpec(memory_space=pltpu.SMEM)
HB = pl.BlockSpec(memory_space=pltpu.HBM)
ANY = pl.BlockSpec(memory_space=pl.ANY)
SPACES = {id(VM): pltpu.VMEM, id(HB): pltpu.HBM, id(SM): pltpu.SMEM}
LIMIT = 4 << 20


def call(kernel, outs, ins, name, aliases={}, scratch=(), flops=0, limit=LIMIT):
    args = []
    for x, spec in ins:
        if spec is VM or spec is HB:
            x = pltpu.with_memory_space_constraint(x, SPACES[id(spec)])
        args.append(x)
    return pl.pallas_call(
        kernel,
        out_shape=[SPACES[id(spec)](shape, dtype) for shape, dtype, spec in outs],
        in_specs=[spec for _, spec in ins],
        out_specs=[spec for _, _, spec in outs],
        input_output_aliases=aliases,
        scratch_shapes=scratch,
        compiler_params=pltpu.CompilerParams(vmem_limit_bytes=limit),
        cost_estimate=pl.CostEstimate(flops=flops, bytes_accessed=0, transcendentals=0),
        name=name,
    )(*args)


def on(spec, *arrays):
    return [(x, spec) for x in arrays]


def from_partner(block, axis, bit):
    count = lax.axis_size(axis)
    route = []
    for low in range(count):
        high = low | 1 << bit
        if high != low and high < count:
            route += [(low, high), (high, low)]
    return lax.ppermute(block, axis, route)


def column(table, row, width):
    return jnp.broadcast_to(table[:, row : row + 1], (table.shape[0], width))


def joined(tiles_ref, row):
    return jnp.concatenate([tiles_ref[row, k] for k in range(tiles_ref.shape[1])], axis=1)


def picked(field_ref, ids_ref, row):
    return jnp.concatenate([field_ref[ids_ref[k, row]] for k in range(ids_ref.shape[0])], axis=0)


def start_kernel(levels, amps, diag, face_ids, *refs):
    small = refs[:3]
    amps_v, scale, field, face_ids_s = refs[3:7]
    small_s, faces = refs[7:10], refs[10 : 10 + levels]
    diag_v, sems = refs[10 + levels :]
    blocks = diag.shape[0]
    parts = 4
    step = blocks // parts
    copies = [
        pltpu.make_async_copy(face_ids, face_ids_s, sems.at[0]),
        pltpu.make_async_copy(diag, diag_v, sems.at[1]),
    ]
    for p in range(parts):
        rows = pl.ds(p * step, step)
        copies.append(pltpu.make_async_copy(amps.at[rows], amps_v.at[rows], sems.at[2 + p]))
    later = []
    for n, (a, b) in enumerate(zip(small, small_s)):
        later.append(pltpu.make_async_copy(a, b, sems.at[2 + parts + n]))
    for c in copies + later:
        c.start()
    copies[1].wait()
    turned = (relax_factor / diag_v[...]).T
    for p in range(parts):
        copies[2 + p].wait()
        for i in range(p * step, (p + 1) * step):
            s = column(turned, i, scale.shape[2])
            scale[i] = s
            field[i] = (s * amps_v[i].astype(F32)).astype(BF16)
    copies[0].wait()
    for b in range(levels):
        for f in range(face_ids.shape[0]):
            faces[b][f] = field[face_ids_s[f, b]]
    for c in later:
        c.wait()


def route(groups, layer, tile, face_ids, slot, rows, flag, place):
    own = lax.axis_index("therm")
    blocks, tiles = slot.shape[0], flag.shape[0]
    levels, width = face_ids.shape[1], face_ids.shape[0]
    early_slots = max(tiles - levels * width, 0)
    lane = lax.broadcasted_iota(I32, rows.shape[1:], 1)

    def away(i):
        a = layer[0, i] - own
        return jnp.where(a < 0, a + groups, a)

    def home(i, c):
        slot[i] = tile[i]
        return c

    lax.fori_loop(0, blocks, home, 0)
    for g in range(1, groups):

        def clear(j, c):
            flag[j] = 0
            return c

        def mark(i, c):
            j = tile[i]
            flag[j] = jnp.where(away(i) == g, 1, flag[j])
            return c

        def late(j, c):
            is_late = flag[j] == 2
            place[j] = jnp.where(is_late, c, 0)
            return c + is_late.astype(I32)

        def early(j, c):
            at, behind, row = c
            is_early = flag[j] == 1
            fits = at < early_slots
            pos = jnp.where(fits, at, behind)
            pos = jnp.where(is_early, pos, place[j])
            place[j] = pos
            used = flag[j] > 0
            row = jnp.where((lane == pos) & used, j, row)
            at = at + (is_early & fits).astype(I32)
            behind = behind + (is_early & jnp.logical_not(fits)).astype(I32)
            return at, behind, row

        def assign(i, c):
            slot[i] = jnp.where(away(i) == g, g * tiles + place[tile[i]], slot[i])
            return c

        lax.fori_loop(0, tiles, clear, 0)
        lax.fori_loop(0, blocks, mark, 0)
        for b in range(levels):
            for f in range(width):
                i = face_ids[f, b]
                j = tile[i]
                flag[j] = jnp.where(away(i) == g, 2, flag[j])
        behind = lax.fori_loop(0, tiles, late, early_slots)
        _, _, row = lax.fori_loop(
            0, tiles, early, (0, behind, jnp.zeros(rows.shape[1:], I32))
        )
        lax.fori_loop(0, blocks, assign, 0)
        rows[g - 1] = row.astype(F32).astype(BF16)


def first_kernel(groups, ids, layer, tile, face_ids, tiles, warmth, kind, field, amps, scale, *refs):
    packed, state_out, field_out, warmth_v, kind_v, slot, rows = refs[:7]
    tiles_v, flag, place, sems, later_sems = refs[7:]
    blocks = packed.shape[0]
    step = blocks // sems.shape[0]
    copies = []
    later = [
        pltpu.make_async_copy(warmth, warmth_v, later_sems.at[0]),
        pltpu.make_async_copy(kind, kind_v, later_sems.at[1]),
    ]
    for p in range(0, blocks, step):
        part = pl.ds(p, step)
        copies.append(
            pltpu.make_async_copy(tiles.at[part], tiles_v.at[part], sems.at[p // step])
        )
    for c in copies + later:
        c.start()
    route(groups, layer, tile, face_ids, slot, rows, flag, place)
    for i in range(blocks):
        if i % step == 0:
            copies[i // step].wait()
        row = joined(tiles_v, i)
        packed[i] = row
        image = jnp.dot(row, picked(field, ids, i), preferred_element_type=F32)
        a = amps[i].astype(F32)
        s = scale[i]
        x = s * a - relax_factor * field[i].astype(F32) + s * (a - image)
        state_out[i] = x
        field_out[i] = x.astype(BF16)
    for c in later:
        c.wait()


def near_kernel(ids, packed, field, state, amps, scale, state_out, field_out):
    for i in range(packed.shape[0]):
        image = jnp.dot(packed[i], picked(field, ids, i), preferred_element_type=F32)
        x = state[i] - relax_factor * field[i].astype(F32)
        x = x + scale[i] * (amps[i].astype(F32) - image)
        state_out[i] = x
        field_out[i] = x.astype(BF16)


def face_terms(levels, face_ids, admittance, incoming, terms):
    width = face_ids.shape[0]
    for b in range(levels):
        for f in range(width):
            terms[b * width + f] = jnp.dot(
                admittance[b * width + f], incoming[b][f], preferred_element_type=F32
            )


def in_level_order(refs, order):
    return [refs[order.index(b)] for b in range(len(order))]


def face_kernel(order, token, face_ids, admittance, scale, *refs):
    levels = len(order)
    incoming = in_level_order(refs[:levels], order)
    state, field = refs[levels + 2 : levels + 4]
    faces, terms = refs[levels + 4 : 2 * levels + 4], refs[-1]
    width = face_ids.shape[0]
    face_terms(levels, face_ids, admittance, incoming, terms)
    for b in range(levels):
        for f in range(width):
            i = face_ids[f, b]
            state[i] = state[i] - scale[i] * terms[b * width + f]
    for b in range(levels):
        for f in range(width):
            i = face_ids[f, b]
            x = state[i].astype(BF16)
            field[i] = x
            faces[b][f] = x


def heat_kernel(slot, ids, packed, field, scale, *refs):
    levels = (len(refs) - 2) // 2
    heat, soon = refs[levels], refs[levels + 1]
    groups, spots = soon.shape[0] + 1, soon.shape[1]
    tiles = heat.shape[0] // groups
    heat[...] = jnp.zeros(heat.shape, F32)
    for i in range(packed.shape[0]):
        image = jnp.dot(packed[i], picked(field, ids, i), preferred_element_type=F32)
        v = field[i].astype(F32)
        s = slot[i]
        heat[s] = heat[s] + v * (relax_factor / scale[i] * v + image)
    for g in range(1, groups):
        soon[g - 1] = heat[g * tiles : g * tiles + spots].astype(BF16)


def heat_face_kernel(order, slot, face_ids, admittance, field, *refs):
    levels = len(order)
    incoming = in_level_order(refs[:levels], order)
    heat, late, terms = refs[levels + 1 :]
    groups, spots = late.shape[0] + 1, late.shape[1]
    tiles = heat.shape[0] // groups
    width = face_ids.shape[0]
    face_terms(levels, face_ids, admittance, incoming, terms)
    for b in range(levels):
        for f in range(width):
            i = face_ids[f, b]
            s = slot[i]
            heat[s] = heat[s] + field[i].astype(F32) * terms[b * width + f]
    for g in range(1, groups):
        late[g - 1] = heat[(g + 1) * tiles - spots : (g + 1) * tiles].astype(BF16)


def flux_kernel(token, kappas, kind, warmth, rows, flux, packet):
    kinds = kind[...]
    kappa = jnp.zeros(kinds.shape, F32)
    for m in range(kappas.shape[0]):
        kappa = jnp.where(kinds == m, kappas[m], kappa)
    turned = kappa.T
    tiles, points, width = flux.shape
    for i in range(tiles):
        w = warmth[i].astype(F32)
        flux[i] = (column(turned, i, width) * (1.0 + 0.4 * jnp.tanh(w)) * w).astype(BF16)
    first = jnp.where(lax.axis_index("therm") == 0, tiles - ZB, 0)
    for z in range(ZB):
        packet[z] = flux[first + z]
    for p in range(0, points, rows.shape[1]):
        packet[ZB, p : p + rows.shape[1]] = rows[0]


def conduction_kernel(
    groups, ids, tiles, coefficient, storage, edge, warmth, flux, below, above, heat, rest, gain
):
    count = tiles.shape[0]
    width = flux.shape[2]
    own = lax.axis_index("therm")
    lowest = (own > 0).astype(F32)
    highest = (own < groups - 1).astype(F32)
    diag = coefficient[...].T
    gains = (time_increment / storage[...]).T
    for i in range(count):
        image = jnp.dot(joined(tiles, i), picked(flux, ids, i), preferred_element_type=F32)
        image = image + column(diag, i, width) * flux[i].astype(F32)
        if i < ZB:
            term = jnp.dot(edge[i], below[i], preferred_element_type=F32)
            image = image + lowest * term
        if i >= count - ZB:
            z = i - (count - ZB)
            term = jnp.dot(edge[ZB + z], above[z], preferred_element_type=F32)
            image = image + highest * term
        g = column(gains, i, width)
        gain[i] = g
        rest[i] = warmth[i].astype(F32) - g * image


def early_kernel(shifts, heat, gain, *refs):
    maps, soon = refs[:shifts], refs[shifts : 2 * shifts]
    rest, out, sem = refs[2 * shifts + 1 :]
    tiles = rest.shape[0]
    for i in range(tiles):
        rest[i] = rest[i] + gain[i] * heat[i]
    for g in range(shifts):
        for p in range(soon[g].shape[0]):
            j = maps[g][p]
            rest[j] = rest[j] + gain[j] * soon[g][p].astype(F32)
    whole = pltpu.make_async_copy(rest, out, sem)
    whole.start()
    whole.wait()


def late_kernel(shifts, gain, *refs):
    maps, late = refs[:shifts], refs[shifts : 2 * shifts]
    rest, out, sems = refs[2 * shifts], refs[2 * shifts + 2], refs[2 * shifts + 3]
    spots = late[0].shape[0]
    first = rest.shape[0] - spots
    for g in range(shifts):
        for p in range(spots):
            j = maps[g][first + p]
            rest[j] = rest[j] + gain[j] * late[g][p].astype(F32)
    copies = []
    for g in range(shifts):
        for p in range(spots):
            j = maps[g][first + p]
            copies.append(pltpu.make_async_copy(rest.at[j], out.at[j], sems.at[g * spots + p]))
    for c in copies:
        c.start()
    for c in copies:
        c.wait()


def body(
    injected_amperage,
    voltage_self_admittance,
    voltage_coupling_tiles,
    voltage_partner_tile_ids,
    interface_tiles_per_level,
    interface_admittance,
    warmth_receiver_layer,
    warmth_receiver_tile,
    warmth_values,
    warmth_self_coefficient,
    warmth_coupling_tiles,
    warmth_partner_tile_ids,
    layer_boundary_couplings,
    substance_kind,
    reference_material_kappas,
    warmth_storage_per_point,
):
    blocks, points, regimes = injected_amperage.shape
    tiles = warmth_values.shape[0]
    levels, width = interface_tiles_per_level.shape
    links = voltage_partner_tile_ids.shape[1]
    groups = lax.axis_size("therm")
    shifts = groups - 1
    whole = (blocks, points, regimes)
    warm = (tiles, points, regimes)
    face = (width, points, regimes)
    late_spots = min(levels * width, tiles)
    early_spots = tiles - late_spots
    near_flops = 2 * blocks * links * points * points * regimes
    terms = pltpu.VMEM((levels * width, points, regimes), F32)
    dma = pltpu.SemaphoreType.DMA

    def exchange(faces, order):
        return [from_partner(faces[b], "elec", b) for b in order]

    far_first = list(range(levels))[::-1]
    turned = far_first[-1:] + far_first[:-1]

    amps, scale, field, face_ids, ids, layer, tile, *faces = call(
        functools.partial(start_kernel, levels),
        [
            (whole, BF16, VM),
            (whole, F32, VM),
            (whole, BF16, VM),
            ((width, levels), I32, SM),
            ((links, blocks), I32, SM),
            ((1, blocks), I32, SM),
            ((blocks,), I32, SM),
        ]
        + [(face, BF16, VM)] * levels,
        on(
            HB,
            injected_amperage,
            voltage_self_admittance,
            interface_tiles_per_level.T,
            voltage_partner_tile_ids.T,
            warmth_receiver_layer.T,
            warmth_receiver_tile,
        ),
        "start",
        scratch=[pltpu.VMEM(voltage_self_admittance.shape, F32), dma((9,))],
    )
    order = far_first
    incoming = exchange(faces, order)

    packed, state, field, warmth, kind, slot, rows = call(
        functools.partial(first_kernel, groups),
        [
            ((blocks, points, links * points), BF16, VM),
            (whole, F32, VM),
            (whole, BF16, VM),
            (warm, BF16, VM),
            (substance_kind.shape, I32, VM),
            ((blocks,), I32, SM),
            ((shifts, 16, regimes), BF16, VM),
        ],
        on(SM, ids, layer, tile, face_ids)
        + on(HB, voltage_coupling_tiles, warmth_values, substance_kind)
        + on(VM, field, amps, scale),
        "first",
        scratch=[
            pltpu.VMEM(voltage_coupling_tiles.shape, BF16),
            pltpu.SMEM((tiles,), I32),
            pltpu.SMEM((tiles,), I32),
            dma((4,)),
            dma((2,)),
        ],
        flops=near_flops,
        limit=8 << 20,
    )
    for sweep_index in range(SWEEPS - 1):
        if sweep_index:
            state, field = call(
                near_kernel,
                [(whole, F32, VM), (whole, BF16, VM)],
                on(SM, ids) + on(VM, packed, field, state, amps, scale),
                "near",
                flops=near_flops,
            )
        token = scale
        if sweep_index == 1:
            flux, packet = call(
                flux_kernel,
                [(warm, BF16, VM), ((ZB + 1, points, regimes), BF16, VM)],
                on(ANY, field)
                + on(SM, reference_material_kappas)
                + on(VM, kind, warmth, rows),
                "flux",
            )
            token = packet
        if sweep_index == 2:
            if groups == 2:
                swap = [(0, 1), (1, 0)]
                got = lax.ppermute(packet, "therm", swap)
                below = above = got
                maps = [got[ZB, 0, :tiles].astype(I32)]
            else:
                up = [(i, i + 1) for i in range(groups - 1)]
                down = [(j, i) for i, j in up]
                below = lax.ppermute(flux[tiles - ZB :], "therm", up)
                above = lax.ppermute(flux[:ZB], "therm", down)
                got = above
            routes = [[(i, (i + s) % groups) for i in range(groups)] for s in range(1, groups)]
            if groups != 2:
                maps = [
                    lax.ppermute(rows[s], "therm", routes[s])[0, :tiles].astype(I32)
                    for s in range(shifts)
                ]
            token = got
        state, field, *faces = call(
            functools.partial(face_kernel, order),
            [(whole, F32, VM), (whole, BF16, VM)] + [(face, BF16, VM)] * levels,
            on(ANY, token)
            + on(SM, face_ids)
            + on(VM, interface_admittance, scale, *incoming, state, field),
            "face",
            aliases={levels + 4: 0, levels + 5: 1},
            scratch=[terms],
        )
        if sweep_index < SWEEPS - 2:
            order = turned if sweep_index == 1 else far_first
            incoming = exchange(faces, order)
    voltage_solution = field

    heat, soon, *faces = call(
        heat_kernel,
        [((groups * tiles, points, regimes), F32, VM), ((shifts, early_spots) + warm[1:], BF16, VM)]
        + [(face, BF16, VM)] * levels,
        on(SM, slot, ids) + on(VM, packed, field, scale, *faces),
        "heat",
        aliases={5 + b: 2 + b for b in range(levels)},
        flops=near_flops,
    )
    soon = [lax.ppermute(soon[s], "therm", routes[s]) for s in range(shifts)]
    order = far_first
    incoming = exchange(faces, order)

    rest, gain = call(
        functools.partial(conduction_kernel, groups),
        [(warm, F32, VM), (warm, F32, VM)],
        on(SM, warmth_partner_tile_ids.T)
        + on(
            VM,
            warmth_coupling_tiles,
            warmth_self_coefficient,
            warmth_storage_per_point,
            layer_boundary_couplings,
            warmth,
            flux,
            below,
            above,
        )
        + on(ANY, heat),
        "conduction",
        flops=near_flops,
    )
    heat, late = call(
        functools.partial(heat_face_kernel, order),
        [((groups * tiles, points, regimes), F32, VM), ((shifts, late_spots) + warm[1:], BF16, VM)],
        on(SM, slot, face_ids) + on(VM, interface_admittance, field, *incoming, heat),
        "heat_face",
        aliases={levels + 4: 0},
        scratch=[terms],
    )
    late = [lax.ppermute(late[s], "therm", routes[s]) for s in range(shifts)]
    rest, out = call(
        functools.partial(early_kernel, shifts),
        [(warm, F32, VM), (warm, F32, HB)],
        on(VM, heat, gain) + on(SM, *maps) + on(VM, *soon, rest),
        "early",
        aliases={2 + 2 * shifts: 0},
        scratch=[dma],
    )
    (advanced_warmth_values,) = call(
        functools.partial(late_kernel, shifts),
        [(warm, F32, HB)],
        on(VM, gain) + on(SM, *maps) + on(VM, *late, rest) + on(HB, out),
        "late",
        aliases={2 + 2 * shifts: 0},
        scratch=[dma((shifts * late_spots,))],
    )
    return (voltage_solution, advanced_warmth_values)


def solution(mesh):
    split = P(("elec", "therm"))
    return jax.shard_map(
        body,
        mesh=mesh,
        in_specs=(split,) * 14 + (P(), split),
        out_specs=(split, split),
        check_vma=False,
    )
```

```python
import functools

import jax
import jax.numpy as jnp
from jax import lax
from jax.experimental import pallas as pl
from jax.experimental.pallas import tpu as pltpu
from jax.sharding import PartitionSpec as P

SWEEPS = 5
ZB = 2

relax_factor = 0.8
time_increment = 0.5

F32 = jnp.float32
BF16 = jnp.bfloat16
I32 = jnp.int32
VM = pl.BlockSpec(memory_space=pltpu.VMEM)
SM = pl.BlockSpec(memory_space=pltpu.SMEM)
HB = pl.BlockSpec(memory_space=pltpu.HBM)
ANY = pl.BlockSpec(memory_space=pl.ANY)
SPACES = {id(VM): pltpu.VMEM, id(HB): pltpu.HBM, id(SM): pltpu.SMEM}
LIMIT = 4 << 20


def call(kernel, outs, ins, name, aliases={}, scratch=(), flops=0, limit=LIMIT):
    args = []
    for x, spec in ins:
        if spec is VM or spec is HB:
            x = pltpu.with_memory_space_constraint(x, SPACES[id(spec)])
        args.append(x)
    return pl.pallas_call(
        kernel,
        out_shape=[SPACES[id(spec)](shape, dtype) for shape, dtype, spec in outs],
        in_specs=[spec for _, spec in ins],
        out_specs=[spec for _, _, spec in outs],
        input_output_aliases=aliases,
        scratch_shapes=scratch,
        compiler_params=pltpu.CompilerParams(vmem_limit_bytes=limit),
        cost_estimate=pl.CostEstimate(flops=flops, bytes_accessed=0, transcendentals=0),
        name=name,
    )(*args)


def on(spec, *arrays):
    return [(x, spec) for x in arrays]


def from_partner(block, axis, bit):
    count = lax.axis_size(axis)
    route = []
    for low in range(count):
        high = low | 1 << bit
        if high != low and high < count:
            route += [(low, high), (high, low)]
    return lax.ppermute(block, axis, route)


def column(table, row, width):
    return jnp.broadcast_to(table[:, row : row + 1], (table.shape[0], width))


def joined(tiles_ref, row):
    return jnp.concatenate([tiles_ref[row, k] for k in range(tiles_ref.shape[1])], axis=1)


def picked(field_ref, ids_ref, row):
    return jnp.concatenate([field_ref[ids_ref[k, row]] for k in range(ids_ref.shape[0])], axis=0)


def start_kernel(levels, amps, diag, face_ids, *refs):
    small = refs[:3]
    amps_v, scale, field, face_ids_s = refs[3:7]
    small_s, faces = refs[7:10], refs[10 : 10 + levels]
    diag_v, sems = refs[10 + levels :]
    blocks = diag.shape[0]
    parts = 4
    step = blocks // parts
    copies = [
        pltpu.make_async_copy(face_ids, face_ids_s, sems.at[0]),
        pltpu.make_async_copy(diag, diag_v, sems.at[1]),
    ]
    for p in range(parts):
        rows = pl.ds(p * step, step)
        copies.append(pltpu.make_async_copy(amps.at[rows], amps_v.at[rows], sems.at[2 + p]))
    later = []
    for n, (a, b) in enumerate(zip(small, small_s)):
        later.append(pltpu.make_async_copy(a, b, sems.at[2 + parts + n]))
    for c in copies + later:
        c.start()
    copies[1].wait()
    turned = (relax_factor / diag_v[...]).T
    for p in range(parts):
        copies[2 + p].wait()
        for i in range(p * step, (p + 1) * step):
            s = column(turned, i, scale.shape[2])
            scale[i] = s
            field[i] = (s * amps_v[i].astype(F32)).astype(BF16)
    copies[0].wait()
    for b in range(levels):
        for f in range(face_ids.shape[0]):
            faces[b][f] = field[face_ids_s[f, b]]
    for c in later:
        c.wait()


def route(groups, layer, tile, face_ids, slot, rows, flag, place):
    own = lax.axis_index("therm")
    blocks, tiles = slot.shape[0], flag.shape[0]
    levels, width = face_ids.shape[1], face_ids.shape[0]
    early_slots = max(tiles - levels * width, 0)
    lane = lax.broadcasted_iota(I32, rows.shape[1:], 1)

    def away(i):
        a = layer[0, i] - own
        return jnp.where(a < 0, a + groups, a)

    def home(i, c):
        slot[i] = tile[i]
        return c

    lax.fori_loop(0, blocks, home, 0)
    for g in range(1, groups):

        def clear(j, c):
            flag[j] = 0
            return c

        def mark(i, c):
            j = tile[i]
            flag[j] = jnp.where(away(i) == g, 1, flag[j])
            return c

        def late(j, c):
            is_late = flag[j] == 2
            place[j] = jnp.where(is_late, c, 0)
            return c + is_late.astype(I32)

        def early(j, c):
            at, behind, row = c
            is_early = flag[j] == 1
            fits = at < early_slots
            pos = jnp.where(fits, at, behind)
            pos = jnp.where(is_early, pos, place[j])
            place[j] = pos
            used = flag[j] > 0
            row = jnp.where((lane == pos) & used, j, row)
            at = at + (is_early & fits).astype(I32)
            behind = behind + (is_early & jnp.logical_not(fits)).astype(I32)
            return at, behind, row

        def assign(i, c):
            slot[i] = jnp.where(away(i) == g, g * tiles + place[tile[i]], slot[i])
            return c

        lax.fori_loop(0, tiles, clear, 0)
        lax.fori_loop(0, blocks, mark, 0)
        for b in range(levels):
            for f in range(width):
                i = face_ids[f, b]
                j = tile[i]
                flag[j] = jnp.where(away(i) == g, 2, flag[j])
        behind = lax.fori_loop(0, tiles, late, early_slots)
        _, _, row = lax.fori_loop(
            0, tiles, early, (0, behind, jnp.zeros(rows.shape[1:], I32))
        )
        lax.fori_loop(0, blocks, assign, 0)
        rows[g - 1] = row.astype(F32).astype(BF16)


def first_kernel(groups, ids, layer, tile, face_ids, tiles, warmth, kind, field, amps, scale, *refs):
    packed, state_out, field_out, warmth_v, kind_v, slot, rows = refs[:7]
    tiles_v, flag, place, sems, later_sems = refs[7:]
    blocks = packed.shape[0]
    step = blocks // sems.shape[0]
    copies = []
    later = [
        pltpu.make_async_copy(warmth, warmth_v, later_sems.at[0]),
        pltpu.make_async_copy(kind, kind_v, later_sems.at[1]),
    ]
    for p in range(0, blocks, step):
        part = pl.ds(p, step)
        copies.append(
            pltpu.make_async_copy(tiles.at[part], tiles_v.at[part], sems.at[p // step])
        )
    for c in copies + later:
        c.start()
    route(groups, layer, tile, face_ids, slot, rows, flag, place)
    for i in range(blocks):
        if i % step == 0:
            copies[i // step].wait()
        row = joined(tiles_v, i)
        packed[i] = row
        image = jnp.dot(row, picked(field, ids, i), preferred_element_type=F32)
        a = amps[i].astype(F32)
        s = scale[i]
        x = s * a - relax_factor * field[i].astype(F32) + s * (a - image)
        state_out[i] = x
        field_out[i] = x.astype(BF16)
    for c in later:
        c.wait()


def near_kernel(ids, packed, field, state, amps, scale, state_out, field_out):
    for i in range(packed.shape[0]):
        image = jnp.dot(packed[i], picked(field, ids, i), preferred_element_type=F32)
        x = state[i] - relax_factor * field[i].astype(F32)
        x = x + scale[i] * (amps[i].astype(F32) - image)
        state_out[i] = x
        field_out[i] = x.astype(BF16)


def face_terms(levels, face_ids, admittance, incoming, terms):
    width = face_ids.shape[0]
    for b in range(levels):
        for f in range(width):
            terms[b * width + f] = jnp.dot(
                admittance[b * width + f], incoming[b][f], preferred_element_type=F32
            )


def in_level_order(refs, order):
    return [refs[order.index(b)] for b in range(len(order))]


def face_kernel(order, token, face_ids, admittance, scale, *refs):
    levels = len(order)
    incoming = in_level_order(refs[:levels], order)
    state, field = refs[levels + 2 : levels + 4]
    faces, terms = refs[levels + 4 : 2 * levels + 4], refs[-1]
    width = face_ids.shape[0]
    face_terms(levels, face_ids, admittance, incoming, terms)
    for b in range(levels):
        for f in range(width):
            i = face_ids[f, b]
            state[i] = state[i] - scale[i] * terms[b * width + f]
    for b in range(levels):
        for f in range(width):
            i = face_ids[f, b]
            x = state[i].astype(BF16)
            field[i] = x
            faces[b][f] = x


def heat_kernel(slot, ids, packed, field, scale, *refs):
    levels = (len(refs) - 2) // 2
    heat, soon = refs[levels], refs[levels + 1]
    groups, spots = soon.shape[0] + 1, soon.shape[1]
    tiles = heat.shape[0] // groups
    heat[...] = jnp.zeros(heat.shape, F32)
    for i in range(packed.shape[0]):
        image = jnp.dot(packed[i], picked(field, ids, i), preferred_element_type=F32)
        v = field[i].astype(F32)
        s = slot[i]
        heat[s] = heat[s] + v * (relax_factor / scale[i] * v + image)
    for g in range(1, groups):
        soon[g - 1] = heat[g * tiles : g * tiles + spots].astype(BF16)


def heat_face_kernel(order, slot, face_ids, admittance, field, *refs):
    levels = len(order)
    incoming = in_level_order(refs[:levels], order)
    heat, late, terms = refs[levels + 1 :]
    groups, spots = late.shape[0] + 1, late.shape[1]
    tiles = heat.shape[0] // groups
    width = face_ids.shape[0]
    face_terms(levels, face_ids, admittance, incoming, terms)
    for b in range(levels):
        for f in range(width):
            i = face_ids[f, b]
            s = slot[i]
            heat[s] = heat[s] + field[i].astype(F32) * terms[b * width + f]
    for g in range(1, groups):
        late[g - 1] = heat[(g + 1) * tiles - spots : (g + 1) * tiles].astype(BF16)


def kappa_columns(kappas, kind):
    kinds = kind[...]
    kappa = jnp.zeros(kinds.shape, F32)
    for m in range(kappas.shape[0]):
        kappa = jnp.where(kinds == m, kappas[m], kappa)
    return kappa.T


def block_flux(kappa, warmth):
    w = warmth.astype(F32)
    return (kappa * (1.0 + 0.4 * jnp.tanh(w)) * w).astype(BF16)


def packet_kernel(token, kappas, kind, warmth, rows, packet):
    turned = kappa_columns(kappas, kind)
    tiles, points, width = warmth.shape
    sends_top = lax.axis_index("therm") == 0
    for z in range(ZB):
        top = tiles - ZB + z
        kappa = jnp.where(sends_top, column(turned, top, width), column(turned, z, width))
        packet[z] = block_flux(kappa, jnp.where(sends_top, warmth[top], warmth[z]))
    for p in range(0, points, rows.shape[1]):
        packet[ZB, p : p + rows.shape[1]] = rows[0]


def edge_kernel(token, kappas, kind, warmth, first, last):
    turned = kappa_columns(kappas, kind)
    tiles, points, width = warmth.shape
    for z in range(ZB):
        first[z] = block_flux(column(turned, z, width), warmth[z])
        top = tiles - ZB + z
        last[z] = block_flux(column(turned, top, width), warmth[top])


def conduction_kernel(
    groups,
    ids,
    kappas,
    tiles,
    kind,
    coefficient,
    storage,
    edge,
    warmth,
    below,
    above,
    heat,
    rest,
    gain,
    flux,
):
    count = tiles.shape[0]
    width = flux.shape[2]
    turned = kappa_columns(kappas, kind)
    for i in range(count):
        flux[i] = block_flux(column(turned, i, width), warmth[i])
    own = lax.axis_index("therm")
    lowest = (own > 0).astype(F32)
    highest = (own < groups - 1).astype(F32)
    diag = coefficient[...].T
    gains = (time_increment / storage[...]).T
    for i in range(count):
        image = jnp.dot(joined(tiles, i), picked(flux, ids, i), preferred_element_type=F32)
        image = image + column(diag, i, width) * flux[i].astype(F32)
        if i < ZB:
            term = jnp.dot(edge[i], below[i], preferred_element_type=F32)
            image = image + lowest * term
        if i >= count - ZB:
            z = i - (count - ZB)
            term = jnp.dot(edge[ZB + z], above[z], preferred_element_type=F32)
            image = image + highest * term
        g = column(gains, i, width)
        gain[i] = g
        rest[i] = warmth[i].astype(F32) - g * image


def early_kernel(shifts, heat, gain, *refs):
    maps, soon = refs[:shifts], refs[shifts : 2 * shifts]
    rest, out = refs[2 * shifts + 1 : 2 * shifts + 3]
    spots, sem = refs[2 * shifts + 3 : -1], refs[-1]
    tiles = rest.shape[0]
    for i in range(tiles):
        rest[i] = rest[i] + gain[i] * heat[i]
    for g in range(shifts):
        for p in range(soon[g].shape[0]):
            j = maps[g][p]
            rest[j] = rest[j] + gain[j] * soon[g][p].astype(F32)
    whole = pltpu.make_async_copy(rest, out, sem)
    whole.start()
    for g in range(shifts):
        for p in range(spots[g].shape[0]):
            spots[g][p] = maps[g][tiles - spots[g].shape[0] + p]
    whole.wait()


def late_kernel(shifts, gain, *refs):
    maps, late = refs[:shifts], refs[shifts : 2 * shifts]
    rest, out, sems = refs[2 * shifts], refs[2 * shifts + 2], refs[2 * shifts + 3]
    spots = late[0].shape[0]
    for g in range(shifts):
        for p in range(spots):
            j = maps[g][p]
            rest[j] = rest[j] + gain[j] * late[g][p].astype(F32)
    copies = []
    for g in range(shifts):
        for p in range(spots):
            j = maps[g][p]
            copies.append(pltpu.make_async_copy(rest.at[j], out.at[j], sems.at[g * spots + p]))
    for c in copies:
        c.start()
    for c in copies:
        c.wait()


def body(
    injected_amperage,
    voltage_self_admittance,
    voltage_coupling_tiles,
    voltage_partner_tile_ids,
    interface_tiles_per_level,
    interface_admittance,
    warmth_receiver_layer,
    warmth_receiver_tile,
    warmth_values,
    warmth_self_coefficient,
    warmth_coupling_tiles,
    warmth_partner_tile_ids,
    layer_boundary_couplings,
    substance_kind,
    reference_material_kappas,
    warmth_storage_per_point,
):
    blocks, points, regimes = injected_amperage.shape
    tiles = warmth_values.shape[0]
    levels, width = interface_tiles_per_level.shape
    links = voltage_partner_tile_ids.shape[1]
    groups = lax.axis_size("therm")
    shifts = groups - 1
    whole = (blocks, points, regimes)
    warm = (tiles, points, regimes)
    face = (width, points, regimes)
    late_spots = min(levels * width, tiles)
    early_spots = tiles - late_spots
    near_flops = 2 * blocks * links * points * points * regimes
    terms = pltpu.VMEM((levels * width, points, regimes), F32)
    dma = pltpu.SemaphoreType.DMA

    def exchange(faces, order):
        return [from_partner(faces[b], "elec", b) for b in order]

    far_first = list(range(levels))[::-1]
    turned = far_first[-1:] + far_first[:-1]

    amps, scale, field, face_ids, ids, layer, tile, *faces = call(
        functools.partial(start_kernel, levels),
        [
            (whole, BF16, VM),
            (whole, F32, VM),
            (whole, BF16, VM),
            ((width, levels), I32, SM),
            ((links, blocks), I32, SM),
            ((1, blocks), I32, SM),
            ((blocks,), I32, SM),
        ]
        + [(face, BF16, VM)] * levels,
        on(
            HB,
            injected_amperage,
            voltage_self_admittance,
            interface_tiles_per_level.T,
            voltage_partner_tile_ids.T,
            warmth_receiver_layer.T,
            warmth_receiver_tile,
        ),
        "start",
        scratch=[pltpu.VMEM(voltage_self_admittance.shape, F32), dma((9,))],
    )
    order = far_first
    incoming = exchange(faces, order)

    packed, state, field, warmth, kind, slot, rows = call(
        functools.partial(first_kernel, groups),
        [
            ((blocks, points, links * points), BF16, VM),
            (whole, F32, VM),
            (whole, BF16, VM),
            (warm, BF16, VM),
            (substance_kind.shape, I32, VM),
            ((blocks,), I32, SM),
            ((shifts, 16, regimes), BF16, VM),
        ],
        on(SM, ids, layer, tile, face_ids)
        + on(HB, voltage_coupling_tiles, warmth_values, substance_kind)
        + on(VM, field, amps, scale),
        "first",
        scratch=[
            pltpu.VMEM(voltage_coupling_tiles.shape, BF16),
            pltpu.SMEM((tiles,), I32),
            pltpu.SMEM((tiles,), I32),
            dma((4,)),
            dma((2,)),
        ],
        flops=near_flops,
        limit=8 << 20,
    )
    for sweep_index in range(SWEEPS - 1):
        if sweep_index:
            state, field = call(
                near_kernel,
                [(whole, F32, VM), (whole, BF16, VM)],
                on(SM, ids) + on(VM, packed, field, state, amps, scale),
                "near",
                flops=near_flops,
            )
        token = scale
        if sweep_index == 1:
            inputs = (
                on(ANY, field)
                + on(SM, reference_material_kappas)
                + on(VM, kind, warmth)
            )
            if groups == 2:
                (packet,) = call(
                    packet_kernel,
                    [((ZB + 1, points, regimes), BF16, VM)],
                    inputs + on(VM, rows),
                    "packet",
                )
                token = packet
            else:
                low, high = call(
                    edge_kernel,
                    [((ZB, points, regimes), BF16, VM)] * 2,
                    inputs,
                    "edge",
                )
                token = low
        if sweep_index == 2:
            if groups == 2:
                swap = [(0, 1), (1, 0)]
                got = lax.ppermute(packet, "therm", swap)
                below = above = got
                maps = [got[ZB, 0, :tiles].astype(I32)]
            else:
                up = [(i, i + 1) for i in range(groups - 1)]
                down = [(j, i) for i, j in up]
                below = lax.ppermute(high, "therm", up)
                above = lax.ppermute(low, "therm", down)
                got = above
            routes = [[(i, (i + s) % groups) for i in range(groups)] for s in range(1, groups)]
            if groups != 2:
                maps = [
                    lax.ppermute(rows[s], "therm", routes[s])[0, :tiles].astype(I32)
                    for s in range(shifts)
                ]
            token = got
        state, field, *faces = call(
            functools.partial(face_kernel, order),
            [(whole, F32, VM), (whole, BF16, VM)] + [(face, BF16, VM)] * levels,
            on(ANY, token)
            + on(SM, face_ids)
            + on(VM, interface_admittance, scale, *incoming, state, field),
            "face",
            aliases={levels + 4: 0, levels + 5: 1},
            scratch=[terms],
        )
        if sweep_index < SWEEPS - 2:
            order = turned if sweep_index == 1 else far_first
            incoming = exchange(faces, order)
    voltage_solution = field

    heat, soon, *faces = call(
        heat_kernel,
        [((groups * tiles, points, regimes), F32, VM), ((shifts, early_spots) + warm[1:], BF16, VM)]
        + [(face, BF16, VM)] * levels,
        on(SM, slot, ids) + on(VM, packed, field, scale, *faces),
        "heat",
        aliases={5 + b: 2 + b for b in range(levels)},
        flops=near_flops,
    )
    soon = [lax.ppermute(soon[s], "therm", routes[s]) for s in range(shifts)]
    order = far_first
    incoming = exchange(faces, order)

    rest, gain = call(
        functools.partial(conduction_kernel, groups),
        [(warm, F32, VM), (warm, F32, VM)],
        on(SM, warmth_partner_tile_ids.T, reference_material_kappas)
        + on(
            VM,
            warmth_coupling_tiles,
            kind,
            warmth_self_coefficient,
            warmth_storage_per_point,
            layer_boundary_couplings,
            warmth,
            below,
            above,
        )
        + on(ANY, heat),
        "conduction",
        scratch=[pltpu.VMEM(warm, BF16)],
        flops=near_flops,
    )
    heat, late = call(
        functools.partial(heat_face_kernel, order),
        [((groups * tiles, points, regimes), F32, VM), ((shifts, late_spots) + warm[1:], BF16, VM)],
        on(SM, slot, face_ids) + on(VM, interface_admittance, field, *incoming, heat),
        "heat_face",
        aliases={levels + 4: 0},
        scratch=[terms],
    )
    late = [lax.ppermute(late[s], "therm", routes[s]) for s in range(shifts)]
    rest, out, *maps = call(
        functools.partial(early_kernel, shifts),
        [(warm, F32, VM), (warm, F32, HB)] + [((late_spots,), I32, SM)] * shifts,
        on(VM, heat, gain) + on(SM, *maps) + on(VM, *soon, rest),
        "early",
        aliases={2 + 2 * shifts: 0},
        scratch=[dma],
    )
    (advanced_warmth_values,) = call(
        functools.partial(late_kernel, shifts),
        [(warm, F32, HB)],
        on(VM, gain) + on(SM, *maps) + on(VM, *late, rest) + on(HB, out),
        "late",
        aliases={2 + 2 * shifts: 0},
        scratch=[dma((shifts * late_spots,))],
    )
    return (voltage_solution, advanced_warmth_values)


def solution(mesh):
    split = P(("elec", "therm"))
    return jax.shard_map(
        body,
        mesh=mesh,
        in_specs=(split,) * 14 + (P(), split),
        out_specs=(split, split),
        check_vma=False,
    )
```

```python
import functools

import jax
import jax.numpy as jnp
from jax import lax
from jax.experimental import pallas as pl
from jax.experimental.pallas import tpu as pltpu
from jax.sharding import PartitionSpec as P

SWEEPS = 5
ZB = 2

relax_factor = 0.8
time_increment = 0.5

F32 = jnp.float32
BF16 = jnp.bfloat16
I32 = jnp.int32
VM = pl.BlockSpec(memory_space=pltpu.VMEM)
SM = pl.BlockSpec(memory_space=pltpu.SMEM)
HB = pl.BlockSpec(memory_space=pltpu.HBM)
ANY = pl.BlockSpec(memory_space=pl.ANY)
SPACES = {id(VM): pltpu.VMEM, id(HB): pltpu.HBM, id(SM): pltpu.SMEM}
LIMIT = 4 << 20


def call(kernel, outs, ins, name, aliases={}, scratch=(), flops=0, limit=LIMIT):
    args = []
    for x, spec in ins:
        if spec is VM or spec is HB:
            x = pltpu.with_memory_space_constraint(x, SPACES[id(spec)])
        args.append(x)
    return pl.pallas_call(
        kernel,
        out_shape=[SPACES[id(spec)](shape, dtype) for shape, dtype, spec in outs],
        in_specs=[spec for _, spec in ins],
        out_specs=[spec for _, _, spec in outs],
        input_output_aliases=aliases,
        scratch_shapes=scratch,
        compiler_params=pltpu.CompilerParams(vmem_limit_bytes=limit),
        cost_estimate=pl.CostEstimate(flops=flops, bytes_accessed=0, transcendentals=0),
        name=name,
    )(*args)


def on(spec, *arrays):
    return [(x, spec) for x in arrays]


def from_partner(block, axis, bit):
    count = lax.axis_size(axis)
    route = []
    for low in range(count):
        high = low | 1 << bit
        if high != low and high < count:
            route += [(low, high), (high, low)]
    return lax.ppermute(block, axis, route)


def column(table, row, width):
    return jnp.broadcast_to(table[:, row : row + 1], (table.shape[0], width))


def joined(tiles_ref, row):
    return jnp.concatenate([tiles_ref[row, k] for k in range(tiles_ref.shape[1])], axis=1)


def picked(field_ref, ids_ref, row):
    return jnp.concatenate([field_ref[ids_ref[k, row]] for k in range(ids_ref.shape[0])], axis=0)


def start_kernel(levels, amps, diag, face_ids, *refs):
    small = refs[:3]
    amps_v, diag_v, face_ids_s = refs[3:6]
    small_s, faces, sems = refs[6:9], refs[9 : 9 + levels], refs[-1]
    pairs = [(face_ids, face_ids_s), (diag, diag_v), (amps, amps_v)]
    copies = [
        pltpu.make_async_copy(a, b, sems.at[n])
        for n, (a, b) in enumerate(pairs + list(zip(small, small_s)))
    ]
    for c in copies:
        c.start()
    copies[0].wait()
    copies[1].wait()
    scale = relax_factor / diag_v[...]
    rows = lax.broadcasted_iota(I32, scale.shape, 0)
    chosen = []
    for b in range(levels):
        for f in range(face_ids.shape[0]):
            mine = jnp.where(rows == face_ids_s[f, b], scale, 0.0)
            chosen.append(jnp.sum(mine, axis=0, keepdims=True))
    turned = jnp.concatenate(chosen, axis=0).T
    copies[2].wait()
    for b in range(levels):
        for f in range(face_ids.shape[0]):
            s = column(turned, b * face_ids.shape[0] + f, amps.shape[2])
            faces[b][f] = (s * amps_v[face_ids_s[f, b]].astype(F32)).astype(BF16)
    for c in copies[3:]:
        c.wait()


def route(groups, layer, tile, face_ids, slot, rows, flag, place):
    own = lax.axis_index("therm")
    blocks, tiles = slot.shape[0], flag.shape[0]
    levels, width = face_ids.shape[1], face_ids.shape[0]
    early_slots = max(tiles - levels * width, 0)
    lane = lax.broadcasted_iota(I32, rows.shape[1:], 1)

    def away(i):
        a = layer[0, i] - own
        return jnp.where(a < 0, a + groups, a)

    def home(i, c):
        slot[i] = tile[i]
        return c

    lax.fori_loop(0, blocks, home, 0)
    for g in range(1, groups):

        def clear(j, c):
            flag[j] = 0
            return c

        def mark(i, c):
            j = tile[i]
            flag[j] = jnp.where(away(i) == g, 1, flag[j])
            return c

        def late(j, c):
            is_late = flag[j] == 2
            place[j] = jnp.where(is_late, c, 0)
            return c + is_late.astype(I32)

        def early(j, c):
            at, behind, row = c
            is_early = flag[j] == 1
            fits = at < early_slots
            pos = jnp.where(fits, at, behind)
            pos = jnp.where(is_early, pos, place[j])
            place[j] = pos
            used = flag[j] > 0
            row = jnp.where((lane == pos) & used, j, row)
            at = at + (is_early & fits).astype(I32)
            behind = behind + (is_early & jnp.logical_not(fits)).astype(I32)
            return at, behind, row

        def assign(i, c):
            slot[i] = jnp.where(away(i) == g, g * tiles + place[tile[i]], slot[i])
            return c

        lax.fori_loop(0, tiles, clear, 0)
        lax.fori_loop(0, blocks, mark, 0)
        for b in range(levels):
            for f in range(width):
                i = face_ids[f, b]
                j = tile[i]
                flag[j] = jnp.where(away(i) == g, 2, flag[j])
        behind = lax.fori_loop(0, tiles, late, early_slots)
        _, _, row = lax.fori_loop(
            0, tiles, early, (0, behind, jnp.zeros(rows.shape[1:], I32))
        )
        lax.fori_loop(0, blocks, assign, 0)
        rows[g - 1] = row.astype(F32).astype(BF16)


def first_kernel(groups, ids, layer, tile, face_ids, tiles, warmth, kind, amps, diag, *refs):
    packed, state_out, field_out, scale, warmth_v, kind_v, slot, rows = refs[:8]
    tiles_v, field, flag, place, sems, later_sems = refs[8:]
    blocks = packed.shape[0]
    step = blocks // sems.shape[0]
    copies = []
    later = [
        pltpu.make_async_copy(warmth, warmth_v, later_sems.at[0]),
        pltpu.make_async_copy(kind, kind_v, later_sems.at[1]),
    ]
    for p in range(0, blocks, step):
        part = pl.ds(p, step)
        copies.append(
            pltpu.make_async_copy(tiles.at[part], tiles_v.at[part], sems.at[p // step])
        )
    for c in copies + later:
        c.start()
    route(groups, layer, tile, face_ids, slot, rows, flag, place)
    turned = (relax_factor / diag[...]).T
    for i in range(blocks):
        s = column(turned, i, scale.shape[2])
        scale[i] = s
        field[i] = (s * amps[i].astype(F32)).astype(BF16)
    for i in range(blocks):
        if i % step == 0:
            copies[i // step].wait()
        row = joined(tiles_v, i)
        packed[i] = row
        image = jnp.dot(row, picked(field, ids, i), preferred_element_type=F32)
        a = amps[i].astype(F32)
        s = scale[i]
        x = s * a - relax_factor * field[i].astype(F32) + s * (a - image)
        state_out[i] = x
        field_out[i] = x.astype(BF16)
    for c in later:
        c.wait()


def near_kernel(ids, packed, field, state, amps, scale, state_out, field_out):
    for i in range(packed.shape[0]):
        image = jnp.dot(packed[i], picked(field, ids, i), preferred_element_type=F32)
        x = state[i] - relax_factor * field[i].astype(F32)
        x = x + scale[i] * (amps[i].astype(F32) - image)
        state_out[i] = x
        field_out[i] = x.astype(BF16)


def face_terms(levels, face_ids, admittance, incoming, terms):
    width = face_ids.shape[0]
    for b in range(levels):
        for f in range(width):
            terms[b * width + f] = jnp.dot(
                admittance[b * width + f], incoming[b][f], preferred_element_type=F32
            )


def in_level_order(refs, order):
    return [refs[order.index(b)] for b in range(len(order))]


def face_kernel(order, token, face_ids, admittance, scale, *refs):
    levels = len(order)
    incoming = in_level_order(refs[:levels], order)
    terms, faces = refs[-1], refs[-1 - levels : -1]
    state, field = refs[-3 - levels : -1 - levels]
    width = face_ids.shape[0]
    face_terms(levels, face_ids, admittance, incoming, terms)
    for b in range(levels):
        for f in range(width):
            i = face_ids[f, b]
            state[i] = state[i] - scale[i] * terms[b * width + f]
    for b in range(levels):
        for f in range(width):
            i = face_ids[f, b]
            x = state[i].astype(BF16)
            field[i] = x
            faces[b][f] = x


def heat_kernel(spots, slot, ids, packed, field, scale, rows, *refs):
    levels = (len(refs) - 2) // 2
    heat, soon = refs[levels], refs[levels + 1]
    groups, points = soon.shape[0] + 1, heat.shape[1]
    tiles = heat.shape[0] // groups
    heat[...] = jnp.zeros(heat.shape, F32)
    for i in range(packed.shape[0]):
        image = jnp.dot(packed[i], picked(field, ids, i), preferred_element_type=F32)
        v = field[i].astype(F32)
        s = slot[i]
        heat[s] = heat[s] + v * (relax_factor / scale[i] * v + image)
    for g in range(1, groups):
        for p in range(spots):
            soon[g - 1, p * points : (p + 1) * points] = heat[g * tiles + p].astype(BF16)
        soon[g - 1, spots * points :] = rows[g - 1]


def heat_face_kernel(order, slot, face_ids, admittance, field, *refs):
    levels = len(order)
    incoming = in_level_order(refs[:levels], order)
    heat, late, terms = refs[levels + 1 :]
    groups, spots = late.shape[0] + 1, late.shape[1]
    tiles = heat.shape[0] // groups
    width = face_ids.shape[0]
    face_terms(levels, face_ids, admittance, incoming, terms)
    for b in range(levels):
        for f in range(width):
            i = face_ids[f, b]
            s = slot[i]
            heat[s] = heat[s] + field[i].astype(F32) * terms[b * width + f]
    for g in range(1, groups):
        late[g - 1] = heat[(g + 1) * tiles - spots : (g + 1) * tiles].astype(BF16)


def kappa_columns(kappas, kind):
    kinds = kind[...]
    kappa = jnp.zeros(kinds.shape, F32)
    for m in range(kappas.shape[0]):
        kappa = jnp.where(kinds == m, kappas[m], kappa)
    return kappa.T


def block_flux(kappa, warmth):
    w = warmth.astype(F32)
    return (kappa * (1.0 + 0.4 * jnp.tanh(w)) * w).astype(BF16)


def packet_kernel(token, kappas, kind, warmth, packet):
    turned = kappa_columns(kappas, kind)
    tiles, points, width = warmth.shape
    sends_top = lax.axis_index("therm") == 0
    for z in range(ZB):
        top = tiles - ZB + z
        kappa = jnp.where(sends_top, column(turned, top, width), column(turned, z, width))
        packet[z] = block_flux(kappa, jnp.where(sends_top, warmth[top], warmth[z]))


def edge_kernel(token, kappas, kind, warmth, first, last):
    turned = kappa_columns(kappas, kind)
    tiles, points, width = warmth.shape
    for z in range(ZB):
        first[z] = block_flux(column(turned, z, width), warmth[z])
        top = tiles - ZB + z
        last[z] = block_flux(column(turned, top, width), warmth[top])


def conduction_kernel(
    groups,
    ids,
    kappas,
    tiles,
    kind,
    coefficient,
    storage,
    edge,
    warmth,
    below,
    above,
    heat,
    rest,
    gain,
    flux,
):
    count = tiles.shape[0]
    width = flux.shape[2]
    turned = kappa_columns(kappas, kind)
    for i in range(count):
        flux[i] = block_flux(column(turned, i, width), warmth[i])
    own = lax.axis_index("therm")
    lowest = (own > 0).astype(F32)
    highest = (own < groups - 1).astype(F32)
    diag = coefficient[...].T
    gains = (time_increment / storage[...]).T
    for i in range(count):
        image = jnp.dot(joined(tiles, i), picked(flux, ids, i), preferred_element_type=F32)
        image = image + column(diag, i, width) * flux[i].astype(F32)
        if i < ZB:
            term = jnp.dot(edge[i], below[i], preferred_element_type=F32)
            image = image + lowest * term
        if i >= count - ZB:
            z = i - (count - ZB)
            term = jnp.dot(edge[ZB + z], above[z], preferred_element_type=F32)
            image = image + highest * term
        g = column(gains, i, width)
        gain[i] = g
        rest[i] = warmth[i].astype(F32) - g * image


def early_kernel(shifts, heat, gain, *refs):
    maps, soon = refs[:shifts], refs[shifts : 2 * shifts]
    rest, out = refs[2 * shifts + 1 : 2 * shifts + 3]
    spots, sem = refs[2 * shifts + 3 : -1], refs[-1]
    tiles, points = rest.shape[:2]
    for i in range(tiles):
        rest[i] = rest[i] + gain[i] * heat[i]
    for g in range(shifts):
        for p in range(tiles - spots[g].shape[0]):
            j = maps[g][p]
            rest[j] = rest[j] + gain[j] * soon[g][p * points : (p + 1) * points].astype(F32)
    whole = pltpu.make_async_copy(rest, out, sem)
    whole.start()
    for g in range(shifts):
        for p in range(spots[g].shape[0]):
            spots[g][p] = maps[g][tiles - spots[g].shape[0] + p]
    whole.wait()


def late_kernel(shifts, gain, *refs):
    maps, late = refs[:shifts], refs[shifts : 2 * shifts]
    rest, out, sems = refs[2 * shifts], refs[2 * shifts + 2], refs[2 * shifts + 3]
    spots = late[0].shape[0]
    for g in range(shifts):
        for p in range(spots):
            j = maps[g][p]
            rest[j] = rest[j] + gain[j] * late[g][p].astype(F32)
    copies = []
    for g in range(shifts):
        for p in range(spots):
            j = maps[g][p]
            copies.append(pltpu.make_async_copy(rest.at[j], out.at[j], sems.at[g * spots + p]))
    for c in copies:
        c.start()
    for c in copies:
        c.wait()


def body(
    injected_amperage,
    voltage_self_admittance,
    voltage_coupling_tiles,
    voltage_partner_tile_ids,
    interface_tiles_per_level,
    interface_admittance,
    warmth_receiver_layer,
    warmth_receiver_tile,
    warmth_values,
    warmth_self_coefficient,
    warmth_coupling_tiles,
    warmth_partner_tile_ids,
    layer_boundary_couplings,
    substance_kind,
    reference_material_kappas,
    warmth_storage_per_point,
):
    blocks, points, regimes = injected_amperage.shape
    tiles = warmth_values.shape[0]
    levels, width = interface_tiles_per_level.shape
    links = voltage_partner_tile_ids.shape[1]
    groups = lax.axis_size("therm")
    shifts = groups - 1
    whole = (blocks, points, regimes)
    warm = (tiles, points, regimes)
    face = (width, points, regimes)
    late_spots = min(levels * width, tiles)
    early_spots = tiles - late_spots
    near_flops = 2 * blocks * links * points * points * regimes
    terms = pltpu.VMEM((levels * width, points, regimes), F32)
    dma = pltpu.SemaphoreType.DMA

    def exchange(faces, order):
        return [from_partner(faces[b], "elec", b) for b in order]

    far_first = list(range(levels))[::-1]
    turned = far_first[-1:] + far_first[:-1]

    amps, diag, face_ids, ids, layer, tile, *faces = call(
        functools.partial(start_kernel, levels),
        [
            (whole, BF16, VM),
            (voltage_self_admittance.shape, F32, VM),
            ((width, levels), I32, SM),
            ((links, blocks), I32, SM),
            ((1, blocks), I32, SM),
            ((blocks,), I32, SM),
        ]
        + [(face, BF16, VM)] * levels,
        on(
            HB,
            injected_amperage,
            voltage_self_admittance,
            interface_tiles_per_level.T,
            voltage_partner_tile_ids.T,
            warmth_receiver_layer.T,
            warmth_receiver_tile,
        ),
        "start",
        scratch=[dma((6,))],
    )
    order = far_first
    incoming = exchange(faces, order)

    packed, state, field, scale, warmth, kind, slot, rows = call(
        functools.partial(first_kernel, groups),
        [
            ((blocks, points, links * points), BF16, VM),
            (whole, F32, VM),
            (whole, BF16, VM),
            (whole, F32, VM),
            (warm, BF16, VM),
            (substance_kind.shape, I32, VM),
            ((blocks,), I32, SM),
            ((shifts, 16, regimes), BF16, VM),
        ],
        on(SM, ids, layer, tile, face_ids)
        + on(HB, voltage_coupling_tiles, warmth_values, substance_kind)
        + on(VM, amps, diag),
        "first",
        scratch=[
            pltpu.VMEM(voltage_coupling_tiles.shape, BF16),
            pltpu.VMEM(whole, BF16),
            pltpu.SMEM((tiles,), I32),
            pltpu.SMEM((tiles,), I32),
            dma((4,)),
            dma((2,)),
        ],
        flops=near_flops,
        limit=8 << 20,
    )
    for sweep_index in range(SWEEPS - 1):
        if sweep_index:
            state, field = call(
                near_kernel,
                [(whole, F32, VM), (whole, BF16, VM)],
                on(SM, ids) + on(VM, packed, field, state, amps, scale),
                "near",
                flops=near_flops,
            )
        token, carried = scale, None
        if sweep_index == 1:
            inputs = (
                on(ANY, field)
                + on(SM, reference_material_kappas)
                + on(VM, kind, warmth)
            )
            if groups == 2:
                (packet,) = call(
                    packet_kernel,
                    [((ZB, points, regimes), BF16, VM)],
                    inputs,
                    "packet",
                )
                carried = packet
            else:
                low, high = call(
                    edge_kernel,
                    [((ZB, points, regimes), BF16, VM)] * 2,
                    inputs,
                    "edge",
                )
                token = low
        if sweep_index == 2:
            if groups == 2:
                swap = [(0, 1), (1, 0)]
                got = lax.ppermute(packet, "therm", swap)
                below = above = got
            else:
                up = [(i, i + 1) for i in range(groups - 1)]
                down = [(j, i) for i, j in up]
                below = lax.ppermute(high, "therm", up)
                above = lax.ppermute(low, "therm", down)
                got = above
            token = got
        outs = [(whole, F32, VM), (whole, BF16, VM)] + [(face, BF16, VM)] * levels
        ins = on(ANY, token) + on(SM, face_ids)
        ins += on(VM, interface_admittance, scale, *incoming, state, field)
        aliases = {levels + 4: 0, levels + 5: 1}
        if carried is not None:
            ins += on(VM, carried)
            outs = [(carried.shape, BF16, VM)] + outs
            aliases = {levels + 4: 1, levels + 5: 2, levels + 6: 0}
        made = call(
            functools.partial(face_kernel, order), outs, ins, "face", aliases, [terms]
        )
        if carried is not None:
            packet, *made = made
        state, field, *faces = made
        if sweep_index < SWEEPS - 2:
            order = turned if sweep_index == 1 else far_first
            incoming = exchange(faces, order)
    voltage_solution = field

    heat, soon, *faces = call(
        functools.partial(heat_kernel, early_spots),
        [
            ((groups * tiles, points, regimes), F32, VM),
            ((shifts, early_spots * points + rows.shape[1], regimes), BF16, VM),
        ]
        + [(face, BF16, VM)] * levels,
        on(SM, slot, ids) + on(VM, packed, field, scale, rows, *faces),
        "heat",
        aliases={6 + b: 2 + b for b in range(levels)},
        flops=near_flops,
    )
    routes = [[(i, (i + s) % groups) for i in range(groups)] for s in range(1, groups)]
    soon = [lax.ppermute(soon[s], "therm", routes[s]) for s in range(shifts)]
    maps = [x[early_spots * points, :tiles].astype(I32) for x in soon]
    order = far_first
    incoming = exchange(faces, order)

    rest, gain = call(
        functools.partial(conduction_kernel, groups),
        [(warm, F32, VM), (warm, F32, VM)],
        on(SM, warmth_partner_tile_ids.T, reference_material_kappas)
        + on(
            VM,
            warmth_coupling_tiles,
            kind,
            warmth_self_coefficient,
            warmth_storage_per_point,
            layer_boundary_couplings,
            warmth,
            below,
            above,
        )
        + on(ANY, heat),
        "conduction",
        scratch=[pltpu.VMEM(warm, BF16)],
        flops=near_flops,
    )
    heat, late = call(
        functools.partial(heat_face_kernel, order),
        [((groups * tiles, points, regimes), F32, VM), ((shifts, late_spots) + warm[1:], BF16, VM)],
        on(SM, slot, face_ids) + on(VM, interface_admittance, field, *incoming, heat),
        "heat_face",
        aliases={levels + 4: 0},
        scratch=[terms],
    )
    late = [lax.ppermute(late[s], "therm", routes[s]) for s in range(shifts)]
    rest, out, *maps = call(
        functools.partial(early_kernel, shifts),
        [(warm, F32, VM), (warm, F32, HB)] + [((late_spots,), I32, SM)] * shifts,
        on(VM, heat, gain) + on(SM, *maps) + on(VM, *soon, rest),
        "early",
        aliases={2 + 2 * shifts: 0},
        scratch=[dma],
    )
    (advanced_warmth_values,) = call(
        functools.partial(late_kernel, shifts),
        [(warm, F32, HB)],
        on(VM, gain) + on(SM, *maps) + on(VM, *late, rest) + on(HB, out),
        "late",
        aliases={2 + 2 * shifts: 0},
        scratch=[dma((shifts * late_spots,))],
    )
    return (voltage_solution, advanced_warmth_values)


def solution(mesh):
    split = P(("elec", "therm"))
    return jax.shard_map(
        body,
        mesh=mesh,
        in_specs=(split,) * 14 + (P(), split),
        out_specs=(split, split),
        check_vma=False,
    )
```

```python
import functools

import jax
import jax.numpy as jnp
from jax import lax
from jax.experimental import pallas as pl
from jax.experimental.pallas import tpu as pltpu
from jax.sharding import PartitionSpec as P

SWEEPS = 5
ZB = 2

relax_factor = 0.8
time_increment = 0.5

F32 = jnp.float32
BF16 = jnp.bfloat16
I32 = jnp.int32
VM = pl.BlockSpec(memory_space=pltpu.VMEM)
SM = pl.BlockSpec(memory_space=pltpu.SMEM)
HB = pl.BlockSpec(memory_space=pltpu.HBM)
ANY = pl.BlockSpec(memory_space=pl.ANY)
SPACES = {id(VM): pltpu.VMEM, id(HB): pltpu.HBM, id(SM): pltpu.SMEM}
LIMIT = 4 << 20


def call(kernel, outs, ins, name, aliases={}, scratch=(), flops=0, limit=LIMIT):
    args = []
    for x, spec in ins:
        if spec is VM or spec is HB:
            x = pltpu.with_memory_space_constraint(x, SPACES[id(spec)])
        args.append(x)
    return pl.pallas_call(
        kernel,
        out_shape=[SPACES[id(spec)](shape, dtype) for shape, dtype, spec in outs],
        in_specs=[spec for _, spec in ins],
        out_specs=[spec for _, _, spec in outs],
        input_output_aliases=aliases,
        scratch_shapes=scratch,
        compiler_params=pltpu.CompilerParams(vmem_limit_bytes=limit),
        cost_estimate=pl.CostEstimate(flops=flops, bytes_accessed=0, transcendentals=0),
        name=name,
    )(*args)


def on(spec, *arrays):
    return [(x, spec) for x in arrays]


def from_partner(block, axis, bit):
    count = lax.axis_size(axis)
    route = []
    for low in range(count):
        high = low | 1 << bit
        if high != low and high < count:
            route += [(low, high), (high, low)]
    return lax.ppermute(block, axis, route)


def column(table, row, width):
    return jnp.broadcast_to(table[:, row : row + 1], (table.shape[0], width))


def joined(tiles_ref, row):
    return jnp.concatenate([tiles_ref[row, k] for k in range(tiles_ref.shape[1])], axis=1)


def picked(field_ref, ids_ref, row):
    return jnp.concatenate([field_ref[ids_ref[k, row]] for k in range(ids_ref.shape[0])], axis=0)


def start_kernel(levels, amps, diag, face_ids, *refs):
    small = refs[:3]
    amps_v, diag_v, face_ids_s = refs[3:6]
    small_s, faces, sems = refs[6:9], refs[9 : 9 + levels], refs[-1]
    pairs = [(face_ids, face_ids_s), (diag, diag_v), (amps, amps_v)]
    copies = [
        pltpu.make_async_copy(a, b, sems.at[n])
        for n, (a, b) in enumerate(pairs + list(zip(small, small_s)))
    ]
    for c in copies:
        c.start()
    copies[0].wait()
    copies[1].wait()
    scale = relax_factor / diag_v[...]
    rows = lax.broadcasted_iota(I32, scale.shape, 0)
    chosen = []
    for b in range(levels):
        for f in range(face_ids.shape[0]):
            mine = jnp.where(rows == face_ids_s[f, b], scale, 0.0)
            chosen.append(jnp.sum(mine, axis=0, keepdims=True))
    turned = jnp.concatenate(chosen, axis=0).T
    copies[2].wait()
    for b in range(levels):
        for f in range(face_ids.shape[0]):
            s = column(turned, b * face_ids.shape[0] + f, amps.shape[2])
            faces[b][f] = (s * amps_v[face_ids_s[f, b]].astype(F32)).astype(BF16)
    for c in copies[3:]:
        c.wait()


def route(groups, layer, tile, face_ids, slot, rows, flag, place):
    own = lax.axis_index("therm")
    blocks, tiles = slot.shape[0], flag.shape[0]
    levels, width = face_ids.shape[1], face_ids.shape[0]
    early_slots = max(tiles - levels * width, 0)
    lane = lax.broadcasted_iota(I32, rows.shape[1:], 1)

    def away(i):
        a = layer[0, i] - own
        return jnp.where(a < 0, a + groups, a)

    def home(i, c):
        slot[i] = tile[i]
        return c

    lax.fori_loop(0, blocks, home, 0)
    for g in range(1, groups):

        def clear(j, c):
            flag[j] = 0
            return c

        def mark(i, c):
            j = tile[i]
            flag[j] = jnp.where(away(i) == g, 1, flag[j])
            return c

        def late(j, c):
            is_late = flag[j] == 2
            place[j] = jnp.where(is_late, c, 0)
            return c + is_late.astype(I32)

        def early(j, c):
            at, behind, row = c
            is_early = flag[j] == 1
            fits = at < early_slots
            pos = jnp.where(fits, at, behind)
            pos = jnp.where(is_early, pos, place[j])
            place[j] = pos
            used = flag[j] > 0
            row = jnp.where((lane == pos) & used, j, row)
            at = at + (is_early & fits).astype(I32)
            behind = behind + (is_early & jnp.logical_not(fits)).astype(I32)
            return at, behind, row

        def assign(i, c):
            slot[i] = jnp.where(away(i) == g, g * tiles + place[tile[i]], slot[i])
            return c

        lax.fori_loop(0, tiles, clear, 0)
        lax.fori_loop(0, blocks, mark, 0)
        for b in range(levels):
            for f in range(width):
                i = face_ids[f, b]
                j = tile[i]
                flag[j] = jnp.where(away(i) == g, 2, flag[j])
        behind = lax.fori_loop(0, tiles, late, early_slots)
        _, _, row = lax.fori_loop(
            0, tiles, early, (0, behind, jnp.zeros(rows.shape[1:], I32))
        )
        lax.fori_loop(0, blocks, assign, 0)
        rows[g - 1] = row.astype(F32).astype(BF16)


def first_kernel(groups, ids, layer, tile, face_ids, tiles, warmth, kind, amps, diag, *refs):
    packed, state_out, field_out, scale, warmth_v, kind_v, slot, rows = refs[:8]
    tiles_v, field, flag, place, sems, later_sems = refs[8:]
    blocks = packed.shape[0]
    step = blocks // sems.shape[0]
    copies = []
    later = [
        pltpu.make_async_copy(warmth, warmth_v, later_sems.at[0]),
        pltpu.make_async_copy(kind, kind_v, later_sems.at[1]),
    ]
    for p in range(0, blocks, step):
        part = pl.ds(p, step)
        copies.append(
            pltpu.make_async_copy(tiles.at[part], tiles_v.at[part], sems.at[p // step])
        )
    for c in copies + later:
        c.start()
    route(groups, layer, tile, face_ids, slot, rows, flag, place)
    turned = (relax_factor / diag[...]).T
    for i in range(blocks):
        s = column(turned, i, scale.shape[2])
        scale[i] = s
        field[i] = (s * amps[i].astype(F32)).astype(BF16)
    for i in range(blocks):
        if i % step == 0:
            copies[i // step].wait()
        row = joined(tiles_v, i)
        packed[i] = row
        image = jnp.dot(row, picked(field, ids, i), preferred_element_type=F32)
        a = amps[i].astype(F32)
        s = scale[i]
        x = s * a - relax_factor * field[i].astype(F32) + s * (a - image)
        state_out[i] = x
        field_out[i] = x.astype(BF16)
    for c in later:
        c.wait()


def near_kernel(ids, packed, field, state, amps, scale, state_out, field_out):
    for i in range(packed.shape[0]):
        image = jnp.dot(packed[i], picked(field, ids, i), preferred_element_type=F32)
        x = state[i] - relax_factor * field[i].astype(F32)
        x = x + scale[i] * (amps[i].astype(F32) - image)
        state_out[i] = x
        field_out[i] = x.astype(BF16)


def face_terms(levels, face_ids, admittance, incoming, terms):
    width = face_ids.shape[0]
    for b in range(levels):
        for f in range(width):
            terms[b * width + f] = jnp.dot(
                admittance[b * width + f], incoming[b][f], preferred_element_type=F32
            )


def in_level_order(refs, order):
    return [refs[order.index(b)] for b in range(len(order))]


def face_kernel(order, token, face_ids, admittance, scale, *refs):
    levels = len(order)
    incoming = in_level_order(refs[:levels], order)
    state, field = refs[levels + 2 : levels + 4]
    faces, terms = refs[levels + 4 : 2 * levels + 4], refs[-1]
    width = face_ids.shape[0]
    face_terms(levels, face_ids, admittance, incoming, terms)
    for b in range(levels):
        for f in range(width):
            i = face_ids[f, b]
            state[i] = state[i] - scale[i] * terms[b * width + f]
    for b in range(levels):
        for f in range(width):
            i = face_ids[f, b]
            x = state[i].astype(BF16)
            field[i] = x
            faces[b][f] = x


def heat_kernel(spots, slot, ids, packed, field, scale, rows, edges, *refs):
    levels = (len(refs) - 2) // 2
    heat, soon = refs[levels], refs[levels + 1]
    groups, points = soon.shape[0] + 1, heat.shape[1]
    tiles = heat.shape[0] // groups
    heat[...] = jnp.zeros(heat.shape, F32)
    for i in range(packed.shape[0]):
        image = jnp.dot(packed[i], picked(field, ids, i), preferred_element_type=F32)
        v = field[i].astype(F32)
        s = slot[i]
        heat[s] = heat[s] + v * (relax_factor / scale[i] * v + image)
    for g in range(1, groups):
        blocks = [heat[g * tiles + p].astype(BF16) for p in range(spots)]
        blocks += [edges[g - 1, z] for z in range(ZB)]
        for p, block in enumerate(blocks):
            soon[g - 1, p * points : (p + 1) * points] = block
        soon[g - 1, len(blocks) * points :] = rows[g - 1]


def heat_face_kernel(order, slot, face_ids, admittance, *refs):
    levels = len(order)
    incoming = in_level_order(refs[:levels], order)
    heat, field, late, terms = refs[levels + 2 :]
    groups, spots = late.shape[0] + 1, late.shape[1]
    tiles = heat.shape[0] // groups
    width = face_ids.shape[0]
    face_terms(levels, face_ids, admittance, incoming, terms)
    for b in range(levels):
        for f in range(width):
            i = face_ids[f, b]
            s = slot[i]
            heat[s] = heat[s] + field[i].astype(F32) * terms[b * width + f]
    for g in range(1, groups):
        late[g - 1] = heat[(g + 1) * tiles - spots : (g + 1) * tiles].astype(BF16)


def kappa_columns(kappas, kind):
    kinds = kind[...]
    kappa = jnp.zeros(kinds.shape, F32)
    for m in range(kappas.shape[0]):
        kappa = jnp.where(kinds == m, kappas[m], kappa)
    return kappa.T


def block_flux(kappa, warmth):
    w = warmth.astype(F32)
    return (kappa * (1.0 + 0.4 * jnp.tanh(w)) * w).astype(BF16)


def edge_kernel(token, kappas, kind, warmth, edges):
    turned = kappa_columns(kappas, kind)
    tiles, points, width = warmth.shape
    shifts = edges.shape[0]
    sends_top = lax.axis_index("therm") == 0
    for z in range(ZB):
        top = tiles - ZB + z
        low = block_flux(column(turned, z, width), warmth[z])
        high = block_flux(column(turned, top, width), warmth[top])
        for s in range(1, shifts - 1):
            edges[s, z] = low
        if shifts == 1:
            edges[0, z] = jnp.where(sends_top, high.astype(F32), low.astype(F32)).astype(BF16)
        else:
            edges[0, z] = high
            edges[shifts - 1, z] = low


def conduction_kernel(
    ids,
    kappas,
    tiles,
    kind,
    coefficient,
    storage,
    warmth,
    heat,
    rest,
    gain,
    flux,
):
    count = tiles.shape[0]
    width = flux.shape[2]
    turned = kappa_columns(kappas, kind)
    for i in range(count):
        flux[i] = block_flux(column(turned, i, width), warmth[i])
    diag = coefficient[...].T
    gains = (time_increment / storage[...]).T
    for i in range(count):
        image = jnp.dot(joined(tiles, i), picked(flux, ids, i), preferred_element_type=F32)
        image = image + column(diag, i, width) * flux[i].astype(F32)
        g = column(gains, i, width)
        gain[i] = g
        rest[i] = warmth[i].astype(F32) - g * image


def early_kernel(shifts, heat, gain, couplings, *refs):
    maps, soon = refs[:shifts], refs[shifts : 2 * shifts]
    rest, out = refs[2 * shifts + 1 : 2 * shifts + 3]
    spots, sem = refs[2 * shifts + 3 : -1], refs[-1]
    tiles, points = rest.shape[:2]
    sent = tiles - spots[0].shape[0]
    own = lax.axis_index("therm")
    lowest = (own > 0).astype(F32)
    highest = (own < shifts).astype(F32)
    terms = []
    for z in range(ZB):
        at = slice((sent + z) * points, (sent + z + 1) * points)
        low = jnp.dot(couplings[z], soon[0][at], preferred_element_type=F32)
        high = jnp.dot(couplings[ZB + z], soon[-1][at], preferred_element_type=F32)
        terms += [(z, lowest * low), (tiles - ZB + z, highest * high)]
    for j, term in terms:
        rest[j] = rest[j] - gain[j] * term
    for i in range(tiles):
        rest[i] = rest[i] + gain[i] * heat[i]
    for g in range(shifts):
        for p in range(sent):
            j = maps[g][p]
            rest[j] = rest[j] + gain[j] * soon[g][p * points : (p + 1) * points].astype(F32)
    whole = pltpu.make_async_copy(rest, out, sem)
    whole.start()
    for g in range(shifts):
        for p in range(spots[g].shape[0]):
            spots[g][p] = maps[g][tiles - spots[g].shape[0] + p]
    whole.wait()


def late_kernel(shifts, gain, *refs):
    maps, late = refs[:shifts], refs[shifts : 2 * shifts]
    rest, out, sems = refs[2 * shifts], refs[2 * shifts + 2], refs[2 * shifts + 3]
    spots = late[0].shape[0]
    for g in range(shifts):
        for p in range(spots):
            j = maps[g][p]
            rest[j] = rest[j] + gain[j] * late[g][p].astype(F32)
    copies = []
    for g in range(shifts):
        for p in range(spots):
            j = maps[g][p]
            copies.append(pltpu.make_async_copy(rest.at[j], out.at[j], sems.at[g * spots + p]))
    for c in copies:
        c.start()
    for c in copies:
        c.wait()


def body(
    injected_amperage,
    voltage_self_admittance,
    voltage_coupling_tiles,
    voltage_partner_tile_ids,
    interface_tiles_per_level,
    interface_admittance,
    warmth_receiver_layer,
    warmth_receiver_tile,
    warmth_values,
    warmth_self_coefficient,
    warmth_coupling_tiles,
    warmth_partner_tile_ids,
    layer_boundary_couplings,
    substance_kind,
    reference_material_kappas,
    warmth_storage_per_point,
):
    blocks, points, regimes = injected_amperage.shape
    tiles = warmth_values.shape[0]
    levels, width = interface_tiles_per_level.shape
    links = voltage_partner_tile_ids.shape[1]
    groups = lax.axis_size("therm")
    shifts = groups - 1
    whole = (blocks, points, regimes)
    warm = (tiles, points, regimes)
    face = (width, points, regimes)
    late_spots = min(levels * width, tiles)
    early_spots = tiles - late_spots
    sent_rows = (early_spots + ZB) * points
    near_flops = 2 * blocks * links * points * points * regimes
    terms = pltpu.VMEM((levels * width, points, regimes), F32)
    dma = pltpu.SemaphoreType.DMA

    def exchange(faces, order):
        return [from_partner(faces[b], "elec", b) for b in order]

    far_first = list(range(levels))[::-1]
    half = levels // 2
    turned = far_first[half:] + far_first[:half]

    amps, diag, face_ids, ids, layer, tile, *faces = call(
        functools.partial(start_kernel, levels),
        [
            (whole, BF16, VM),
            (voltage_self_admittance.shape, F32, VM),
            ((width, levels), I32, SM),
            ((links, blocks), I32, SM),
            ((1, blocks), I32, SM),
            ((blocks,), I32, SM),
        ]
        + [(face, BF16, VM)] * levels,
        on(
            HB,
            injected_amperage,
            voltage_self_admittance,
            interface_tiles_per_level.T,
            voltage_partner_tile_ids.T,
            warmth_receiver_layer.T,
            warmth_receiver_tile,
        ),
        "start",
        scratch=[dma((6,))],
    )
    order = far_first
    incoming = exchange(faces, order)

    packed, state, field, scale, warmth, kind, slot, rows = call(
        functools.partial(first_kernel, groups),
        [
            ((blocks, points, links * points), BF16, VM),
            (whole, F32, VM),
            (whole, BF16, VM),
            (whole, F32, VM),
            (warm, BF16, VM),
            (substance_kind.shape, I32, VM),
            ((blocks,), I32, SM),
            ((shifts, 16, regimes), BF16, VM),
        ],
        on(SM, ids, layer, tile, face_ids)
        + on(HB, voltage_coupling_tiles, warmth_values, substance_kind)
        + on(VM, amps, diag),
        "first",
        scratch=[
            pltpu.VMEM(voltage_coupling_tiles.shape, BF16),
            pltpu.VMEM(whole, BF16),
            pltpu.SMEM((tiles,), I32),
            pltpu.SMEM((tiles,), I32),
            dma((4,)),
            dma((2,)),
        ],
        flops=near_flops,
        limit=8 << 20,
    )
    for sweep_index in range(SWEEPS - 1):
        if sweep_index:
            state, field = call(
                near_kernel,
                [(whole, F32, VM), (whole, BF16, VM)],
                on(SM, ids) + on(VM, packed, field, state, amps, scale),
                "near",
                flops=near_flops,
            )
        token = scale
        if sweep_index == 1:
            (edges,) = call(
                edge_kernel,
                [((shifts, ZB, points, regimes), BF16, VM)],
                on(ANY, field) + on(SM, reference_material_kappas) + on(VM, kind, warmth),
                "edge",
            )
            token = edges
        state, field, *faces = call(
            functools.partial(face_kernel, order),
            [(whole, F32, VM), (whole, BF16, VM)] + [(face, BF16, VM)] * levels,
            on(ANY, token)
            + on(SM, face_ids)
            + on(VM, interface_admittance, scale, *incoming, state, field),
            "face",
            aliases={levels + 4: 0, levels + 5: 1},
            scratch=[terms],
        )
        if sweep_index < SWEEPS - 2:
            order = turned if sweep_index == 1 else far_first
            incoming = exchange(faces, order)
    heat, soon, *faces = call(
        functools.partial(heat_kernel, early_spots),
        [
            ((groups * tiles, points, regimes), F32, VM),
            ((shifts, sent_rows + rows.shape[1], regimes), BF16, VM),
        ]
        + [(face, BF16, VM)] * levels,
        on(SM, slot, ids) + on(VM, packed, field, scale, rows, edges, *faces),
        "heat",
        aliases={7 + b: 2 + b for b in range(levels)},
        flops=near_flops,
    )
    routes = [[(i, (i + s) % groups) for i in range(groups)] for s in range(1, groups)]
    soon = [lax.ppermute(soon[s], "therm", routes[s]) for s in range(shifts)]
    maps = [x[sent_rows, :tiles].astype(I32) for x in soon]
    order = far_first
    incoming = exchange(faces, order)

    rest, gain = call(
        conduction_kernel,
        [(warm, F32, VM), (warm, F32, VM)],
        on(SM, warmth_partner_tile_ids.T, reference_material_kappas)
        + on(
            VM,
            warmth_coupling_tiles,
            kind,
            warmth_self_coefficient,
            warmth_storage_per_point,
            warmth,
        )
        + on(ANY, heat),
        "conduction",
        scratch=[pltpu.VMEM(warm, BF16)],
        flops=near_flops,
    )
    heat, voltage_solution, late = call(
        functools.partial(heat_face_kernel, order),
        [
            ((groups * tiles, points, regimes), F32, VM),
            (whole, BF16, VM),
            ((shifts, late_spots, points, regimes), BF16, VM),
        ],
        on(SM, slot, face_ids) + on(VM, interface_admittance, *incoming, heat, field),
        "heat_face",
        aliases={levels + 3: 0, levels + 4: 1},
        scratch=[terms],
    )
    late = [lax.ppermute(late[s], "therm", routes[s]) for s in range(shifts)]
    rest, out, *maps = call(
        functools.partial(early_kernel, shifts),
        [(warm, F32, VM), (warm, F32, HB)] + [((late_spots,), I32, SM)] * shifts,
        on(VM, heat, gain, layer_boundary_couplings) + on(SM, *maps) + on(VM, *soon, rest),
        "early",
        aliases={3 + 2 * shifts: 0},
        scratch=[dma],
    )
    (advanced_warmth_values,) = call(
        functools.partial(late_kernel, shifts),
        [(warm, F32, HB)],
        on(VM, gain) + on(SM, *maps) + on(VM, *late, rest) + on(HB, out),
        "late",
        aliases={2 + 2 * shifts: 0},
        scratch=[dma((shifts * late_spots,))],
    )
    return (voltage_solution, advanced_warmth_values)


def solution(mesh):
    split = P(("elec", "therm"))
    return jax.shard_map(
        body,
        mesh=mesh,
        in_specs=(split,) * 14 + (P(), split),
        out_specs=(split, split),
        check_vma=False,
    )
```

```python
import functools

import jax
import jax.numpy as jnp
from jax import lax
from jax.experimental import pallas as pl
from jax.experimental.pallas import tpu as pltpu
from jax.sharding import PartitionSpec as P

SWEEPS = 5
ZB = 2

relax_factor = 0.8
time_increment = 0.5

F32 = jnp.float32
BF16 = jnp.bfloat16
I32 = jnp.int32
VM = pl.BlockSpec(memory_space=pltpu.VMEM)
SM = pl.BlockSpec(memory_space=pltpu.SMEM)
HB = pl.BlockSpec(memory_space=pltpu.HBM)
ANY = pl.BlockSpec(memory_space=pl.ANY)
SPACES = {id(VM): pltpu.VMEM, id(HB): pltpu.HBM, id(SM): pltpu.SMEM}
LIMIT = 4 << 20


def call(kernel, outs, ins, name, aliases={}, scratch=(), flops=0, limit=LIMIT):
    args = []
    for x, spec in ins:
        if spec is VM or spec is HB:
            x = pltpu.with_memory_space_constraint(x, SPACES[id(spec)])
        args.append(x)
    return pl.pallas_call(
        kernel,
        out_shape=[SPACES[id(spec)](shape, dtype) for shape, dtype, spec in outs],
        in_specs=[spec for _, spec in ins],
        out_specs=[spec for _, _, spec in outs],
        input_output_aliases=aliases,
        scratch_shapes=scratch,
        compiler_params=pltpu.CompilerParams(vmem_limit_bytes=limit),
        cost_estimate=pl.CostEstimate(flops=flops, bytes_accessed=0, transcendentals=0),
        name=name,
    )(*args)


def on(spec, *arrays):
    return [(x, spec) for x in arrays]


def from_partner(block, axis, bit):
    count = lax.axis_size(axis)
    route = []
    for low in range(count):
        high = low | 1 << bit
        if high != low and high < count:
            route += [(low, high), (high, low)]
    return lax.ppermute(block, axis, route)


def column(table, row, width):
    return jnp.broadcast_to(table[:, row : row + 1], (table.shape[0], width))


def joined(tiles_ref, row):
    return jnp.concatenate([tiles_ref[row, k] for k in range(tiles_ref.shape[1])], axis=1)


def picked(field_ref, ids_ref, row):
    return jnp.concatenate([field_ref[ids_ref[k, row]] for k in range(ids_ref.shape[0])], axis=0)


def start_kernel(levels, amps, diag, face_ids, *refs):
    small = refs[:3]
    amps_v, diag_v, face_ids_s = refs[3:6]
    small_s, faces, sems = refs[6:9], refs[9 : 9 + levels], refs[-1]
    pairs = [(face_ids, face_ids_s), (diag, diag_v), (amps, amps_v)]
    copies = [
        pltpu.make_async_copy(a, b, sems.at[n])
        for n, (a, b) in enumerate(pairs + list(zip(small, small_s)))
    ]
    for c in copies:
        c.start()
    copies[0].wait()
    copies[1].wait()
    scale = relax_factor / diag_v[...]
    rows = lax.broadcasted_iota(I32, scale.shape, 0)
    chosen = []
    for b in range(levels):
        for f in range(face_ids.shape[0]):
            mine = jnp.where(rows == face_ids_s[f, b], scale, 0.0)
            chosen.append(jnp.sum(mine, axis=0, keepdims=True))
    turned = jnp.concatenate(chosen, axis=0).T
    copies[2].wait()
    for b in range(levels):
        for f in range(face_ids.shape[0]):
            s = column(turned, b * face_ids.shape[0] + f, amps.shape[2])
            points = amps.shape[1]
            block = s * amps_v[face_ids_s[f, b]].astype(F32)
            faces[b][f * points : (f + 1) * points] = block.astype(BF16)
    for c in copies[3:]:
        c.wait()


def route(groups, layer, tile, face_ids, slot, rows, flag, place):
    own = lax.axis_index("therm")
    blocks, tiles = slot.shape[0], flag.shape[0]
    levels, width = face_ids.shape[1], face_ids.shape[0]
    early_slots = max(tiles - levels * width, 0)
    lane = lax.broadcasted_iota(I32, rows.shape[1:], 1)

    def away(i):
        a = layer[0, i] - own
        return jnp.where(a < 0, a + groups, a)

    def home(i, c):
        slot[i] = tile[i]
        return c

    lax.fori_loop(0, blocks, home, 0)
    for g in range(1, groups):

        def clear(j, c):
            flag[j] = 0
            return c

        def mark(i, c):
            j = tile[i]
            flag[j] = jnp.where(away(i) == g, 1, flag[j])
            return c

        def late(j, c):
            is_late = flag[j] == 2
            place[j] = jnp.where(is_late, c, 0)
            return c + is_late.astype(I32)

        def early(j, c):
            at, behind, row = c
            is_early = flag[j] == 1
            fits = at < early_slots
            pos = jnp.where(fits, at, behind)
            pos = jnp.where(is_early, pos, place[j])
            place[j] = pos
            used = flag[j] > 0
            row = jnp.where((lane == pos) & used, j, row)
            at = at + (is_early & fits).astype(I32)
            behind = behind + (is_early & jnp.logical_not(fits)).astype(I32)
            return at, behind, row

        def assign(i, c):
            slot[i] = jnp.where(away(i) == g, g * tiles + place[tile[i]], slot[i])
            return c

        lax.fori_loop(0, tiles, clear, 0)
        lax.fori_loop(0, blocks, mark, 0)
        for b in range(levels):
            for f in range(width):
                i = face_ids[f, b]
                j = tile[i]
                flag[j] = jnp.where(away(i) == g, 2, flag[j])
        behind = lax.fori_loop(0, tiles, late, early_slots)
        _, _, row = lax.fori_loop(
            0, tiles, early, (0, behind, jnp.zeros(rows.shape[1:], I32))
        )
        lax.fori_loop(0, blocks, assign, 0)
        rows[g - 1] = row.astype(F32).astype(BF16)


def first_kernel(groups, ids, layer, tile, face_ids, tiles, warmth, kind, amps, diag, *refs):
    packed, state_out, field_out, scale, warmth_v, kind_v, slot, rows = refs[:8]
    tiles_v, field, flag, place, sems, later_sems = refs[8:]
    blocks = packed.shape[0]
    step = blocks // sems.shape[0]
    copies = []
    later = [
        pltpu.make_async_copy(warmth, warmth_v, later_sems.at[0]),
        pltpu.make_async_copy(kind, kind_v, later_sems.at[1]),
    ]
    for p in range(0, blocks, step):
        part = pl.ds(p, step)
        copies.append(
            pltpu.make_async_copy(tiles.at[part], tiles_v.at[part], sems.at[p // step])
        )
    for c in copies + later:
        c.start()
    route(groups, layer, tile, face_ids, slot, rows, flag, place)
    turned = (relax_factor / diag[...]).T
    for i in range(blocks):
        s = column(turned, i, scale.shape[2])
        scale[i] = s
        field[i] = (s * amps[i].astype(F32)).astype(BF16)
    for i in range(blocks):
        if i % step == 0:
            copies[i // step].wait()
        row = joined(tiles_v, i)
        packed[i] = row
        image = jnp.dot(row, picked(field, ids, i), preferred_element_type=F32)
        a = amps[i].astype(F32)
        s = scale[i]
        x = s * a - relax_factor * field[i].astype(F32) + s * (a - image)
        state_out[i] = x
        field_out[i] = x.astype(BF16)
    for c in later:
        c.wait()


def near_kernel(ids, packed, field, state, amps, scale, state_out, field_out, *for_heat):
    for i in range(packed.shape[0]):
        image = jnp.dot(packed[i], picked(field, ids, i), preferred_element_type=F32)
        x = state[i] - relax_factor * field[i].astype(F32)
        x = x + scale[i] * (amps[i].astype(F32) - image)
        state_out[i] = x
        field_out[i] = x.astype(BF16)
    if for_heat:
        heat, diag = for_heat
        heat[...] = jnp.zeros(heat.shape, F32)
        for i in range(packed.shape[0]):
            diag[i] = relax_factor / scale[i]


def face_terms(levels, face_ids, admittance, incoming, terms):
    width, points = face_ids.shape[0], terms.shape[1]
    for b in range(levels):
        for f in range(width):
            block = incoming[b][f * points : (f + 1) * points]
            terms[b * width + f] = jnp.dot(
                admittance[b * width + f], block, preferred_element_type=F32
            )


def in_level_order(refs, order):
    return [refs[order.index(b)] for b in range(len(order))]


def update_faces(face_ids, admittance, scale, incoming, state, field, faces, terms):
    levels, width, points = len(faces), face_ids.shape[0], terms.shape[1]
    face_terms(levels, face_ids, admittance, incoming, terms)
    for b in range(levels):
        for f in range(width):
            i = face_ids[f, b]
            state[i] = state[i] - scale[i] * terms[b * width + f]
    for b in range(levels):
        for f in range(width):
            i = face_ids[f, b]
            x = state[i].astype(BF16)
            field[i] = x
            faces[b][f * points : (f + 1) * points] = x


def face_kernel(order, token, face_ids, admittance, scale, *refs):
    levels = len(order)
    incoming = in_level_order(refs[:levels], order)
    state, field = refs[levels + 2 : levels + 4]
    faces, terms = refs[levels + 4 : 2 * levels + 4], refs[-1]
    update_faces(face_ids, admittance, scale, incoming, state, field, faces, terms)


def heat_kernel(
    order, spots, slot, ids, face_ids, admittance, scale, packed, diag, rows, edges, *refs
):
    levels = len(order)
    incoming = in_level_order(refs[:levels], order)
    state, field, heat, soon = refs[levels + 3 : levels + 7]
    faces, terms = refs[levels + 7 : 2 * levels + 7], refs[-1]
    groups, points = soon.shape[0] + 1, heat.shape[1]
    tiles = heat.shape[0] // groups
    update_faces(face_ids, admittance, scale, incoming, state, field, faces, terms)
    for i in range(packed.shape[0]):
        image = jnp.dot(packed[i], picked(field, ids, i), preferred_element_type=F32)
        v = field[i].astype(F32)
        s = slot[i]
        heat[s] = heat[s] + v * (diag[i] * v + image)
    for g in range(1, groups):
        blocks = [heat[g * tiles + p].astype(BF16) for p in range(spots)]
        blocks += [edges[g - 1, z] for z in range(ZB)]
        for p, block in enumerate(blocks):
            soon[g - 1, p * points : (p + 1) * points] = block
        soon[g - 1, len(blocks) * points :] = rows[g - 1]


def heat_face_kernel(order, slot, face_ids, admittance, *refs):
    levels = len(order)
    incoming = in_level_order(refs[:levels], order)
    heat, field, late, terms = refs[levels + 2 :]
    groups, spots = late.shape[0] + 1, late.shape[1]
    tiles = heat.shape[0] // groups
    width = face_ids.shape[0]
    face_terms(levels, face_ids, admittance, incoming, terms)
    for b in range(levels):
        for f in range(width):
            i = face_ids[f, b]
            s = slot[i]
            heat[s] = heat[s] + field[i].astype(F32) * terms[b * width + f]
    for g in range(1, groups):
        late[g - 1] = heat[(g + 1) * tiles - spots : (g + 1) * tiles].astype(BF16)


def kappa_columns(kappas, kind):
    kinds = kind[...]
    kappa = jnp.zeros(kinds.shape, F32)
    for m in range(kappas.shape[0]):
        kappa = jnp.where(kinds == m, kappas[m], kappa)
    return kappa.T


def block_flux(kappa, warmth):
    w = warmth.astype(F32)
    return (kappa * (1.0 + 0.4 * jnp.tanh(w)) * w).astype(BF16)


def edge_kernel(token, kappas, kind, warmth, edges):
    turned = kappa_columns(kappas, kind)
    tiles, points, width = warmth.shape
    shifts = edges.shape[0]
    sends_top = lax.axis_index("therm") == 0
    for z in range(ZB):
        top = tiles - ZB + z
        low = block_flux(column(turned, z, width), warmth[z])
        high = block_flux(column(turned, top, width), warmth[top])
        for s in range(1, shifts - 1):
            edges[s, z] = low
        if shifts == 1:
            edges[0, z] = jnp.where(sends_top, high.astype(F32), low.astype(F32)).astype(BF16)
        else:
            edges[0, z] = high
            edges[shifts - 1, z] = low


def conduction_kernel(
    ids,
    kappas,
    tiles,
    kind,
    coefficient,
    storage,
    warmth,
    heat,
    rest,
    gain,
    flux,
):
    count = tiles.shape[0]
    width = flux.shape[2]
    turned = kappa_columns(kappas, kind)
    for i in range(count):
        flux[i] = block_flux(column(turned, i, width), warmth[i])
    diag = coefficient[...].T
    gains = (time_increment / storage[...]).T
    for i in range(count):
        image = jnp.dot(joined(tiles, i), picked(flux, ids, i), preferred_element_type=F32)
        image = image + column(diag, i, width) * flux[i].astype(F32)
        g = column(gains, i, width)
        gain[i] = g
        rest[i] = warmth[i].astype(F32) - g * image


def early_kernel(shifts, heat, gain, couplings, *refs):
    maps, soon = refs[:shifts], refs[shifts : 2 * shifts]
    rest, field, out = refs[2 * shifts + 2 : 2 * shifts + 5]
    spots, sem = refs[2 * shifts + 5 : -1], refs[-1]
    tiles, points = rest.shape[:2]
    sent = tiles - spots[0].shape[0]
    own = lax.axis_index("therm")
    lowest = (own > 0).astype(F32)
    highest = (own < shifts).astype(F32)
    terms = []
    for z in range(ZB):
        at = slice((sent + z) * points, (sent + z + 1) * points)
        low = jnp.dot(couplings[z], soon[0][at], preferred_element_type=F32)
        high = jnp.dot(couplings[ZB + z], soon[-1][at], preferred_element_type=F32)
        terms += [(z, lowest * low), (tiles - ZB + z, highest * high)]
    for j, term in terms:
        rest[j] = rest[j] - gain[j] * term
    for i in range(tiles):
        rest[i] = rest[i] + gain[i] * heat[i]
    for g in range(shifts):
        for p in range(sent):
            j = maps[g][p]
            rest[j] = rest[j] + gain[j] * soon[g][p * points : (p + 1) * points].astype(F32)
    whole = pltpu.make_async_copy(rest, out, sem)
    whole.start()
    for g in range(shifts):
        for p in range(spots[g].shape[0]):
            spots[g][p] = maps[g][tiles - spots[g].shape[0] + p]
    whole.wait()


def late_kernel(shifts, gain, *refs):
    maps, late = refs[:shifts], refs[shifts : 2 * shifts]
    rest, out, sems = refs[2 * shifts], refs[2 * shifts + 2], refs[2 * shifts + 3]
    spots = late[0].shape[0]
    for g in range(shifts):
        for p in range(spots):
            j = maps[g][p]
            rest[j] = rest[j] + gain[j] * late[g][p].astype(F32)
    copies = []
    for g in range(shifts):
        for p in range(spots):
            j = maps[g][p]
            copies.append(pltpu.make_async_copy(rest.at[j], out.at[j], sems.at[g * spots + p]))
    for c in copies:
        c.start()
    for c in copies:
        c.wait()


def body(
    injected_amperage,
    voltage_self_admittance,
    voltage_coupling_tiles,
    voltage_partner_tile_ids,
    interface_tiles_per_level,
    interface_admittance,
    warmth_receiver_layer,
    warmth_receiver_tile,
    warmth_values,
    warmth_self_coefficient,
    warmth_coupling_tiles,
    warmth_partner_tile_ids,
    layer_boundary_couplings,
    substance_kind,
    reference_material_kappas,
    warmth_storage_per_point,
):
    blocks, points, regimes = injected_amperage.shape
    tiles = warmth_values.shape[0]
    levels, width = interface_tiles_per_level.shape
    links = voltage_partner_tile_ids.shape[1]
    groups = lax.axis_size("therm")
    shifts = groups - 1
    whole = (blocks, points, regimes)
    warm = (tiles, points, regimes)
    face = (width * points, regimes)
    late_spots = min(levels * width, tiles)
    early_spots = tiles - late_spots
    sent_rows = (early_spots + ZB) * points
    near_flops = 2 * blocks * links * points * points * regimes
    terms = pltpu.VMEM((levels * width, points, regimes), F32)
    dma = pltpu.SemaphoreType.DMA

    def exchange(faces, order):
        return [from_partner(faces[b], "elec", b) for b in order]

    far_first = list(range(levels))[::-1]

    amps, diag, face_ids, ids, layer, tile, *faces = call(
        functools.partial(start_kernel, levels),
        [
            (whole, BF16, VM),
            (voltage_self_admittance.shape, F32, VM),
            ((width, levels), I32, SM),
            ((links, blocks), I32, SM),
            ((1, blocks), I32, SM),
            ((blocks,), I32, SM),
        ]
        + [(face, BF16, VM)] * levels,
        on(
            HB,
            injected_amperage,
            voltage_self_admittance,
            interface_tiles_per_level.T,
            voltage_partner_tile_ids.T,
            warmth_receiver_layer.T,
            warmth_receiver_tile,
        ),
        "start",
        scratch=[dma((6,))],
    )
    order = far_first
    incoming = exchange(faces, order)

    packed, state, field, scale, warmth, kind, slot, rows = call(
        functools.partial(first_kernel, groups),
        [
            ((blocks, points, links * points), BF16, VM),
            (whole, F32, VM),
            (whole, BF16, VM),
            (whole, F32, VM),
            (warm, BF16, VM),
            (substance_kind.shape, I32, VM),
            ((blocks,), I32, SM),
            ((shifts, 16, regimes), BF16, VM),
        ],
        on(SM, ids, layer, tile, face_ids)
        + on(HB, voltage_coupling_tiles, warmth_values, substance_kind)
        + on(VM, amps, diag),
        "first",
        scratch=[
            pltpu.VMEM(voltage_coupling_tiles.shape, BF16),
            pltpu.VMEM(whole, BF16),
            pltpu.SMEM((tiles,), I32),
            pltpu.SMEM((tiles,), I32),
            dma((4,)),
            dma((2,)),
        ],
        flops=near_flops,
        limit=8 << 20,
    )
    for sweep_index in range(SWEEPS - 1):
        if sweep_index:
            last = sweep_index == SWEEPS - 2
            state, field, *for_heat = call(
                near_kernel,
                [(whole, F32, VM), (whole, BF16, VM)]
                + [((groups * tiles, points, regimes), F32, VM), (whole, F32, VM)] * last,
                on(SM, ids) + on(VM, packed, field, state, amps, scale),
                "near",
                flops=near_flops,
            )
        token = scale
        if sweep_index == 1:
            (edges,) = call(
                edge_kernel,
                [((shifts, ZB, points, regimes), BF16, VM)],
                on(ANY, field) + on(SM, reference_material_kappas) + on(VM, kind, warmth),
                "edge",
            )
            token = edges
        if sweep_index < SWEEPS - 2:
            state, field, *faces = call(
                functools.partial(face_kernel, order),
                [(whole, F32, VM), (whole, BF16, VM)] + [(face, BF16, VM)] * levels,
                on(ANY, token)
                + on(SM, face_ids)
                + on(VM, interface_admittance, scale, *incoming, state, field),
                "face",
                aliases={levels + 4: 0, levels + 5: 1},
                scratch=[terms],
            )
            incoming = exchange(faces, order)

    heat, diag = for_heat
    _, field, heat, soon, *faces = call(
        functools.partial(heat_kernel, order, early_spots),
        [
            (whole, F32, VM),
            (whole, BF16, VM),
            (heat.shape, F32, VM),
            ((shifts, sent_rows + rows.shape[1], regimes), BF16, VM),
        ]
        + [(face, BF16, VM)] * levels,
        on(SM, slot, ids, face_ids)
        + on(VM, interface_admittance, scale, packed, diag, rows, edges, *incoming)
        + on(VM, state, field, heat),
        "heat",
        aliases={9 + levels + n: n for n in range(3)},
        scratch=[terms],
        flops=near_flops,
    )
    routes = [[(i, (i + s) % groups) for i in range(groups)] for s in range(1, groups)]
    soon = [lax.ppermute(soon[s], "therm", routes[s]) for s in range(shifts)]
    maps = [x[sent_rows, :tiles].astype(I32) for x in soon]
    order = far_first
    incoming = exchange(faces, order)

    rest, gain = call(
        conduction_kernel,
        [(warm, F32, VM), (warm, F32, VM)],
        on(SM, warmth_partner_tile_ids.T, reference_material_kappas)
        + on(
            VM,
            warmth_coupling_tiles,
            kind,
            warmth_self_coefficient,
            warmth_storage_per_point,
            warmth,
        )
        + on(ANY, heat),
        "conduction",
        scratch=[pltpu.VMEM(warm, BF16)],
        flops=near_flops,
    )
    heat, field, late = call(
        functools.partial(heat_face_kernel, order),
        [
            ((groups * tiles, points, regimes), F32, VM),
            (whole, BF16, VM),
            ((shifts, late_spots, points, regimes), BF16, VM),
        ],
        on(SM, slot, face_ids) + on(VM, interface_admittance, *incoming, heat, field),
        "heat_face",
        aliases={levels + 3: 0, levels + 4: 1},
        scratch=[terms],
    )
    late = [lax.ppermute(late[s], "therm", routes[s]) for s in range(shifts)]
    rest, voltage_solution, out, *maps = call(
        functools.partial(early_kernel, shifts),
        [(warm, F32, VM), (whole, BF16, VM), (warm, F32, HB)] + [((late_spots,), I32, SM)] * shifts,
        on(VM, heat, gain, layer_boundary_couplings) + on(SM, *maps) + on(VM, *soon, rest, field),
        "early",
        aliases={3 + 2 * shifts: 0, 4 + 2 * shifts: 1},
        scratch=[dma],
    )
    (advanced_warmth_values,) = call(
        functools.partial(late_kernel, shifts),
        [(warm, F32, HB)],
        on(VM, gain) + on(SM, *maps) + on(VM, *late, rest) + on(HB, out),
        "late",
        aliases={2 + 2 * shifts: 0},
        scratch=[dma((shifts * late_spots,))],
    )
    return (voltage_solution, advanced_warmth_values)


def solution(mesh):
    split = P(("elec", "therm"))
    return jax.shard_map(
        body,
        mesh=mesh,
        in_specs=(split,) * 14 + (P(), split),
        out_specs=(split, split),
        check_vma=False,
    )
```

```python
import functools

import jax
import jax.numpy as jnp
from jax import lax
from jax.experimental import pallas as pl
from jax.experimental.pallas import tpu as pltpu
from jax.sharding import PartitionSpec as P

SWEEPS = 5
ZB = 2
GATHERED = 1

relax_factor = 0.8
time_increment = 0.5

F32 = jnp.float32
BF16 = jnp.bfloat16
I32 = jnp.int32
VM = pl.BlockSpec(memory_space=pltpu.VMEM)
SM = pl.BlockSpec(memory_space=pltpu.SMEM)
HB = pl.BlockSpec(memory_space=pltpu.HBM)
ANY = pl.BlockSpec(memory_space=pl.ANY)
SPACES = {id(VM): pltpu.VMEM, id(HB): pltpu.HBM, id(SM): pltpu.SMEM}
LIMIT = 4 << 20


def call(kernel, outs, ins, name, aliases={}, scratch=(), flops=0, limit=LIMIT):
    args = []
    for x, spec in ins:
        if spec is VM or spec is HB:
            x = pltpu.with_memory_space_constraint(x, SPACES[id(spec)])
        args.append(x)
    return pl.pallas_call(
        kernel,
        out_shape=[SPACES[id(spec)](shape, dtype) for shape, dtype, spec in outs],
        in_specs=[spec for _, spec in ins],
        out_specs=[spec for _, _, spec in outs],
        input_output_aliases=aliases,
        scratch_shapes=scratch,
        compiler_params=pltpu.CompilerParams(vmem_limit_bytes=limit),
        cost_estimate=pl.CostEstimate(flops=flops, bytes_accessed=0, transcendentals=0),
        name=name,
    )(*args)


def on(spec, *arrays):
    return [(x, spec) for x in arrays]


def from_partner(block, axis, bit):
    count = lax.axis_size(axis)
    route = []
    for low in range(count):
        high = low | 1 << bit
        if high != low and high < count:
            route += [(low, high), (high, low)]
    return lax.ppermute(block, axis, route)


def both_halves(block, axis, bit):
    low = [i for i in range(lax.axis_size(axis)) if not i >> bit & 1]
    pairs = [[i, i | 1 << bit] for i in low]
    return lax.all_gather(block, axis, axis=0, axis_index_groups=pairs)


def column(table, row, width):
    return jnp.broadcast_to(table[:, row : row + 1], (table.shape[0], width))


def joined(tiles_ref, row):
    return jnp.concatenate([tiles_ref[row, k] for k in range(tiles_ref.shape[1])], axis=1)


def picked(field_ref, ids_ref, row):
    return jnp.concatenate([field_ref[ids_ref[k, row]] for k in range(ids_ref.shape[0])], axis=0)


def start_kernel(levels, amps, diag, face_ids, *refs):
    small = refs[:3]
    amps_v, diag_v, face_ids_s = refs[3:6]
    small_s, faces, sems = refs[6:9], refs[9 : 9 + levels], refs[-1]
    pairs = [(face_ids, face_ids_s), (diag, diag_v), (amps, amps_v)]
    copies = [
        pltpu.make_async_copy(a, b, sems.at[n])
        for n, (a, b) in enumerate(pairs + list(zip(small, small_s)))
    ]
    for c in copies:
        c.start()
    copies[0].wait()
    copies[1].wait()
    scale = relax_factor / diag_v[...]
    rows = lax.broadcasted_iota(I32, scale.shape, 0)
    chosen = []
    for b in range(levels):
        for f in range(face_ids.shape[0]):
            mine = jnp.where(rows == face_ids_s[f, b], scale, 0.0)
            chosen.append(jnp.sum(mine, axis=0, keepdims=True))
    turned = jnp.concatenate(chosen, axis=0).T
    copies[2].wait()
    for b in range(levels):
        for f in range(face_ids.shape[0]):
            s = column(turned, b * face_ids.shape[0] + f, amps.shape[2])
            points = amps.shape[1]
            block = s * amps_v[face_ids_s[f, b]].astype(F32)
            faces[b][f * points : (f + 1) * points] = block.astype(BF16)
    for c in copies[3:]:
        c.wait()


def route(groups, layer, tile, face_ids, slot, rows, flag, place):
    own = lax.axis_index("therm")
    blocks, tiles = slot.shape[0], flag.shape[0]
    levels, width = face_ids.shape[1], face_ids.shape[0]
    early_slots = max(tiles - levels * width, 0)
    lane = lax.broadcasted_iota(I32, rows.shape[1:], 1)

    def away(i):
        a = layer[0, i] - own
        return jnp.where(a < 0, a + groups, a)

    def home(i, c):
        slot[i] = tile[i]
        return c

    lax.fori_loop(0, blocks, home, 0)
    for g in range(1, groups):

        def clear(j, c):
            flag[j] = 0
            return c

        def mark(i, c):
            j = tile[i]
            flag[j] = jnp.where(away(i) == g, 1, flag[j])
            return c

        def late(j, c):
            is_late = flag[j] == 2
            place[j] = jnp.where(is_late, c, 0)
            return c + is_late.astype(I32)

        def early(j, c):
            at, behind, row = c
            is_early = flag[j] == 1
            fits = at < early_slots
            pos = jnp.where(fits, at, behind)
            pos = jnp.where(is_early, pos, place[j])
            place[j] = pos
            used = flag[j] > 0
            row = jnp.where((lane == pos) & used, j, row)
            at = at + (is_early & fits).astype(I32)
            behind = behind + (is_early & jnp.logical_not(fits)).astype(I32)
            return at, behind, row

        def assign(i, c):
            slot[i] = jnp.where(away(i) == g, g * tiles + place[tile[i]], slot[i])
            return c

        lax.fori_loop(0, tiles, clear, 0)
        lax.fori_loop(0, blocks, mark, 0)
        for b in range(levels):
            for f in range(width):
                i = face_ids[f, b]
                j = tile[i]
                flag[j] = jnp.where(away(i) == g, 2, flag[j])
        behind = lax.fori_loop(0, tiles, late, early_slots)
        _, _, row = lax.fori_loop(
            0, tiles, early, (0, behind, jnp.zeros(rows.shape[1:], I32))
        )
        lax.fori_loop(0, blocks, assign, 0)
        rows[g - 1] = row.astype(F32).astype(BF16)


def first_kernel(groups, ids, layer, tile, face_ids, tiles, warmth, kind, amps, diag, *refs):
    packed, state_out, field_out, scale, warmth_v, kind_v, slot, rows = refs[:8]
    tiles_v, field, flag, place, sems, later_sems = refs[8:]
    blocks = packed.shape[0]
    step = blocks // sems.shape[0]
    copies = []
    later = [
        pltpu.make_async_copy(warmth, warmth_v, later_sems.at[0]),
        pltpu.make_async_copy(kind, kind_v, later_sems.at[1]),
    ]
    for p in range(0, blocks, step):
        part = pl.ds(p, step)
        copies.append(
            pltpu.make_async_copy(tiles.at[part], tiles_v.at[part], sems.at[p // step])
        )
    for c in copies + later:
        c.start()
    route(groups, layer, tile, face_ids, slot, rows, flag, place)
    turned = (relax_factor / diag[...]).T
    for i in range(blocks):
        s = column(turned, i, scale.shape[2])
        scale[i] = s
        field[i] = (s * amps[i].astype(F32)).astype(BF16)
    for i in range(blocks):
        if i % step == 0:
            copies[i // step].wait()
        row = joined(tiles_v, i)
        packed[i] = row
        image = jnp.dot(row, picked(field, ids, i), preferred_element_type=F32)
        a = amps[i].astype(F32)
        s = scale[i]
        x = s * a - relax_factor * field[i].astype(F32) + s * (a - image)
        state_out[i] = x
        field_out[i] = x.astype(BF16)
    for c in later:
        c.wait()


def near_kernel(ids, packed, field, state, amps, scale, state_out, field_out, *for_heat):
    for i in range(packed.shape[0]):
        image = jnp.dot(packed[i], picked(field, ids, i), preferred_element_type=F32)
        x = state[i] - relax_factor * field[i].astype(F32)
        x = x + scale[i] * (amps[i].astype(F32) - image)
        state_out[i] = x
        field_out[i] = x.astype(BF16)
    if for_heat:
        heat, diag = for_heat
        heat[...] = jnp.zeros(heat.shape, F32)
        for i in range(packed.shape[0]):
            diag[i] = relax_factor / scale[i]


def other_half(bit):
    return 1 - lax.rem(lax.div(lax.axis_index("elec"), 1 << bit), 2)


def face_terms(levels, face_ids, admittance, incoming, terms):
    width, points = face_ids.shape[0], terms.shape[1]
    for b in range(levels):
        for f in range(width):
            rows = slice(f * points, (f + 1) * points)
            block = incoming[b][rows] if b != GATHERED else incoming[b][other_half(b), rows]
            terms[b * width + f] = jnp.dot(
                admittance[b * width + f], block, preferred_element_type=F32
            )


def in_level_order(refs, order):
    return [refs[order.index(b)] for b in range(len(order))]


def update_faces(face_ids, admittance, scale, incoming, state, field, faces, terms):
    levels, width, points = len(faces), face_ids.shape[0], terms.shape[1]
    face_terms(levels, face_ids, admittance, incoming, terms)
    for b in range(levels):
        for f in range(width):
            i = face_ids[f, b]
            state[i] = state[i] - scale[i] * terms[b * width + f]
    for b in range(levels):
        for f in range(width):
            i = face_ids[f, b]
            x = state[i].astype(BF16)
            field[i] = x
            faces[b][f * points : (f + 1) * points] = x


def face_kernel(order, token, face_ids, admittance, scale, *refs):
    levels = len(order)
    incoming = in_level_order(refs[:levels], order)
    state, field = refs[levels + 2 : levels + 4]
    faces, terms = refs[levels + 4 : 2 * levels + 4], refs[-1]
    update_faces(face_ids, admittance, scale, incoming, state, field, faces, terms)


def heat_kernel(
    order, spots, slot, ids, face_ids, admittance, scale, packed, diag, rows, edges, *refs
):
    levels = len(order)
    incoming = in_level_order(refs[:levels], order)
    state, field, heat, soon = refs[levels + 3 : levels + 7]
    faces, terms = refs[levels + 7 : 2 * levels + 7], refs[-1]
    groups, points = soon.shape[0] + 1, heat.shape[1]
    tiles = heat.shape[0] // groups
    update_faces(face_ids, admittance, scale, incoming, state, field, faces, terms)
    for i in range(packed.shape[0]):
        image = jnp.dot(packed[i], picked(field, ids, i), preferred_element_type=F32)
        v = field[i].astype(F32)
        s = slot[i]
        heat[s] = heat[s] + v * (diag[i] * v + image)
    for g in range(1, groups):
        blocks = [heat[g * tiles + p].astype(BF16) for p in range(spots)]
        blocks += [edges[g - 1, z] for z in range(ZB)]
        for p, block in enumerate(blocks):
            soon[g - 1, p * points : (p + 1) * points] = block
        soon[g - 1, len(blocks) * points :] = rows[g - 1]


def heat_face_kernel(order, slot, face_ids, admittance, *refs):
    levels = len(order)
    incoming = in_level_order(refs[:levels], order)
    heat, field, late, terms = refs[levels + 2 :]
    groups, spots = late.shape[0] + 1, late.shape[1]
    tiles = heat.shape[0] // groups
    width = face_ids.shape[0]
    face_terms(levels, face_ids, admittance, incoming, terms)
    for b in range(levels):
        for f in range(width):
            i = face_ids[f, b]
            s = slot[i]
            heat[s] = heat[s] + field[i].astype(F32) * terms[b * width + f]
    for g in range(1, groups):
        late[g - 1] = heat[(g + 1) * tiles - spots : (g + 1) * tiles].astype(BF16)


def kappa_columns(kappas, kind):
    kinds = kind[...]
    kappa = jnp.zeros(kinds.shape, F32)
    for m in range(kappas.shape[0]):
        kappa = jnp.where(kinds == m, kappas[m], kappa)
    return kappa.T


def block_flux(kappa, warmth):
    w = warmth.astype(F32)
    return (kappa * (1.0 + 0.4 * jnp.tanh(w)) * w).astype(BF16)


def edge_kernel(token, kappas, kind, warmth, edges):
    turned = kappa_columns(kappas, kind)
    tiles, points, width = warmth.shape
    shifts = edges.shape[0]
    sends_top = lax.axis_index("therm") == 0
    for z in range(ZB):
        top = tiles - ZB + z
        low = block_flux(column(turned, z, width), warmth[z])
        high = block_flux(column(turned, top, width), warmth[top])
        for s in range(1, shifts - 1):
            edges[s, z] = low
        if shifts == 1:
            edges[0, z] = jnp.where(sends_top, high.astype(F32), low.astype(F32)).astype(BF16)
        else:
            edges[0, z] = high
            edges[shifts - 1, z] = low


def conduction_kernel(
    ids,
    kappas,
    tiles,
    kind,
    coefficient,
    storage,
    warmth,
    heat,
    rest,
    gain,
    flux,
):
    count = tiles.shape[0]
    width = flux.shape[2]
    turned = kappa_columns(kappas, kind)
    for i in range(count):
        flux[i] = block_flux(column(turned, i, width), warmth[i])
    diag = coefficient[...].T
    gains = (time_increment / storage[...]).T
    for i in range(count):
        image = jnp.dot(joined(tiles, i), picked(flux, ids, i), preferred_element_type=F32)
        image = image + column(diag, i, width) * flux[i].astype(F32)
        g = column(gains, i, width)
        gain[i] = g
        rest[i] = warmth[i].astype(F32) - g * image


def early_kernel(shifts, heat, gain, couplings, *refs):
    maps, soon = refs[:shifts], refs[shifts : 2 * shifts]
    rest, field, out = refs[2 * shifts + 2 : 2 * shifts + 5]
    spots, sem = refs[2 * shifts + 5 : -1], refs[-1]
    tiles, points = rest.shape[:2]
    sent = tiles - spots[0].shape[0]
    own = lax.axis_index("therm")
    lowest = (own > 0).astype(F32)
    highest = (own < shifts).astype(F32)
    terms = []
    for z in range(ZB):
        at = slice((sent + z) * points, (sent + z + 1) * points)
        low = jnp.dot(couplings[z], soon[0][at], preferred_element_type=F32)
        high = jnp.dot(couplings[ZB + z], soon[-1][at], preferred_element_type=F32)
        terms += [(z, lowest * low), (tiles - ZB + z, highest * high)]
    for j, term in terms:
        rest[j] = rest[j] - gain[j] * term
    for i in range(tiles):
        rest[i] = rest[i] + gain[i] * heat[i]
    for g in range(shifts):
        for p in range(sent):
            j = maps[g][p]
            rest[j] = rest[j] + gain[j] * soon[g][p * points : (p + 1) * points].astype(F32)
    whole = pltpu.make_async_copy(rest, out, sem)
    whole.start()
    for g in range(shifts):
        for p in range(spots[g].shape[0]):
            spots[g][p] = maps[g][tiles - spots[g].shape[0] + p]
    whole.wait()


def late_kernel(shifts, gain, *refs):
    maps, late = refs[:shifts], refs[shifts : 2 * shifts]
    rest, out, sems = refs[2 * shifts], refs[2 * shifts + 2], refs[2 * shifts + 3]
    spots = late[0].shape[0]
    for g in range(shifts):
        for p in range(spots):
            j = maps[g][p]
            rest[j] = rest[j] + gain[j] * late[g][p].astype(F32)
    copies = []
    for g in range(shifts):
        for p in range(spots):
            j = maps[g][p]
            copies.append(pltpu.make_async_copy(rest.at[j], out.at[j], sems.at[g * spots + p]))
    for c in copies:
        c.start()
    for c in copies:
        c.wait()


def body(
    injected_amperage,
    voltage_self_admittance,
    voltage_coupling_tiles,
    voltage_partner_tile_ids,
    interface_tiles_per_level,
    interface_admittance,
    warmth_receiver_layer,
    warmth_receiver_tile,
    warmth_values,
    warmth_self_coefficient,
    warmth_coupling_tiles,
    warmth_partner_tile_ids,
    layer_boundary_couplings,
    substance_kind,
    reference_material_kappas,
    warmth_storage_per_point,
):
    blocks, points, regimes = injected_amperage.shape
    tiles = warmth_values.shape[0]
    levels, width = interface_tiles_per_level.shape
    links = voltage_partner_tile_ids.shape[1]
    groups = lax.axis_size("therm")
    shifts = groups - 1
    whole = (blocks, points, regimes)
    warm = (tiles, points, regimes)
    face = (width * points, regimes)
    late_spots = min(levels * width, tiles)
    early_spots = tiles - late_spots
    sent_rows = (early_spots + ZB) * points
    near_flops = 2 * blocks * links * points * points * regimes
    terms = pltpu.VMEM((levels * width, points, regimes), F32)
    dma = pltpu.SemaphoreType.DMA

    def exchange(faces, order):
        return [
            from_partner(faces[b], "elec", b) if b != GATHERED else both_halves(faces[b], "elec", b)
            for b in order
        ]

    far_first = list(range(levels))[::-1]

    amps, diag, face_ids, ids, layer, tile, *faces = call(
        functools.partial(start_kernel, levels),
        [
            (whole, BF16, VM),
            (voltage_self_admittance.shape, F32, VM),
            ((width, levels), I32, SM),
            ((links, blocks), I32, SM),
            ((1, blocks), I32, SM),
            ((blocks,), I32, SM),
        ]
        + [(face, BF16, VM)] * levels,
        on(
            HB,
            injected_amperage,
            voltage_self_admittance,
            interface_tiles_per_level.T,
            voltage_partner_tile_ids.T,
            warmth_receiver_layer.T,
            warmth_receiver_tile,
        ),
        "start",
        scratch=[dma((6,))],
    )
    order = far_first
    incoming = exchange(faces, order)

    packed, state, field, scale, warmth, kind, slot, rows = call(
        functools.partial(first_kernel, groups),
        [
            ((blocks, points, links * points), BF16, VM),
            (whole, F32, VM),
            (whole, BF16, VM),
            (whole, F32, VM),
            (warm, BF16, VM),
            (substance_kind.shape, I32, VM),
            ((blocks,), I32, SM),
            ((shifts, 16, regimes), BF16, VM),
        ],
        on(SM, ids, layer, tile, face_ids)
        + on(HB, voltage_coupling_tiles, warmth_values, substance_kind)
        + on(VM, amps, diag),
        "first",
        scratch=[
            pltpu.VMEM(voltage_coupling_tiles.shape, BF16),
            pltpu.VMEM(whole, BF16),
            pltpu.SMEM((tiles,), I32),
            pltpu.SMEM((tiles,), I32),
            dma((4,)),
            dma((2,)),
        ],
        flops=near_flops,
        limit=8 << 20,
    )
    for sweep_index in range(SWEEPS - 1):
        if sweep_index:
            last = sweep_index == SWEEPS - 2
            state, field, *for_heat = call(
                near_kernel,
                [(whole, F32, VM), (whole, BF16, VM)]
                + [((groups * tiles, points, regimes), F32, VM), (whole, F32, VM)] * last,
                on(SM, ids) + on(VM, packed, field, state, amps, scale),
                "near",
                flops=near_flops,
            )
        token = scale
        if sweep_index == 1:
            (edges,) = call(
                edge_kernel,
                [((shifts, ZB, points, regimes), BF16, VM)],
                on(ANY, field) + on(SM, reference_material_kappas) + on(VM, kind, warmth),
                "edge",
            )
            token = edges
        if sweep_index < SWEEPS - 2:
            state, field, *faces = call(
                functools.partial(face_kernel, order),
                [(whole, F32, VM), (whole, BF16, VM)] + [(face, BF16, VM)] * levels,
                on(ANY, token)
                + on(SM, face_ids)
                + on(VM, interface_admittance, scale, *incoming, state, field),
                "face",
                aliases={levels + 4: 0, levels + 5: 1},
                scratch=[terms],
            )
            incoming = exchange(faces, order)

    heat, diag = for_heat
    _, field, heat, soon, *faces = call(
        functools.partial(heat_kernel, order, early_spots),
        [
            (whole, F32, VM),
            (whole, BF16, VM),
            (heat.shape, F32, VM),
            ((shifts, sent_rows + rows.shape[1], regimes), BF16, VM),
        ]
        + [(face, BF16, VM)] * levels,
        on(SM, slot, ids, face_ids)
        + on(VM, interface_admittance, scale, packed, diag, rows, edges, *incoming)
        + on(VM, state, field, heat),
        "heat",
        aliases={9 + levels + n: n for n in range(3)},
        scratch=[terms],
        flops=near_flops,
    )
    routes = [[(i, (i + s) % groups) for i in range(groups)] for s in range(1, groups)]
    soon = [lax.ppermute(soon[s], "therm", routes[s]) for s in range(shifts)]
    maps = [x[sent_rows, :tiles].astype(I32) for x in soon]
    order = far_first
    incoming = exchange(faces, order)

    rest, gain = call(
        conduction_kernel,
        [(warm, F32, VM), (warm, F32, VM)],
        on(SM, warmth_partner_tile_ids.T, reference_material_kappas)
        + on(
            VM,
            warmth_coupling_tiles,
            kind,
            warmth_self_coefficient,
            warmth_storage_per_point,
            warmth,
        )
        + on(ANY, heat),
        "conduction",
        scratch=[pltpu.VMEM(warm, BF16)],
        flops=near_flops,
    )
    heat, field, late = call(
        functools.partial(heat_face_kernel, order),
        [
            ((groups * tiles, points, regimes), F32, VM),
            (whole, BF16, VM),
            ((shifts, late_spots, points, regimes), BF16, VM),
        ],
        on(SM, slot, face_ids) + on(VM, interface_admittance, *incoming, heat, field),
        "heat_face",
        aliases={levels + 3: 0, levels + 4: 1},
        scratch=[terms],
    )
    late = [lax.ppermute(late[s], "therm", routes[s]) for s in range(shifts)]
    rest, voltage_solution, out, *maps = call(
        functools.partial(early_kernel, shifts),
        [(warm, F32, VM), (whole, BF16, VM), (warm, F32, HB)] + [((late_spots,), I32, SM)] * shifts,
        on(VM, heat, gain, layer_boundary_couplings) + on(SM, *maps) + on(VM, *soon, rest, field),
        "early",
        aliases={3 + 2 * shifts: 0, 4 + 2 * shifts: 1},
        scratch=[dma],
    )
    (advanced_warmth_values,) = call(
        functools.partial(late_kernel, shifts),
        [(warm, F32, HB)],
        on(VM, gain) + on(SM, *maps) + on(VM, *late, rest) + on(HB, out),
        "late",
        aliases={2 + 2 * shifts: 0},
        scratch=[dma((shifts * late_spots,))],
    )
    return (voltage_solution, advanced_warmth_values)


def solution(mesh):
    split = P(("elec", "therm"))
    return jax.shard_map(
        body,
        mesh=mesh,
        in_specs=(split,) * 14 + (P(), split),
        out_specs=(split, split),
        check_vma=False,
    )
```

```python
import functools

import jax
import jax.numpy as jnp
from jax import lax
from jax.experimental import pallas as pl
from jax.experimental.pallas import tpu as pltpu
from jax.sharding import PartitionSpec as P

SWEEPS = 5
ZB = 2

relax_factor = 0.8
time_increment = 0.5

F32 = jnp.float32
BF16 = jnp.bfloat16
I32 = jnp.int32
VM = pl.BlockSpec(memory_space=pltpu.VMEM)
SM = pl.BlockSpec(memory_space=pltpu.SMEM)
HB = pl.BlockSpec(memory_space=pltpu.HBM)
ANY = pl.BlockSpec(memory_space=pl.ANY)
SPACES = {id(VM): pltpu.VMEM, id(HB): pltpu.HBM, id(SM): pltpu.SMEM}
LIMIT = 4 << 20


def call(kernel, outs, ins, name, aliases={}, scratch=(), flops=0, limit=LIMIT):
    args = []
    for x, spec in ins:
        if spec is VM or spec is HB:
            x = pltpu.with_memory_space_constraint(x, SPACES[id(spec)])
        args.append(x)
    return pl.pallas_call(
        kernel,
        out_shape=[SPACES[id(spec)](shape, dtype) for shape, dtype, spec in outs],
        in_specs=[spec for _, spec in ins],
        out_specs=[spec for _, _, spec in outs],
        input_output_aliases=aliases,
        scratch_shapes=scratch,
        compiler_params=pltpu.CompilerParams(vmem_limit_bytes=limit),
        cost_estimate=pl.CostEstimate(flops=flops, bytes_accessed=0, transcendentals=0),
        name=name,
    )(*args)


def on(spec, *arrays):
    return [(x, spec) for x in arrays]


def from_partner(block, axis, bit):
    count = lax.axis_size(axis)
    route = []
    for low in range(count):
        high = low | 1 << bit
        if high != low and high < count:
            route += [(low, high), (high, low)]
    return lax.ppermute(block, axis, route)


def column(table, row, width):
    return jnp.broadcast_to(table[:, row : row + 1], (table.shape[0], width))


def joined(tiles_ref, row):
    return jnp.concatenate([tiles_ref[row, k] for k in range(tiles_ref.shape[1])], axis=1)


def picked(field_ref, ids_ref, row):
    return jnp.concatenate([field_ref[ids_ref[k, row]] for k in range(ids_ref.shape[0])], axis=0)


def start_kernel(levels, amps, diag, face_ids, *refs):
    small = refs[:3]
    amps_v, diag_v, face_ids_s = refs[3:6]
    small_s, faces, sems = refs[6:9], refs[9 : 9 + levels], refs[-1]
    parts = 8
    step = amps.shape[0] // parts
    pairs = [(face_ids, face_ids_s), (diag, diag_v)]
    for p in range(parts):
        rows = pl.ds(p * step, step)
        pairs.append((amps.at[rows], amps_v.at[rows]))
    copies = [
        pltpu.make_async_copy(a, b, sems.at[n])
        for n, (a, b) in enumerate(pairs + list(zip(small, small_s)))
    ]
    for c in copies:
        c.start()
    copies[0].wait()
    copies[1].wait()
    scale = relax_factor / diag_v[...]
    rows = lax.broadcasted_iota(I32, scale.shape, 0)
    chosen = []
    for b in range(levels):
        for f in range(face_ids.shape[0]):
            mine = jnp.where(rows == face_ids_s[f, b], scale, 0.0)
            chosen.append(jnp.sum(mine, axis=0, keepdims=True))
    turned = jnp.concatenate(chosen, axis=0).T
    for c in copies[2 : 2 + parts]:
        c.wait()
    for b in range(levels):
        for f in range(face_ids.shape[0]):
            s = column(turned, b * face_ids.shape[0] + f, amps.shape[2])
            points = amps.shape[1]
            block = s * amps_v[face_ids_s[f, b]].astype(F32)
            faces[b][f * points : (f + 1) * points] = block.astype(BF16)
    for c in copies[2 + parts :]:
        c.wait()


def route(groups, layer, tile, face_ids, slot, rows, flag, place):
    own = lax.axis_index("therm")
    blocks, tiles = slot.shape[0], flag.shape[0]
    levels, width = face_ids.shape[1], face_ids.shape[0]
    early_slots = max(tiles - levels * width, 0)
    lane = lax.broadcasted_iota(I32, rows.shape[1:], 1)

    def away(i):
        a = layer[0, i] - own
        return jnp.where(a < 0, a + groups, a)

    def home(i, c):
        slot[i] = tile[i]
        return c

    lax.fori_loop(0, blocks, home, 0)
    for g in range(1, groups):

        def clear(j, c):
            flag[j] = 0
            return c

        def mark(i, c):
            j = tile[i]
            flag[j] = jnp.where(away(i) == g, 1, flag[j])
            return c

        def late(j, c):
            is_late = flag[j] == 2
            place[j] = jnp.where(is_late, c, 0)
            return c + is_late.astype(I32)

        def early(j, c):
            at, behind, row = c
            is_early = flag[j] == 1
            fits = at < early_slots
            pos = jnp.where(fits, at, behind)
            pos = jnp.where(is_early, pos, place[j])
            place[j] = pos
            used = flag[j] > 0
            row = jnp.where((lane == pos) & used, j, row)
            at = at + (is_early & fits).astype(I32)
            behind = behind + (is_early & jnp.logical_not(fits)).astype(I32)
            return at, behind, row

        def assign(i, c):
            slot[i] = jnp.where(away(i) == g, g * tiles + place[tile[i]], slot[i])
            return c

        lax.fori_loop(0, tiles, clear, 0)
        lax.fori_loop(0, blocks, mark, 0)
        for b in range(levels):
            for f in range(width):
                i = face_ids[f, b]
                j = tile[i]
                flag[j] = jnp.where(away(i) == g, 2, flag[j])
        behind = lax.fori_loop(0, tiles, late, early_slots)
        _, _, row = lax.fori_loop(
            0, tiles, early, (0, behind, jnp.zeros(rows.shape[1:], I32))
        )
        lax.fori_loop(0, blocks, assign, 0)
        rows[g - 1] = row.astype(F32).astype(BF16)


def first_kernel(groups, ids, layer, tile, face_ids, tiles, warmth, kind, amps, diag, *refs):
    packed, state_out, field_out, scale, warmth_v, kind_v, slot, rows = refs[:8]
    tiles_v, field, flag, place, sems, later_sems = refs[8:]
    blocks = packed.shape[0]
    step = blocks // sems.shape[0]
    copies = []
    later = [
        pltpu.make_async_copy(warmth, warmth_v, later_sems.at[0]),
        pltpu.make_async_copy(kind, kind_v, later_sems.at[1]),
    ]
    for p in range(0, blocks, step):
        part = pl.ds(p, step)
        copies.append(
            pltpu.make_async_copy(tiles.at[part], tiles_v.at[part], sems.at[p // step])
        )
    for c in copies + later:
        c.start()
    route(groups, layer, tile, face_ids, slot, rows, flag, place)
    turned = (relax_factor / diag[...]).T
    for i in range(blocks):
        s = column(turned, i, scale.shape[2])
        scale[i] = s
        field[i] = (s * amps[i].astype(F32)).astype(BF16)
    for i in range(blocks):
        if i % step == 0:
            copies[i // step].wait()
        row = joined(tiles_v, i)
        packed[i] = row
        image = jnp.dot(row, picked(field, ids, i), preferred_element_type=F32)
        a = amps[i].astype(F32)
        s = scale[i]
        x = s * a - relax_factor * field[i].astype(F32) + s * (a - image)
        state_out[i] = x
        field_out[i] = x.astype(BF16)
    for c in later:
        c.wait()


def near_kernel(ids, packed, field, state, amps, scale, state_out, field_out, *for_heat):
    for i in range(packed.shape[0]):
        image = jnp.dot(packed[i], picked(field, ids, i), preferred_element_type=F32)
        x = state[i] - relax_factor * field[i].astype(F32)
        x = x + scale[i] * (amps[i].astype(F32) - image)
        state_out[i] = x
        field_out[i] = x.astype(BF16)
    if for_heat:
        heat, diag = for_heat
        heat[...] = jnp.zeros(heat.shape, F32)
        for i in range(packed.shape[0]):
            diag[i] = relax_factor / scale[i]


def face_terms(levels, face_ids, admittance, incoming, terms):
    width, points = face_ids.shape[0], terms.shape[1]
    for b in range(levels):
        for f in range(width):
            block = incoming[b][f * points : (f + 1) * points]
            terms[b * width + f] = jnp.dot(
                admittance[b * width + f], block, preferred_element_type=F32
            )


def in_level_order(refs, order):
    return [refs[order.index(b)] for b in range(len(order))]


def update_faces(face_ids, admittance, scale, incoming, state, field, faces, terms):
    levels, width, points = len(faces), face_ids.shape[0], terms.shape[1]
    face_terms(levels, face_ids, admittance, incoming, terms)
    for b in range(levels):
        for f in range(width):
            i = face_ids[f, b]
            state[i] = state[i] - scale[i] * terms[b * width + f]
    for b in range(levels):
        for f in range(width):
            i = face_ids[f, b]
            x = state[i].astype(BF16)
            field[i] = x
            faces[b][f * points : (f + 1) * points] = x


def face_kernel(order, token, face_ids, admittance, scale, *refs):
    levels = len(order)
    incoming = in_level_order(refs[:levels], order)
    state, field = refs[levels + 2 : levels + 4]
    faces, terms = refs[levels + 4 : 2 * levels + 4], refs[-1]
    update_faces(face_ids, admittance, scale, incoming, state, field, faces, terms)


def heat_kernel(
    order, spots, token, slot, ids, face_ids, admittance, scale, packed, diag, rows, *refs
):
    levels = len(order)
    incoming = in_level_order(refs[:levels], order)
    state, field, heat, soon = refs[levels + 3 : levels + 7]
    faces, terms = refs[levels + 7 : 2 * levels + 7], refs[-1]
    groups, points = soon.shape[0] + 1, heat.shape[1]
    tiles = heat.shape[0] // groups
    update_faces(face_ids, admittance, scale, incoming, state, field, faces, terms)
    for i in range(packed.shape[0]):
        image = jnp.dot(packed[i], picked(field, ids, i), preferred_element_type=F32)
        v = field[i].astype(F32)
        s = slot[i]
        heat[s] = heat[s] + v * (diag[i] * v + image)
    for g in range(1, groups):
        blocks = [heat[g * tiles + p].astype(BF16) for p in range(spots)]
        for p, block in enumerate(blocks):
            soon[g - 1, p * points : (p + 1) * points] = block
        soon[g - 1, len(blocks) * points :] = rows[g - 1]


def heat_face_kernel(order, slot, face_ids, admittance, *refs):
    levels = len(order)
    incoming = in_level_order(refs[:levels], order)
    heat, field, late, terms = refs[levels + 2 :]
    groups, spots = late.shape[0] + 1, late.shape[1]
    tiles = heat.shape[0] // groups
    width = face_ids.shape[0]
    face_terms(levels, face_ids, admittance, incoming, terms)
    for b in range(levels):
        for f in range(width):
            i = face_ids[f, b]
            s = slot[i]
            heat[s] = heat[s] + field[i].astype(F32) * terms[b * width + f]
    for g in range(1, groups):
        late[g - 1] = heat[(g + 1) * tiles - spots : (g + 1) * tiles].astype(BF16)


def kappa_columns(kappas, kind):
    kinds = kind[...]
    kappa = jnp.zeros(kinds.shape, F32)
    for m in range(kappas.shape[0]):
        kappa = jnp.where(kinds == m, kappas[m], kappa)
    return kappa.T


def block_flux(kappa, warmth):
    w = warmth.astype(F32)
    return (kappa * (1.0 + 0.4 * jnp.tanh(w)) * w).astype(BF16)


def edge_kernel(token, kappas, kind, warmth, *edges):
    turned = kappa_columns(kappas, kind)
    tiles, points, width = warmth.shape
    sends_top = lax.axis_index("therm") == 0
    for z in range(ZB):
        top = tiles - ZB + z
        low = block_flux(column(turned, z, width), warmth[z])
        high = block_flux(column(turned, top, width), warmth[top])
        if len(edges) == 1:
            both = jnp.where(sends_top, high.astype(F32), low.astype(F32))
            edges[0][z] = both.astype(BF16)
        else:
            edges[0][z], edges[1][z] = low, high


def conduction_kernel(
    groups,
    ids,
    kappas,
    tiles,
    kind,
    coefficient,
    storage,
    couplings,
    warmth,
    below,
    above,
    heat,
    rest,
    gain,
    flux,
):
    count = tiles.shape[0]
    width = flux.shape[2]
    turned = kappa_columns(kappas, kind)
    for i in range(count):
        flux[i] = block_flux(column(turned, i, width), warmth[i])
    own = lax.axis_index("therm")
    lowest = (own > 0).astype(F32)
    highest = (own < groups - 1).astype(F32)
    diag = coefficient[...].T
    gains = (time_increment / storage[...]).T
    for i in range(count):
        image = jnp.dot(joined(tiles, i), picked(flux, ids, i), preferred_element_type=F32)
        image = image + column(diag, i, width) * flux[i].astype(F32)
        if i < ZB:
            term = jnp.dot(couplings[i], below[i], preferred_element_type=F32)
            image = image + lowest * term
        if i >= count - ZB:
            z = i - (count - ZB)
            term = jnp.dot(couplings[ZB + z], above[z], preferred_element_type=F32)
            image = image + highest * term
        g = column(gains, i, width)
        gain[i] = g
        rest[i] = warmth[i].astype(F32) - g * image


def early_kernel(shifts, heat, gain, *refs):
    maps, soon = refs[:shifts], refs[shifts : 2 * shifts]
    rest, field, out = refs[2 * shifts + 2 : 2 * shifts + 5]
    spots, sem = refs[2 * shifts + 5 : -1], refs[-1]
    tiles, points = rest.shape[:2]
    sent = tiles - spots[0].shape[0]
    for i in range(tiles):
        rest[i] = rest[i] + gain[i] * heat[i]
    for g in range(shifts):
        for p in range(sent):
            j = maps[g][p]
            rest[j] = rest[j] + gain[j] * soon[g][p * points : (p + 1) * points].astype(F32)
    whole = pltpu.make_async_copy(rest, out, sem)
    whole.start()
    for g in range(shifts):
        for p in range(spots[g].shape[0]):
            spots[g][p] = maps[g][tiles - spots[g].shape[0] + p]
    whole.wait()


def late_kernel(shifts, gain, *refs):
    maps, late = refs[:shifts], refs[shifts : 2 * shifts]
    rest, out, sems = refs[2 * shifts], refs[2 * shifts + 2], refs[2 * shifts + 3]
    spots = late[0].shape[0]
    for g in range(shifts):
        for p in range(spots):
            j = maps[g][p]
            rest[j] = rest[j] + gain[j] * late[g][p].astype(F32)
    copies = []
    for g in range(shifts):
        for p in range(spots):
            j = maps[g][p]
            copies.append(pltpu.make_async_copy(rest.at[j], out.at[j], sems.at[g * spots + p]))
    for c in copies:
        c.start()
    for c in copies:
        c.wait()


def body(
    injected_amperage,
    voltage_self_admittance,
    voltage_coupling_tiles,
    voltage_partner_tile_ids,
    interface_tiles_per_level,
    interface_admittance,
    warmth_receiver_layer,
    warmth_receiver_tile,
    warmth_values,
    warmth_self_coefficient,
    warmth_coupling_tiles,
    warmth_partner_tile_ids,
    layer_boundary_couplings,
    substance_kind,
    reference_material_kappas,
    warmth_storage_per_point,
):
    blocks, points, regimes = injected_amperage.shape
    tiles = warmth_values.shape[0]
    levels, width = interface_tiles_per_level.shape
    links = voltage_partner_tile_ids.shape[1]
    groups = lax.axis_size("therm")
    shifts = groups - 1
    whole = (blocks, points, regimes)
    warm = (tiles, points, regimes)
    face = (width * points, regimes)
    late_spots = min(levels * width, tiles)
    early_spots = tiles - late_spots
    sent_rows = early_spots * points
    near_flops = 2 * blocks * links * points * points * regimes
    terms = pltpu.VMEM((levels * width, points, regimes), F32)
    dma = pltpu.SemaphoreType.DMA

    def exchange(faces, order):
        return [from_partner(faces[b], "elec", b) for b in order]

    far_first = list(range(levels))[::-1]

    amps, diag, face_ids, ids, layer, tile, *faces = call(
        functools.partial(start_kernel, levels),
        [
            (whole, BF16, VM),
            (voltage_self_admittance.shape, F32, VM),
            ((width, levels), I32, SM),
            ((links, blocks), I32, SM),
            ((1, blocks), I32, SM),
            ((blocks,), I32, SM),
        ]
        + [(face, BF16, VM)] * levels,
        on(
            HB,
            injected_amperage,
            voltage_self_admittance,
            interface_tiles_per_level.T,
            voltage_partner_tile_ids.T,
            warmth_receiver_layer.T,
            warmth_receiver_tile,
        ),
        "start",
        scratch=[dma((13,))],
    )
    order = far_first
    incoming = exchange(faces, order)

    packed, state, field, scale, warmth, kind, slot, rows = call(
        functools.partial(first_kernel, groups),
        [
            ((blocks, points, links * points), BF16, VM),
            (whole, F32, VM),
            (whole, BF16, VM),
            (whole, F32, VM),
            (warm, BF16, VM),
            (substance_kind.shape, I32, VM),
            ((blocks,), I32, SM),
            ((shifts, 16, regimes), BF16, VM),
        ],
        on(SM, ids, layer, tile, face_ids)
        + on(HB, voltage_coupling_tiles, warmth_values, substance_kind)
        + on(VM, amps, diag),
        "first",
        scratch=[
            pltpu.VMEM(voltage_coupling_tiles.shape, BF16),
            pltpu.VMEM(whole, BF16),
            pltpu.SMEM((tiles,), I32),
            pltpu.SMEM((tiles,), I32),
            dma((4,)),
            dma((2,)),
        ],
        flops=near_flops,
        limit=8 << 20,
    )
    for sweep_index in range(SWEEPS - 1):
        if sweep_index:
            last = sweep_index == SWEEPS - 2
            state, field, *for_heat = call(
                near_kernel,
                [(whole, F32, VM), (whole, BF16, VM)]
                + [((groups * tiles, points, regimes), F32, VM), (whole, F32, VM)] * last,
                on(SM, ids) + on(VM, packed, field, state, amps, scale),
                "near",
                flops=near_flops,
            )
        token = scale
        if sweep_index == 1:
            edges = call(
                edge_kernel,
                [((ZB, points, regimes), BF16, VM)] * min(2, shifts),
                on(ANY, field) + on(SM, reference_material_kappas) + on(VM, kind, warmth),
                "edge",
            )
            token = edges[0]
        if sweep_index < SWEEPS - 2:
            state, field, *faces = call(
                functools.partial(face_kernel, order),
                [(whole, F32, VM), (whole, BF16, VM)] + [(face, BF16, VM)] * levels,
                on(ANY, token)
                + on(SM, face_ids)
                + on(VM, interface_admittance, scale, *incoming, state, field),
                "face",
                aliases={levels + 4: 0, levels + 5: 1},
                scratch=[terms],
            )
            incoming = exchange(faces, order)

    if groups == 2:
        below = above = lax.ppermute(edges[0], "therm", [(0, 1), (1, 0)])
    else:
        up = [(i, i + 1) for i in range(groups - 1)]
        above = lax.ppermute(edges[0], "therm", [(j, i) for i, j in up])
        below = lax.ppermute(edges[1], "therm", up)
    heat, diag = for_heat
    _, field, heat, soon, *faces = call(
        functools.partial(heat_kernel, order, early_spots),
        [
            (whole, F32, VM),
            (whole, BF16, VM),
            (heat.shape, F32, VM),
            ((shifts, sent_rows + rows.shape[1], regimes), BF16, VM),
        ]
        + [(face, BF16, VM)] * levels,
        on(ANY, above)
        + on(SM, slot, ids, face_ids)
        + on(VM, interface_admittance, scale, packed, diag, rows, *incoming)
        + on(VM, state, field, heat),
        "heat",
        aliases={9 + levels + n: n for n in range(3)},
        scratch=[terms],
        flops=near_flops,
    )
    routes = [[(i, (i + s) % groups) for i in range(groups)] for s in range(1, groups)]
    soon = [lax.ppermute(soon[s], "therm", routes[s]) for s in range(shifts)]
    maps = [x[sent_rows, :tiles].astype(I32) for x in soon]
    order = far_first
    incoming = exchange(faces, order)

    rest, gain = call(
        functools.partial(conduction_kernel, groups),
        [(warm, F32, VM), (warm, F32, VM)],
        on(SM, warmth_partner_tile_ids.T, reference_material_kappas)
        + on(
            VM,
            warmth_coupling_tiles,
            kind,
            warmth_self_coefficient,
            warmth_storage_per_point,
            layer_boundary_couplings,
            warmth,
            below,
            above,
        )
        + on(ANY, heat),
        "conduction",
        scratch=[pltpu.VMEM(warm, BF16)],
        flops=near_flops,
    )
    heat, field, late = call(
        functools.partial(heat_face_kernel, order),
        [
            ((groups * tiles, points, regimes), F32, VM),
            (whole, BF16, VM),
            ((shifts, late_spots, points, regimes), BF16, VM),
        ],
        on(SM, slot, face_ids) + on(VM, interface_admittance, *incoming, heat, field),
        "heat_face",
        aliases={levels + 3: 0, levels + 4: 1},
        scratch=[terms],
    )
    late = [lax.ppermute(late[s], "therm", routes[s]) for s in range(shifts)]
    rest, voltage_solution, out, *maps = call(
        functools.partial(early_kernel, shifts),
        [(warm, F32, VM), (whole, BF16, VM), (warm, F32, HB)] + [((late_spots,), I32, SM)] * shifts,
        on(VM, heat, gain) + on(SM, *maps) + on(VM, *soon, rest, field),
        "early",
        aliases={2 + 2 * shifts: 0, 3 + 2 * shifts: 1},
        scratch=[dma],
    )
    (advanced_warmth_values,) = call(
        functools.partial(late_kernel, shifts),
        [(warm, F32, HB)],
        on(VM, gain) + on(SM, *maps) + on(VM, *late, rest) + on(HB, out),
        "late",
        aliases={2 + 2 * shifts: 0},
        scratch=[dma((shifts * late_spots,))],
    )
    return (voltage_solution, advanced_warmth_values)


def solution(mesh):
    split = P(("elec", "therm"))
    return jax.shard_map(
        body,
        mesh=mesh,
        in_specs=(split,) * 14 + (P(), split),
        out_specs=(split, split),
        check_vma=False,
    )
```

```python
import functools

import jax
import jax.numpy as jnp
from jax import lax
from jax.experimental import pallas as pl
from jax.experimental.pallas import tpu as pltpu
from jax.sharding import PartitionSpec as P

SWEEPS = 5
ZB = 2

relax_factor = 0.8
time_increment = 0.5

F32 = jnp.float32
BF16 = jnp.bfloat16
I32 = jnp.int32
VM = pl.BlockSpec(memory_space=pltpu.VMEM)
SM = pl.BlockSpec(memory_space=pltpu.SMEM)
HB = pl.BlockSpec(memory_space=pltpu.HBM)
ANY = pl.BlockSpec(memory_space=pl.ANY)
SPACES = {id(VM): pltpu.VMEM, id(HB): pltpu.HBM, id(SM): pltpu.SMEM}
LIMIT = 4 << 20


def call(kernel, outs, ins, name, aliases={}, scratch=(), flops=0, limit=LIMIT):
    args = []
    for x, spec in ins:
        if spec is VM or spec is HB:
            x = pltpu.with_memory_space_constraint(x, SPACES[id(spec)])
        args.append(x)
    return pl.pallas_call(
        kernel,
        out_shape=[SPACES[id(spec)](shape, dtype) for shape, dtype, spec in outs],
        in_specs=[spec for _, spec in ins],
        out_specs=[spec for _, _, spec in outs],
        input_output_aliases=aliases,
        scratch_shapes=scratch,
        compiler_params=pltpu.CompilerParams(vmem_limit_bytes=limit),
        cost_estimate=pl.CostEstimate(flops=flops, bytes_accessed=0, transcendentals=0),
        name=name,
    )(*args)


def on(spec, *arrays):
    return [(x, spec) for x in arrays]


def from_partner(block, axis, bit):
    count = lax.axis_size(axis)
    route = []
    for low in range(count):
        high = low | 1 << bit
        if high != low and high < count:
            route += [(low, high), (high, low)]
    return lax.ppermute(block, axis, route)


def column(table, row, width):
    return jnp.broadcast_to(table[:, row : row + 1], (table.shape[0], width))


def joined(tiles_ref, row):
    return jnp.concatenate([tiles_ref[row, k] for k in range(tiles_ref.shape[1])], axis=1)


def picked(field_ref, ids_ref, row):
    return jnp.concatenate([field_ref[ids_ref[k, row]] for k in range(ids_ref.shape[0])], axis=0)


def start_kernel(levels, amps, diag, face_ids, *refs):
    small = refs[:3]
    amps_v, diag_v, face_ids_s = refs[3:6]
    small_s, faces, sems = refs[6:9], refs[9 : 9 + levels], refs[-1]
    pairs = [(face_ids, face_ids_s), (diag, diag_v), (amps, amps_v)]
    copies = [
        pltpu.make_async_copy(a, b, sems.at[n])
        for n, (a, b) in enumerate(pairs + list(zip(small, small_s)))
    ]
    for c in copies:
        c.start()
    copies[0].wait()
    copies[1].wait()
    scale = relax_factor / diag_v[...]
    rows = lax.broadcasted_iota(I32, scale.shape, 0)
    chosen = []
    for b in range(levels):
        for f in range(face_ids.shape[0]):
            mine = jnp.where(rows == face_ids_s[f, b], scale, 0.0)
            chosen.append(jnp.sum(mine, axis=0, keepdims=True))
    turned = jnp.concatenate(chosen, axis=0).T
    copies[2].wait()
    for b in range(levels):
        for f in range(face_ids.shape[0]):
            s = column(turned, b * face_ids.shape[0] + f, amps.shape[2])
            points = amps.shape[1]
            block = s * amps_v[face_ids_s[f, b]].astype(F32)
            faces[b][f * points : (f + 1) * points] = block.astype(BF16)
    for c in copies[3:]:
        c.wait()


def route(groups, layer, tile, face_ids, slot, rows, flag, place):
    own = lax.axis_index("therm")
    blocks, tiles = slot.shape[0], flag.shape[0]
    levels, width = face_ids.shape[1], face_ids.shape[0]
    early_slots = max(tiles - levels * width, 0)
    lane = lax.broadcasted_iota(I32, rows.shape[1:], 1)

    def away(i):
        a = layer[0, i] - own
        return jnp.where(a < 0, a + groups, a)

    def home(i, c):
        slot[i] = tile[i]
        return c

    lax.fori_loop(0, blocks, home, 0)
    for g in range(1, groups):

        def clear(j, c):
            flag[j] = 0
            return c

        def mark(i, c):
            j = tile[i]
            flag[j] = jnp.where(away(i) == g, 1, flag[j])
            return c

        def late(j, c):
            is_late = flag[j] == 2
            place[j] = jnp.where(is_late, c, 0)
            return c + is_late.astype(I32)

        def early(j, c):
            at, behind, row = c
            is_early = flag[j] == 1
            fits = at < early_slots
            pos = jnp.where(fits, at, behind)
            pos = jnp.where(is_early, pos, place[j])
            place[j] = pos
            used = flag[j] > 0
            row = jnp.where((lane == pos) & used, j, row)
            at = at + (is_early & fits).astype(I32)
            behind = behind + (is_early & jnp.logical_not(fits)).astype(I32)
            return at, behind, row

        def assign(i, c):
            slot[i] = jnp.where(away(i) == g, g * tiles + place[tile[i]], slot[i])
            return c

        lax.fori_loop(0, tiles, clear, 0)
        lax.fori_loop(0, blocks, mark, 0)
        for b in range(levels):
            for f in range(width):
                i = face_ids[f, b]
                j = tile[i]
                flag[j] = jnp.where(away(i) == g, 2, flag[j])
        behind = lax.fori_loop(0, tiles, late, early_slots)
        _, _, row = lax.fori_loop(
            0, tiles, early, (0, behind, jnp.zeros(rows.shape[1:], I32))
        )
        lax.fori_loop(0, blocks, assign, 0)
        rows[g - 1] = row.astype(F32).astype(BF16)


def first_kernel(groups, ids, layer, tile, face_ids, tiles, warmth, kind, amps, diag, *refs):
    packed, state_out, field_out, scale, warmth_v, kind_v, slot, rows = refs[:8]
    tiles_v, field, flag, place, sems, later_sems = refs[8:]
    blocks = packed.shape[0]
    step = blocks // sems.shape[0]
    copies = []
    later = [
        pltpu.make_async_copy(warmth, warmth_v, later_sems.at[0]),
        pltpu.make_async_copy(kind, kind_v, later_sems.at[1]),
    ]
    for p in range(0, blocks, step):
        part = pl.ds(p, step)
        copies.append(
            pltpu.make_async_copy(tiles.at[part], tiles_v.at[part], sems.at[p // step])
        )
    for c in copies + later:
        c.start()
    route(groups, layer, tile, face_ids, slot, rows, flag, place)
    turned = (relax_factor / diag[...]).T
    for i in range(blocks):
        s = column(turned, i, scale.shape[2])
        scale[i] = s
        field[i] = (s * amps[i].astype(F32)).astype(BF16)
    for i in range(blocks):
        if i % step == 0:
            copies[i // step].wait()
        row = joined(tiles_v, i)
        packed[i] = row
        image = jnp.dot(row, picked(field, ids, i), preferred_element_type=F32)
        a = amps[i].astype(F32)
        s = scale[i]
        x = s * a - relax_factor * field[i].astype(F32) + s * (a - image)
        state_out[i] = x
        field_out[i] = x.astype(BF16)
    for c in later:
        c.wait()


def near_kernel(ids, packed, field, state, amps, scale, state_out, field_out, *for_heat):
    for i in range(packed.shape[0]):
        image = jnp.dot(packed[i], picked(field, ids, i), preferred_element_type=F32)
        x = state[i] - relax_factor * field[i].astype(F32)
        x = x + scale[i] * (amps[i].astype(F32) - image)
        state_out[i] = x
        field_out[i] = x.astype(BF16)
    if for_heat:
        heat, diag = for_heat
        heat[...] = jnp.zeros(heat.shape, F32)
        for i in range(packed.shape[0]):
            diag[i] = relax_factor / scale[i]


def face_terms(levels, face_ids, admittance, incoming, terms):
    width, points = face_ids.shape[0], terms.shape[1]
    for b in range(levels):
        for f in range(width):
            block = incoming[b][f * points : (f + 1) * points]
            terms[b * width + f] = jnp.dot(
                admittance[b * width + f], block, preferred_element_type=F32
            )


def in_level_order(refs, order):
    return [refs[order.index(b)] for b in range(len(order))]


def update_faces(face_ids, admittance, scale, incoming, state, field, faces, terms):
    levels, width, points = len(faces), face_ids.shape[0], terms.shape[1]
    face_terms(levels, face_ids, admittance, incoming, terms)
    for b in range(levels):
        for f in range(width):
            i = face_ids[f, b]
            state[i] = state[i] - scale[i] * terms[b * width + f]
    for b in range(levels):
        for f in range(width):
            i = face_ids[f, b]
            x = state[i].astype(BF16)
            field[i] = x
            faces[b][f * points : (f + 1) * points] = x


def face_kernel(order, token, face_ids, admittance, scale, *refs):
    levels = len(order)
    incoming = in_level_order(refs[:levels], order)
    state, field = refs[levels + 2 : levels + 4]
    faces, terms = refs[levels + 4 : 2 * levels + 4], refs[-1]
    update_faces(face_ids, admittance, scale, incoming, state, field, faces, terms)


def heat_kernel(
    order, spots, token, slot, ids, face_ids, admittance, scale, packed, diag, rows, *refs
):
    levels = len(order)
    incoming = in_level_order(refs[:levels], order)
    state, field, heat, soon = refs[levels + 3 : levels + 7]
    faces, terms = refs[levels + 7 : 2 * levels + 7], refs[-1]
    groups, points = soon.shape[0] + 1, heat.shape[1]
    tiles = heat.shape[0] // groups
    update_faces(face_ids, admittance, scale, incoming, state, field, faces, terms)
    for i in range(packed.shape[0]):
        image = jnp.dot(packed[i], picked(field, ids, i), preferred_element_type=F32)
        v = field[i].astype(F32)
        s = slot[i]
        heat[s] = heat[s] + v * (diag[i] * v + image)
    for g in range(1, groups):
        blocks = [heat[g * tiles + p].astype(BF16) for p in range(spots)]
        for p, block in enumerate(blocks):
            soon[g - 1, p * points : (p + 1) * points] = block
        soon[g - 1, len(blocks) * points :] = rows[g - 1]


def heat_face_kernel(order, slot, face_ids, admittance, *refs):
    levels = len(order)
    incoming = in_level_order(refs[:levels], order)
    heat, field, late, terms = refs[levels + 2 :]
    groups, spots = late.shape[0] + 1, late.shape[1]
    tiles = heat.shape[0] // groups
    width = face_ids.shape[0]
    face_terms(levels, face_ids, admittance, incoming, terms)
    for b in range(levels):
        for f in range(width):
            i = face_ids[f, b]
            s = slot[i]
            heat[s] = heat[s] + field[i].astype(F32) * terms[b * width + f]
    for g in range(1, groups):
        late[g - 1] = heat[(g + 1) * tiles - spots : (g + 1) * tiles].astype(BF16)


def kappa_columns(kappas, kind):
    kinds = kind[...]
    kappa = jnp.zeros(kinds.shape, F32)
    for m in range(kappas.shape[0]):
        kappa = jnp.where(kinds == m, kappas[m], kappa)
    return kappa.T


def block_flux(kappa, warmth):
    w = warmth.astype(F32)
    return (kappa * (1.0 + 0.4 * jnp.tanh(w)) * w).astype(BF16)


def edge_kernel(token, kappas, kind, warmth, *edges):
    turned = kappa_columns(kappas, kind)
    tiles, points, width = warmth.shape
    sends_top = lax.axis_index("therm") == 0
    for z in range(ZB):
        top = tiles - ZB + z
        low = block_flux(column(turned, z, width), warmth[z])
        high = block_flux(column(turned, top, width), warmth[top])
        if len(edges) == 1:
            both = jnp.where(sends_top, high.astype(F32), low.astype(F32))
            edges[0][z] = both.astype(BF16)
        else:
            edges[0][z], edges[1][z] = low, high


def conduction_kernel(
    groups,
    ids,
    kappas,
    tiles,
    kind,
    coefficient,
    storage,
    couplings,
    warmth,
    below,
    above,
    heat,
    rest,
    gain,
    flux,
):
    count = tiles.shape[0]
    width = flux.shape[2]
    turned = kappa_columns(kappas, kind)
    for i in range(count):
        flux[i] = block_flux(column(turned, i, width), warmth[i])
    own = lax.axis_index("therm")
    lowest = (own > 0).astype(F32)
    highest = (own < groups - 1).astype(F32)
    diag = coefficient[...].T
    gains = (time_increment / storage[...]).T
    for i in range(count):
        image = jnp.dot(joined(tiles, i), picked(flux, ids, i), preferred_element_type=F32)
        image = image + column(diag, i, width) * flux[i].astype(F32)
        if i < ZB:
            term = jnp.dot(couplings[i], below[i], preferred_element_type=F32)
            image = image + lowest * term
        if i >= count - ZB:
            z = i - (count - ZB)
            term = jnp.dot(couplings[ZB + z], above[z], preferred_element_type=F32)
            image = image + highest * term
        g = column(gains, i, width)
        gain[i] = g
        rest[i] = warmth[i].astype(F32) - g * image


def early_kernel(shifts, heat, gain, *refs):
    maps, soon = refs[:shifts], refs[shifts : 2 * shifts]
    rest, field, out = refs[2 * shifts + 2 : 2 * shifts + 5]
    spots, sem = refs[2 * shifts + 5 : -1], refs[-1]
    tiles, points = rest.shape[:2]
    sent = tiles - spots[0].shape[0]
    for i in range(tiles):
        rest[i] = rest[i] + gain[i] * heat[i]
    for g in range(shifts):
        for p in range(sent):
            j = maps[g][p]
            rest[j] = rest[j] + gain[j] * soon[g][p * points : (p + 1) * points].astype(F32)
    whole = pltpu.make_async_copy(rest, out, sem)
    whole.start()
    for g in range(shifts):
        for p in range(spots[g].shape[0]):
            spots[g][p] = maps[g][tiles - spots[g].shape[0] + p]
    whole.wait()


def late_kernel(shifts, gain, *refs):
    maps, late = refs[:shifts], refs[shifts : 2 * shifts]
    rest, out, sems = refs[2 * shifts], refs[2 * shifts + 2], refs[2 * shifts + 3]
    spots = late[0].shape[0]
    for g in range(shifts):
        for p in range(spots):
            j = maps[g][p]
            rest[j] = rest[j] + gain[j] * late[g][p].astype(F32)
    copies = []
    for g in range(shifts):
        for p in range(spots):
            j = maps[g][p]
            copies.append(pltpu.make_async_copy(rest.at[j], out.at[j], sems.at[g * spots + p]))
    for c in copies:
        c.start()
    for c in copies:
        c.wait()


def body(
    injected_amperage,
    voltage_self_admittance,
    voltage_coupling_tiles,
    voltage_partner_tile_ids,
    interface_tiles_per_level,
    interface_admittance,
    warmth_receiver_layer,
    warmth_receiver_tile,
    warmth_values,
    warmth_self_coefficient,
    warmth_coupling_tiles,
    warmth_partner_tile_ids,
    layer_boundary_couplings,
    substance_kind,
    reference_material_kappas,
    warmth_storage_per_point,
):
    blocks, points, regimes = injected_amperage.shape
    tiles = warmth_values.shape[0]
    levels, width = interface_tiles_per_level.shape
    links = voltage_partner_tile_ids.shape[1]
    groups = lax.axis_size("therm")
    shifts = groups - 1
    whole = (blocks, points, regimes)
    warm = (tiles, points, regimes)
    face = (width * points, regimes)
    late_spots = min(levels * width, tiles)
    early_spots = tiles - late_spots
    sent_rows = early_spots * points
    near_flops = 2 * blocks * links * points * points * regimes
    terms = pltpu.VMEM((levels * width, points, regimes), F32)
    dma = pltpu.SemaphoreType.DMA

    def exchange(faces, order):
        return [from_partner(faces[b], "elec", b) for b in order]

    far_first = list(range(levels))[::-1]
    near, *middle, far = range(levels)
    orders = [far_first, [far] + middle + [near], middle[::-1] + [far, near]]

    amps, diag, face_ids, ids, layer, tile, *faces = call(
        functools.partial(start_kernel, levels),
        [
            (whole, BF16, VM),
            (voltage_self_admittance.shape, F32, VM),
            ((width, levels), I32, SM),
            ((links, blocks), I32, SM),
            ((1, blocks), I32, SM),
            ((blocks,), I32, SM),
        ]
        + [(face, BF16, VM)] * levels,
        on(
            HB,
            injected_amperage,
            voltage_self_admittance,
            interface_tiles_per_level.T,
            voltage_partner_tile_ids.T,
            warmth_receiver_layer.T,
            warmth_receiver_tile,
        ),
        "start",
        scratch=[dma((6,))],
    )
    order = far_first
    incoming = exchange(faces, order)

    packed, state, field, scale, warmth, kind, slot, rows = call(
        functools.partial(first_kernel, groups),
        [
            ((blocks, points, links * points), BF16, VM),
            (whole, F32, VM),
            (whole, BF16, VM),
            (whole, F32, VM),
            (warm, BF16, VM),
            (substance_kind.shape, I32, VM),
            ((blocks,), I32, SM),
            ((shifts, 16, regimes), BF16, VM),
        ],
        on(SM, ids, layer, tile, face_ids)
        + on(HB, voltage_coupling_tiles, warmth_values, substance_kind)
        + on(VM, amps, diag),
        "first",
        scratch=[
            pltpu.VMEM(voltage_coupling_tiles.shape, BF16),
            pltpu.VMEM(whole, BF16),
            pltpu.SMEM((tiles,), I32),
            pltpu.SMEM((tiles,), I32),
            dma((4,)),
            dma((2,)),
        ],
        flops=near_flops,
        limit=8 << 20,
    )
    for sweep_index in range(SWEEPS - 1):
        if sweep_index:
            last = sweep_index == SWEEPS - 2
            state, field, *for_heat = call(
                near_kernel,
                [(whole, F32, VM), (whole, BF16, VM)]
                + [((groups * tiles, points, regimes), F32, VM), (whole, F32, VM)] * last,
                on(SM, ids) + on(VM, packed, field, state, amps, scale),
                "near",
                flops=near_flops,
            )
        token = scale
        if sweep_index == 1:
            edges = call(
                edge_kernel,
                [((ZB, points, regimes), BF16, VM)] * min(2, shifts),
                on(ANY, field) + on(SM, reference_material_kappas) + on(VM, kind, warmth),
                "edge",
            )
            token = edges[0]
        if sweep_index < SWEEPS - 2:
            state, field, *faces = call(
                functools.partial(face_kernel, order),
                [(whole, F32, VM), (whole, BF16, VM)] + [(face, BF16, VM)] * levels,
                on(ANY, token)
                + on(SM, face_ids)
                + on(VM, interface_admittance, scale, *incoming, state, field),
                "face",
                aliases={levels + 4: 0, levels + 5: 1},
                scratch=[terms],
            )
            order = orders[sweep_index]
            incoming = exchange(faces, order)

    if groups == 2:
        below = above = lax.ppermute(edges[0], "therm", [(0, 1), (1, 0)])
    else:
        up = [(i, i + 1) for i in range(groups - 1)]
        above = lax.ppermute(edges[0], "therm", [(j, i) for i, j in up])
        below = lax.ppermute(edges[1], "therm", up)
    heat, diag = for_heat
    _, field, heat, soon, *faces = call(
        functools.partial(heat_kernel, order, early_spots),
        [
            (whole, F32, VM),
            (whole, BF16, VM),
            (heat.shape, F32, VM),
            ((shifts, sent_rows + rows.shape[1], regimes), BF16, VM),
        ]
        + [(face, BF16, VM)] * levels,
        on(ANY, above)
        + on(SM, slot, ids, face_ids)
        + on(VM, interface_admittance, scale, packed, diag, rows, *incoming)
        + on(VM, state, field, heat),
        "heat",
        aliases={9 + levels + n: n for n in range(3)},
        scratch=[terms],
        flops=near_flops,
    )
    routes = [[(i, (i + s) % groups) for i in range(groups)] for s in range(1, groups)]
    soon = [lax.ppermute(soon[s], "therm", routes[s]) for s in range(shifts)]
    maps = [x[sent_rows, :tiles].astype(I32) for x in soon]
    order = far_first
    incoming = exchange(faces, order)

    rest, gain = call(
        functools.partial(conduction_kernel, groups),
        [(warm, F32, VM), (warm, F32, VM)],
        on(SM, warmth_partner_tile_ids.T, reference_material_kappas)
        + on(
            VM,
            warmth_coupling_tiles,
            kind,
            warmth_self_coefficient,
            warmth_storage_per_point,
            layer_boundary_couplings,
            warmth,
            below,
            above,
        )
        + on(ANY, heat),
        "conduction",
        scratch=[pltpu.VMEM(warm, BF16)],
        flops=near_flops,
    )
    heat, field, late = call(
        functools.partial(heat_face_kernel, order),
        [
            ((groups * tiles, points, regimes), F32, VM),
            (whole, BF16, VM),
            ((shifts, late_spots, points, regimes), BF16, VM),
        ],
        on(SM, slot, face_ids) + on(VM, interface_admittance, *incoming, heat, field),
        "heat_face",
        aliases={levels + 3: 0, levels + 4: 1},
        scratch=[terms],
    )
    late = [lax.ppermute(late[s], "therm", routes[s]) for s in range(shifts)]
    rest, voltage_solution, out, *maps = call(
        functools.partial(early_kernel, shifts),
        [(warm, F32, VM), (whole, BF16, VM), (warm, F32, HB)] + [((late_spots,), I32, SM)] * shifts,
        on(VM, heat, gain) + on(SM, *maps) + on(VM, *soon, rest, field),
        "early",
        aliases={2 + 2 * shifts: 0, 3 + 2 * shifts: 1},
        scratch=[dma],
    )
    (advanced_warmth_values,) = call(
        functools.partial(late_kernel, shifts),
        [(warm, F32, HB)],
        on(VM, gain) + on(SM, *maps) + on(VM, *late, rest) + on(HB, out),
        "late",
        aliases={2 + 2 * shifts: 0},
        scratch=[dma((shifts * late_spots,))],
    )
    return (voltage_solution, advanced_warmth_values)


def solution(mesh):
    split = P(("elec", "therm"))
    return jax.shard_map(
        body,
        mesh=mesh,
        in_specs=(split,) * 14 + (P(), split),
        out_specs=(split, split),
        check_vma=False,
    )
```

```python
import functools

import jax
import jax.numpy as jnp
from jax import lax
from jax.experimental import pallas as pl
from jax.experimental.pallas import tpu as pltpu
from jax.sharding import PartitionSpec as P

SWEEPS = 5
ZB = 2

relax_factor = 0.8
time_increment = 0.5

F32 = jnp.float32
BF16 = jnp.bfloat16
I32 = jnp.int32
VM = pl.BlockSpec(memory_space=pltpu.VMEM)
SM = pl.BlockSpec(memory_space=pltpu.SMEM)
HB = pl.BlockSpec(memory_space=pltpu.HBM)
ANY = pl.BlockSpec(memory_space=pl.ANY)
SPACES = {id(VM): pltpu.VMEM, id(HB): pltpu.HBM, id(SM): pltpu.SMEM}
LIMIT = 4 << 20


def call(kernel, outs, ins, name, aliases={}, scratch=(), flops=0, limit=LIMIT):
    args = []
    for x, spec in ins:
        if spec is VM or spec is HB:
            x = pltpu.with_memory_space_constraint(x, SPACES[id(spec)])
        args.append(x)
    return pl.pallas_call(
        kernel,
        out_shape=[SPACES[id(spec)](shape, dtype) for shape, dtype, spec in outs],
        in_specs=[spec for _, spec in ins],
        out_specs=[spec for _, _, spec in outs],
        input_output_aliases=aliases,
        scratch_shapes=scratch,
        compiler_params=pltpu.CompilerParams(vmem_limit_bytes=limit),
        cost_estimate=pl.CostEstimate(flops=flops, bytes_accessed=0, transcendentals=0),
        name=name,
    )(*args)


def on(spec, *arrays):
    return [(x, spec) for x in arrays]


def from_partner(block, axis, bit):
    count = lax.axis_size(axis)
    route = []
    for low in range(count):
        high = low | 1 << bit
        if high != low and high < count:
            route += [(low, high), (high, low)]
    return lax.ppermute(block, axis, route)


def column(table, row, width):
    return jnp.broadcast_to(table[:, row : row + 1], (table.shape[0], width))


def joined(tiles_ref, row):
    return jnp.concatenate([tiles_ref[row, k] for k in range(tiles_ref.shape[1])], axis=1)


def picked(field_ref, ids_ref, row):
    return jnp.concatenate([field_ref[ids_ref[k, row]] for k in range(ids_ref.shape[0])], axis=0)


def start_kernel(levels, amps, diag, face_ids, *refs):
    small = refs[:3]
    amps_v, diag_v, face_ids_s = refs[3:6]
    small_s, faces, sems = refs[6:9], refs[9 : 9 + levels], refs[-1]
    pairs = [(face_ids, face_ids_s), (diag, diag_v), (amps, amps_v)]
    copies = [
        pltpu.make_async_copy(a, b, sems.at[n])
        for n, (a, b) in enumerate(pairs + list(zip(small, small_s)))
    ]
    for c in copies:
        c.start()
    copies[0].wait()
    copies[1].wait()
    scale = relax_factor / diag_v[...]
    rows = lax.broadcasted_iota(I32, scale.shape, 0)
    chosen = []
    for b in range(levels):
        for f in range(face_ids.shape[0]):
            mine = jnp.where(rows == face_ids_s[f, b], scale, 0.0)
            chosen.append(jnp.sum(mine, axis=0, keepdims=True))
    turned = jnp.concatenate(chosen, axis=0).T
    copies[2].wait()
    for b in range(levels):
        for f in range(face_ids.shape[0]):
            s = column(turned, b * face_ids.shape[0] + f, amps.shape[2])
            points = amps.shape[1]
            block = s * amps_v[face_ids_s[f, b]].astype(F32)
            faces[b][f * points : (f + 1) * points] = block.astype(BF16)
    for c in copies[3:]:
        c.wait()


def route(groups, layer, tile, face_ids, slot, rows, flag, place):
    own = lax.axis_index("therm")
    blocks, tiles = slot.shape[0], flag.shape[0]
    levels, width = face_ids.shape[1], face_ids.shape[0]
    early_slots = max(tiles - levels * width, 0)
    lane = lax.broadcasted_iota(I32, rows.shape[1:], 1)

    def away(i):
        a = layer[0, i] - own
        return jnp.where(a < 0, a + groups, a)

    def home(i, c):
        slot[i] = tile[i]
        return c

    lax.fori_loop(0, blocks, home, 0)
    for g in range(1, groups):

        def clear(j, c):
            flag[j] = 0
            return c

        def mark(i, c):
            j = tile[i]
            flag[j] = jnp.where(away(i) == g, 1, flag[j])
            return c

        def late(j, c):
            is_late = flag[j] == 2
            place[j] = jnp.where(is_late, c, 0)
            return c + is_late.astype(I32)

        def early(j, c):
            at, behind, row = c
            is_early = flag[j] == 1
            fits = at < early_slots
            pos = jnp.where(fits, at, behind)
            pos = jnp.where(is_early, pos, place[j])
            place[j] = pos
            used = flag[j] > 0
            row = jnp.where((lane == pos) & used, j, row)
            at = at + (is_early & fits).astype(I32)
            behind = behind + (is_early & jnp.logical_not(fits)).astype(I32)
            return at, behind, row

        def spare(j, c):
            at, behind, row = c
            free = flag[j] == 0
            fits = at < early_slots
            row = jnp.where((lane == jnp.where(fits, at, behind)) & free, j, row)
            at = at + (free & fits).astype(I32)
            behind = behind + (free & jnp.logical_not(fits)).astype(I32)
            return at, behind, row

        def assign(i, c):
            slot[i] = jnp.where(away(i) == g, g * tiles + place[tile[i]], slot[i])
            return c

        lax.fori_loop(0, tiles, clear, 0)
        lax.fori_loop(0, blocks, mark, 0)
        for b in range(levels):
            for f in range(width):
                i = face_ids[f, b]
                j = tile[i]
                flag[j] = jnp.where(away(i) == g, 2, flag[j])
        behind = lax.fori_loop(0, tiles, late, early_slots)
        filled = lax.fori_loop(0, tiles, early, (0, behind, jnp.zeros(rows.shape[1:], I32)))
        _, _, row = lax.fori_loop(0, tiles, spare, filled)
        lax.fori_loop(0, blocks, assign, 0)
        rows[g - 1] = row.astype(F32).astype(BF16)


def first_kernel(groups, ids, layer, tile, face_ids, tiles, warmth, kind, amps, diag, *refs):
    packed, state_out, field_out, scale, warmth_v, kind_v, slot, rows = refs[:8]
    tiles_v, field, flag, place, sems, later_sems = refs[8:]
    blocks = packed.shape[0]
    step = blocks // sems.shape[0]
    copies = []
    later = [
        pltpu.make_async_copy(warmth, warmth_v, later_sems.at[0]),
        pltpu.make_async_copy(kind, kind_v, later_sems.at[1]),
    ]
    for p in range(0, blocks, step):
        part = pl.ds(p, step)
        copies.append(
            pltpu.make_async_copy(tiles.at[part], tiles_v.at[part], sems.at[p // step])
        )
    for c in copies + later:
        c.start()
    route(groups, layer, tile, face_ids, slot, rows, flag, place)
    turned = (relax_factor / diag[...]).T
    for i in range(blocks):
        s = column(turned, i, scale.shape[2])
        scale[i] = s
        field[i] = (s * amps[i].astype(F32)).astype(BF16)
    for i in range(blocks):
        if i % step == 0:
            copies[i // step].wait()
        row = joined(tiles_v, i)
        packed[i] = row
        image = jnp.dot(row, picked(field, ids, i), preferred_element_type=F32)
        a = amps[i].astype(F32)
        s = scale[i]
        x = s * a - relax_factor * field[i].astype(F32) + s * (a - image)
        state_out[i] = x
        field_out[i] = x.astype(BF16)
    for c in later:
        c.wait()


def near_kernel(ids, packed, field, state, amps, scale, state_out, field_out, *for_heat):
    for i in range(packed.shape[0]):
        image = jnp.dot(packed[i], picked(field, ids, i), preferred_element_type=F32)
        x = state[i] - relax_factor * field[i].astype(F32)
        x = x + scale[i] * (amps[i].astype(F32) - image)
        state_out[i] = x
        field_out[i] = x.astype(BF16)
    if for_heat:
        heat, diag = for_heat
        heat[...] = jnp.zeros(heat.shape, F32)
        for i in range(packed.shape[0]):
            diag[i] = relax_factor / scale[i]


def face_terms(levels, face_ids, admittance, incoming, terms):
    width, points = face_ids.shape[0], terms.shape[1]
    for b in range(levels):
        for f in range(width):
            block = incoming[b][f * points : (f + 1) * points]
            terms[b * width + f] = jnp.dot(
                admittance[b * width + f], block, preferred_element_type=F32
            )


def in_level_order(refs, order):
    return [refs[order.index(b)] for b in range(len(order))]


def update_faces(face_ids, admittance, scale, incoming, state, field, faces, terms):
    levels, width, points = len(faces), face_ids.shape[0], terms.shape[1]
    face_terms(levels, face_ids, admittance, incoming, terms)
    for b in range(levels):
        for f in range(width):
            i = face_ids[f, b]
            state[i] = state[i] - scale[i] * terms[b * width + f]
    for b in range(levels):
        for f in range(width):
            i = face_ids[f, b]
            x = state[i].astype(BF16)
            field[i] = x
            faces[b][f * points : (f + 1) * points] = x


def face_kernel(order, token, face_ids, admittance, scale, *refs):
    levels = len(order)
    incoming = in_level_order(refs[:levels], order)
    state, field = refs[levels + 2 : levels + 4]
    faces, terms = refs[levels + 4 : 2 * levels + 4], refs[-1]
    update_faces(face_ids, admittance, scale, incoming, state, field, faces, terms)


def heat_kernel(
    order, spots, token, slot, ids, face_ids, admittance, scale, packed, diag, rows, *refs
):
    levels = len(order)
    incoming = in_level_order(refs[:levels], order)
    state, field, heat, soon = refs[levels + 3 : levels + 7]
    faces, terms = refs[levels + 7 : 2 * levels + 7], refs[-1]
    groups, points = soon.shape[0] + 1, heat.shape[1]
    tiles = heat.shape[0] // groups
    update_faces(face_ids, admittance, scale, incoming, state, field, faces, terms)
    for i in range(packed.shape[0]):
        image = jnp.dot(packed[i], picked(field, ids, i), preferred_element_type=F32)
        v = field[i].astype(F32)
        s = slot[i]
        heat[s] = heat[s] + v * (diag[i] * v + image)
    for g in range(1, groups):
        blocks = [heat[g * tiles + p].astype(BF16) for p in range(spots)]
        for p, block in enumerate(blocks):
            soon[g - 1, p * points : (p + 1) * points] = block
        soon[g - 1, len(blocks) * points :] = rows[g - 1]


def heat_face_kernel(order, slot, face_ids, admittance, *refs):
    levels = len(order)
    incoming = in_level_order(refs[:levels], order)
    heat, field, late, terms = refs[levels + 2 :]
    groups, spots = late.shape[0] + 1, late.shape[1]
    tiles = heat.shape[0] // groups
    width = face_ids.shape[0]
    face_terms(levels, face_ids, admittance, incoming, terms)
    for b in range(levels):
        for f in range(width):
            i = face_ids[f, b]
            s = slot[i]
            heat[s] = heat[s] + field[i].astype(F32) * terms[b * width + f]
    for g in range(1, groups):
        late[g - 1] = heat[(g + 1) * tiles - spots : (g + 1) * tiles].astype(BF16)


def kappa_columns(kappas, kind):
    kinds = kind[...]
    kappa = jnp.zeros(kinds.shape, F32)
    for m in range(kappas.shape[0]):
        kappa = jnp.where(kinds == m, kappas[m], kappa)
    return kappa.T


def block_flux(kappa, warmth):
    w = warmth.astype(F32)
    return (kappa * (1.0 + 0.4 * jnp.tanh(w)) * w).astype(BF16)


def flux_kernel(token, kappas, kind, warmth, flux, *edges):
    turned = kappa_columns(kappas, kind)
    tiles, points, width = warmth.shape
    for i in range(tiles):
        flux[i] = block_flux(column(turned, i, width), warmth[i])
    sends_top = lax.axis_index("therm") == 0
    for z in range(ZB):
        top = tiles - ZB + z
        if len(edges) == 1:
            edges[0][z] = flux[jnp.where(sends_top, top, z)]
        else:
            edges[0][z], edges[1][z] = flux[z], flux[top]


def conduction_kernel(
    groups,
    ids,
    tiles,
    coefficient,
    storage,
    couplings,
    warmth,
    flux,
    below,
    above,
    heat,
    rest,
    gain,
):
    count = tiles.shape[0]
    width = flux.shape[2]
    own = lax.axis_index("therm")
    lowest = (own > 0).astype(F32)
    highest = (own < groups - 1).astype(F32)
    diag = coefficient[...].T
    gains = (time_increment / storage[...]).T
    for i in range(count):
        image = jnp.dot(joined(tiles, i), picked(flux, ids, i), preferred_element_type=F32)
        image = image + column(diag, i, width) * flux[i].astype(F32)
        if i < ZB:
            term = jnp.dot(couplings[i], below[i], preferred_element_type=F32)
            image = image + lowest * term
        if i >= count - ZB:
            z = i - (count - ZB)
            term = jnp.dot(couplings[ZB + z], above[z], preferred_element_type=F32)
            image = image + highest * term
        g = column(gains, i, width)
        gain[i] = g
        rest[i] = warmth[i].astype(F32) - g * image


def early_kernel(shifts, heat, gain, *refs):
    maps, soon = refs[:shifts], refs[shifts : 2 * shifts]
    rest, field, out = refs[2 * shifts + 2 : 2 * shifts + 5]
    spots, sem = refs[2 * shifts + 5 : -1], refs[-1]
    tiles, points = rest.shape[:2]
    sent = tiles - spots[0].shape[0]
    for i in range(tiles):
        rest[i] = rest[i] + gain[i] * heat[i]
    for g in range(shifts):
        for p in range(sent):
            j = maps[g][p]
            rest[j] = rest[j] + gain[j] * soon[g][p * points : (p + 1) * points].astype(F32)
    whole = pltpu.make_async_copy(rest, out, sem)
    whole.start()
    for g in range(shifts):
        for p in range(spots[g].shape[0]):
            spots[g][p] = maps[g][tiles - spots[g].shape[0] + p]
    whole.wait()


def late_kernel(shifts, gain, *refs):
    maps, late = refs[:shifts], refs[shifts : 2 * shifts]
    rest, out = refs[2 * shifts], refs[2 * shifts + 2]
    ready, sems = refs[2 * shifts + 3 :]
    spots = late[0].shape[0]
    copies = []
    if shifts == 1:
        for p in range(spots):
            j = maps[0][p]
            ready[p] = rest[j] + gain[j] * late[0][p].astype(F32)
            copies.append(pltpu.make_async_copy(ready.at[p], out.at[j], sems.at[p]))
            copies[-1].start()
    else:
        for g in range(shifts):
            for p in range(spots):
                j = maps[g][p]
                rest[j] = rest[j] + gain[j] * late[g][p].astype(F32)
        for g in range(shifts):
            for p in range(spots):
                j = maps[g][p]
                copy = pltpu.make_async_copy(rest.at[j], out.at[j], sems.at[g * spots + p])
                copy.start()
                copies.append(copy)
    for c in copies:
        c.wait()


def body(
    injected_amperage,
    voltage_self_admittance,
    voltage_coupling_tiles,
    voltage_partner_tile_ids,
    interface_tiles_per_level,
    interface_admittance,
    warmth_receiver_layer,
    warmth_receiver_tile,
    warmth_values,
    warmth_self_coefficient,
    warmth_coupling_tiles,
    warmth_partner_tile_ids,
    layer_boundary_couplings,
    substance_kind,
    reference_material_kappas,
    warmth_storage_per_point,
):
    blocks, points, regimes = injected_amperage.shape
    tiles = warmth_values.shape[0]
    levels, width = interface_tiles_per_level.shape
    links = voltage_partner_tile_ids.shape[1]
    groups = lax.axis_size("therm")
    shifts = groups - 1
    whole = (blocks, points, regimes)
    warm = (tiles, points, regimes)
    face = (width * points, regimes)
    late_spots = min(levels * width, tiles)
    early_spots = tiles - late_spots
    sent_rows = early_spots * points
    near_flops = 2 * blocks * links * points * points * regimes
    terms = pltpu.VMEM((levels * width, points, regimes), F32)
    dma = pltpu.SemaphoreType.DMA

    def exchange(faces, order):
        return [from_partner(faces[b], "elec", b) for b in order]

    far_first = list(range(levels))[::-1]
    near, *middle, far = range(levels)
    orders = [far_first, [far] + middle + [near], middle[::-1] + [far, near]]

    amps, diag, face_ids, ids, layer, tile, *faces = call(
        functools.partial(start_kernel, levels),
        [
            (whole, BF16, VM),
            (voltage_self_admittance.shape, F32, VM),
            ((width, levels), I32, SM),
            ((links, blocks), I32, SM),
            ((1, blocks), I32, SM),
            ((blocks,), I32, SM),
        ]
        + [(face, BF16, VM)] * levels,
        on(
            HB,
            injected_amperage,
            voltage_self_admittance,
            interface_tiles_per_level.T,
            voltage_partner_tile_ids.T,
            warmth_receiver_layer.T,
            warmth_receiver_tile,
        ),
        "start",
        scratch=[dma((6,))],
    )
    order = far_first
    incoming = exchange(faces, order)

    packed, state, field, scale, warmth, kind, slot, rows = call(
        functools.partial(first_kernel, groups),
        [
            ((blocks, points, links * points), BF16, VM),
            (whole, F32, VM),
            (whole, BF16, VM),
            (whole, F32, VM),
            (warm, BF16, VM),
            (substance_kind.shape, I32, VM),
            ((blocks,), I32, SM),
            ((shifts, 16, regimes), BF16, VM),
        ],
        on(SM, ids, layer, tile, face_ids)
        + on(HB, voltage_coupling_tiles, warmth_values, substance_kind)
        + on(VM, amps, diag),
        "first",
        scratch=[
            pltpu.VMEM(voltage_coupling_tiles.shape, BF16),
            pltpu.VMEM(whole, BF16),
            pltpu.SMEM((tiles,), I32),
            pltpu.SMEM((tiles,), I32),
            dma((4,)),
            dma((2,)),
        ],
        flops=near_flops,
        limit=8 << 20,
    )
    for sweep_index in range(SWEEPS - 1):
        if sweep_index:
            last = sweep_index == SWEEPS - 2
            state, field, *for_heat = call(
                near_kernel,
                [(whole, F32, VM), (whole, BF16, VM)]
                + [((groups * tiles, points, regimes), F32, VM), (whole, F32, VM)] * last,
                on(SM, ids) + on(VM, packed, field, state, amps, scale),
                "near",
                flops=near_flops,
            )
        token = scale
        if sweep_index == 1:
            flux, *edges = call(
                flux_kernel,
                [(warm, BF16, VM)] + [((ZB, points, regimes), BF16, VM)] * min(2, shifts),
                on(ANY, field) + on(SM, reference_material_kappas) + on(VM, kind, warmth),
                "flux",
            )
            token = edges[0]
        if sweep_index < SWEEPS - 2:
            state, field, *faces = call(
                functools.partial(face_kernel, order),
                [(whole, F32, VM), (whole, BF16, VM)] + [(face, BF16, VM)] * levels,
                on(ANY, token)
                + on(SM, face_ids)
                + on(VM, interface_admittance, scale, *incoming, state, field),
                "face",
                aliases={levels + 4: 0, levels + 5: 1},
                scratch=[terms],
            )
            order = orders[sweep_index]
            incoming = exchange(faces, order)

    if groups == 2:
        below = above = lax.ppermute(edges[0], "therm", [(0, 1), (1, 0)])
    else:
        up = [(i, i + 1) for i in range(groups - 1)]
        above = lax.ppermute(edges[0], "therm", [(j, i) for i, j in up])
        below = lax.ppermute(edges[1], "therm", up)
    heat, diag = for_heat
    _, field, heat, soon, *faces = call(
        functools.partial(heat_kernel, order, early_spots),
        [
            (whole, F32, VM),
            (whole, BF16, VM),
            (heat.shape, F32, VM),
            ((shifts, sent_rows + rows.shape[1], regimes), BF16, VM),
        ]
        + [(face, BF16, VM)] * levels,
        on(ANY, above)
        + on(SM, slot, ids, face_ids)
        + on(VM, interface_admittance, scale, packed, diag, rows, *incoming)
        + on(VM, state, field, heat),
        "heat",
        aliases={9 + levels + n: n for n in range(3)},
        scratch=[terms],
        flops=near_flops,
    )
    routes = [[(i, (i + s) % groups) for i in range(groups)] for s in range(1, groups)]
    soon = [lax.ppermute(soon[s], "therm", routes[s]) for s in range(shifts)]
    maps = [x[sent_rows, :tiles].astype(I32) for x in soon]
    order = far_first
    incoming = exchange(faces, order)

    rest, gain = call(
        functools.partial(conduction_kernel, groups),
        [(warm, F32, VM), (warm, F32, VM)],
        on(SM, warmth_partner_tile_ids.T)
        + on(
            VM,
            warmth_coupling_tiles,
            warmth_self_coefficient,
            warmth_storage_per_point,
            layer_boundary_couplings,
            warmth,
            flux,
            below,
            above,
        )
        + on(ANY, heat),
        "conduction",
        flops=near_flops,
    )
    heat, field, late = call(
        functools.partial(heat_face_kernel, order),
        [
            ((groups * tiles, points, regimes), F32, VM),
            (whole, BF16, VM),
            ((shifts, late_spots, points, regimes), BF16, VM),
        ],
        on(SM, slot, face_ids) + on(VM, interface_admittance, *incoming, heat, field),
        "heat_face",
        aliases={levels + 3: 0, levels + 4: 1},
        scratch=[terms],
    )
    late = [lax.ppermute(late[s], "therm", routes[s]) for s in range(shifts)]
    rest, voltage_solution, out, *maps = call(
        functools.partial(early_kernel, shifts),
        [(warm, F32, VM), (whole, BF16, VM), (warm, F32, HB)] + [((late_spots,), I32, SM)] * shifts,
        on(VM, heat, gain) + on(SM, *maps) + on(VM, *soon, rest, field),
        "early",
        aliases={2 + 2 * shifts: 0, 3 + 2 * shifts: 1},
        scratch=[dma],
    )
    (advanced_warmth_values,) = call(
        functools.partial(late_kernel, shifts),
        [(warm, F32, HB)],
        on(VM, gain) + on(SM, *maps) + on(VM, *late, rest) + on(HB, out),
        "late",
        aliases={2 + 2 * shifts: 0},
        scratch=[
            pltpu.VMEM((late_spots, points, regimes), F32),
            dma((shifts * late_spots,)),
        ],
    )
    return (voltage_solution, advanced_warmth_values)


def solution(mesh):
    split = P(("elec", "therm"))
    return jax.shard_map(
        body,
        mesh=mesh,
        in_specs=(split,) * 14 + (P(), split),
        out_specs=(split, split),
        check_vma=False,
    )
```

```python
import functools

import jax
import jax.numpy as jnp
from jax import lax
from jax.experimental import pallas as pl
from jax.experimental.pallas import tpu as pltpu
from jax.sharding import PartitionSpec as P

SWEEPS = 5
ZB = 2

relax_factor = 0.8
time_increment = 0.5

F32 = jnp.float32
BF16 = jnp.bfloat16
I32 = jnp.int32
VM = pl.BlockSpec(memory_space=pltpu.VMEM)
SM = pl.BlockSpec(memory_space=pltpu.SMEM)
HB = pl.BlockSpec(memory_space=pltpu.HBM)
ANY = pl.BlockSpec(memory_space=pl.ANY)
SPACES = {id(VM): pltpu.VMEM, id(HB): pltpu.HBM, id(SM): pltpu.SMEM}
LIMIT = 4 << 20


def call(kernel, outs, ins, name, aliases={}, scratch=(), flops=0, limit=LIMIT):
    args = []
    for x, spec in ins:
        if spec is VM or spec is HB:
            x = pltpu.with_memory_space_constraint(x, SPACES[id(spec)])
        args.append(x)
    return pl.pallas_call(
        kernel,
        out_shape=[SPACES[id(spec)](shape, dtype) for shape, dtype, spec in outs],
        in_specs=[spec for _, spec in ins],
        out_specs=[spec for _, _, spec in outs],
        input_output_aliases=aliases,
        scratch_shapes=scratch,
        compiler_params=pltpu.CompilerParams(vmem_limit_bytes=limit),
        cost_estimate=pl.CostEstimate(flops=flops, bytes_accessed=0, transcendentals=0),
        name=name,
    )(*args)


def on(spec, *arrays):
    return [(x, spec) for x in arrays]


def from_partner(block, axis, bit):
    count = lax.axis_size(axis)
    route = []
    for low in range(count):
        high = low | 1 << bit
        if high != low and high < count:
            route += [(low, high), (high, low)]
    return lax.ppermute(block, axis, route)


def column(table, row, width):
    return jnp.broadcast_to(table[:, row : row + 1], (table.shape[0], width))


def joined(tiles_ref, row):
    return jnp.concatenate([tiles_ref[row, k] for k in range(tiles_ref.shape[1])], axis=1)


def picked(field_ref, ids_ref, row):
    return jnp.concatenate([field_ref[ids_ref[k, row]] for k in range(ids_ref.shape[0])], axis=0)


def start_kernel(levels, amps, diag, face_ids, *refs):
    small = refs[:3]
    amps_v, diag_v, face_ids_s = refs[3:6]
    small_s, faces, sems = refs[6:9], refs[9 : 9 + levels], refs[-1]
    pairs = [(face_ids, face_ids_s), (diag, diag_v), (amps, amps_v)]
    copies = [
        pltpu.make_async_copy(a, b, sems.at[n])
        for n, (a, b) in enumerate(pairs + list(zip(small, small_s)))
    ]
    for c in copies:
        c.start()
    copies[0].wait()
    copies[1].wait()
    scale = relax_factor / diag_v[...]
    rows = lax.broadcasted_iota(I32, scale.shape, 0)
    chosen = []
    for b in range(levels):
        for f in range(face_ids.shape[0]):
            mine = jnp.where(rows == face_ids_s[f, b], scale, 0.0)
            chosen.append(jnp.sum(mine, axis=0, keepdims=True))
    turned = jnp.concatenate(chosen, axis=0).T
    copies[2].wait()
    for b in range(levels):
        for f in range(face_ids.shape[0]):
            s = column(turned, b * face_ids.shape[0] + f, amps.shape[2])
            points = amps.shape[1]
            block = s * amps_v[face_ids_s[f, b]].astype(F32)
            faces[b][f * points : (f + 1) * points] = block.astype(BF16)
    for c in copies[3:]:
        c.wait()


def route(groups, layer, tile, face_ids, slot, rows, flag, place):
    own = lax.axis_index("therm")
    blocks, tiles = slot.shape[0], flag.shape[0]
    levels, width = face_ids.shape[1], face_ids.shape[0]
    early_slots = max(tiles - levels * width, 0)
    lane = lax.broadcasted_iota(I32, rows.shape[1:], 1)

    def away(i):
        a = layer[0, i] - own
        return jnp.where(a < 0, a + groups, a)

    def home(i, c):
        slot[i] = tile[i]
        return c

    lax.fori_loop(0, blocks, home, 0)
    for g in range(1, groups):

        def clear(j, c):
            flag[j] = 0
            return c

        def mark(i, c):
            j = tile[i]
            flag[j] = jnp.where(away(i) == g, 1, flag[j])
            return c

        def late(j, c):
            is_late = flag[j] == 2
            place[j] = jnp.where(is_late, c, 0)
            return c + is_late.astype(I32)

        def early(j, c):
            at, behind, row = c
            is_early = flag[j] == 1
            fits = at < early_slots
            pos = jnp.where(fits, at, behind)
            pos = jnp.where(is_early, pos, place[j])
            place[j] = pos
            used = flag[j] > 0
            row = jnp.where((lane == pos) & used, j, row)
            at = at + (is_early & fits).astype(I32)
            behind = behind + (is_early & jnp.logical_not(fits)).astype(I32)
            return at, behind, row

        def assign(i, c):
            slot[i] = jnp.where(away(i) == g, g * tiles + place[tile[i]], slot[i])
            return c

        lax.fori_loop(0, tiles, clear, 0)
        lax.fori_loop(0, blocks, mark, 0)
        for b in range(levels):
            for f in range(width):
                i = face_ids[f, b]
                j = tile[i]
                flag[j] = jnp.where(away(i) == g, 2, flag[j])
        behind = lax.fori_loop(0, tiles, late, early_slots)
        _, _, row = lax.fori_loop(
            0, tiles, early, (0, behind, jnp.zeros(rows.shape[1:], I32))
        )
        lax.fori_loop(0, blocks, assign, 0)
        rows[g - 1] = row.astype(F32).astype(BF16)


def first_kernel(groups, ids, layer, tile, face_ids, tiles, warmth, kind, amps, diag, *refs):
    packed, state_out, field_out, scale, warmth_v, kind_v, slot, rows = refs[:8]
    tiles_v, field, flag, place, sems, later_sems = refs[8:]
    blocks = packed.shape[0]
    step = blocks // sems.shape[0]
    copies = []
    later = [
        pltpu.make_async_copy(warmth, warmth_v, later_sems.at[0]),
        pltpu.make_async_copy(kind, kind_v, later_sems.at[1]),
    ]
    for p in range(0, blocks, step):
        part = pl.ds(p, step)
        copies.append(
            pltpu.make_async_copy(tiles.at[part], tiles_v.at[part], sems.at[p // step])
        )
    for c in copies + later:
        c.start()
    route(groups, layer, tile, face_ids, slot, rows, flag, place)
    turned = (relax_factor / diag[...]).T
    for i in range(blocks):
        s = column(turned, i, scale.shape[2])
        scale[i] = s
        field[i] = (s * amps[i].astype(F32)).astype(BF16)
    for i in range(blocks):
        if i % step == 0:
            copies[i // step].wait()
        row = joined(tiles_v, i)
        packed[i] = row
        image = jnp.dot(row, picked(field, ids, i), preferred_element_type=F32)
        a = amps[i].astype(F32)
        s = scale[i]
        x = s * a - relax_factor * field[i].astype(F32) + s * (a - image)
        state_out[i] = x
        field_out[i] = x.astype(BF16)
    for c in later:
        c.wait()


def near_kernel(ids, packed, field, state, amps, scale, state_out, field_out, *for_heat):
    for i in range(packed.shape[0]):
        image = jnp.dot(packed[i], picked(field, ids, i), preferred_element_type=F32)
        x = state[i] - relax_factor * field[i].astype(F32)
        x = x + scale[i] * (amps[i].astype(F32) - image)
        state_out[i] = x
        field_out[i] = x.astype(BF16)
    if for_heat:
        heat, diag = for_heat
        heat[...] = jnp.zeros(heat.shape, F32)
        for i in range(packed.shape[0]):
            diag[i] = relax_factor / scale[i]


def face_terms(levels, face_ids, admittance, incoming, terms):
    width, points = face_ids.shape[0], terms.shape[1]
    for b in range(levels):
        for f in range(width):
            block = incoming[b][f * points : (f + 1) * points]
            terms[b * width + f] = jnp.dot(
                admittance[b * width + f], block, preferred_element_type=F32
            )


def in_level_order(refs, order):
    return [refs[order.index(b)] for b in range(len(order))]


def update_faces(face_ids, admittance, scale, incoming, state, field, faces, terms):
    levels, width, points = len(faces), face_ids.shape[0], terms.shape[1]
    face_terms(levels, face_ids, admittance, incoming, terms)
    for b in range(levels):
        for f in range(width):
            i = face_ids[f, b]
            state[i] = state[i] - scale[i] * terms[b * width + f]
    for b in range(levels):
        for f in range(width):
            i = face_ids[f, b]
            x = state[i].astype(BF16)
            field[i] = x
            faces[b][f * points : (f + 1) * points] = x


def face_kernel(order, token, face_ids, admittance, scale, *refs):
    levels = len(order)
    incoming = in_level_order(refs[:levels], order)
    state, field = refs[levels + 2 : levels + 4]
    faces, terms = refs[levels + 4 : 2 * levels + 4], refs[-1]
    update_faces(face_ids, admittance, scale, incoming, state, field, faces, terms)


def heat_kernel(
    order, spots, token, slot, ids, face_ids, admittance, scale, packed, diag, rows, *refs
):
    levels = len(order)
    incoming = in_level_order(refs[:levels], order)
    state, field, heat, soon = refs[levels + 3 : levels + 7]
    faces, terms = refs[levels + 7 : 2 * levels + 7], refs[-1]
    groups, points = soon.shape[0] + 1, heat.shape[1]
    tiles = heat.shape[0] // groups
    update_faces(face_ids, admittance, scale, incoming, state, field, faces, terms)
    for i in range(packed.shape[0]):
        image = jnp.dot(packed[i], picked(field, ids, i), preferred_element_type=F32)
        v = field[i].astype(F32)
        s = slot[i]
        heat[s] = heat[s] + v * (diag[i] * v + image)
    for g in range(1, groups):
        blocks = [heat[g * tiles + p].astype(BF16) for p in range(spots)]
        for p, block in enumerate(blocks):
            soon[g - 1, p * points : (p + 1) * points] = block
        soon[g - 1, len(blocks) * points :] = rows[g - 1]


def heat_face_kernel(order, slot, face_ids, admittance, *refs):
    levels = len(order)
    incoming = in_level_order(refs[:levels], order)
    heat, field, late, terms = refs[levels + 2 :]
    groups, spots = late.shape[0] + 1, late.shape[1]
    tiles = heat.shape[0] // groups
    width = face_ids.shape[0]
    face_terms(levels, face_ids, admittance, incoming, terms)
    for b in range(levels):
        for f in range(width):
            i = face_ids[f, b]
            s = slot[i]
            heat[s] = heat[s] + field[i].astype(F32) * terms[b * width + f]
    for g in range(1, groups):
        late[g - 1] = heat[(g + 1) * tiles - spots : (g + 1) * tiles].astype(BF16)


def kappa_columns(kappas, kind):
    kinds = kind[...]
    kappa = jnp.zeros(kinds.shape, F32)
    for m in range(kappas.shape[0]):
        kappa = jnp.where(kinds == m, kappas[m], kappa)
    return kappa.T


def block_flux(kappa, warmth):
    w = warmth.astype(F32)
    return (kappa * (1.0 + 0.4 * jnp.tanh(w)) * w).astype(BF16)


def flux_kernel(token, kappas, kind, warmth, flux, *edges):
    turned = kappa_columns(kappas, kind)
    tiles, points, width = warmth.shape
    for i in range(tiles):
        flux[i] = block_flux(column(turned, i, width), warmth[i])
    sends_top = lax.axis_index("therm") == 0
    for z in range(ZB):
        top = tiles - ZB + z
        if len(edges) == 1:
            edges[0][z] = flux[jnp.where(sends_top, top, z)]
        else:
            edges[0][z], edges[1][z] = flux[z], flux[top]


def conduction_kernel(
    groups,
    ids,
    tiles,
    coefficient,
    storage,
    couplings,
    warmth,
    flux,
    below,
    above,
    heat,
    rest,
    gain,
):
    count = tiles.shape[0]
    width = flux.shape[2]
    own = lax.axis_index("therm")
    lowest = (own > 0).astype(F32)
    highest = (own < groups - 1).astype(F32)
    diag = coefficient[...].T
    gains = (time_increment / storage[...]).T
    for i in range(count):
        image = jnp.dot(joined(tiles, i), picked(flux, ids, i), preferred_element_type=F32)
        image = image + column(diag, i, width) * flux[i].astype(F32)
        if i < ZB:
            term = jnp.dot(couplings[i], below[i], preferred_element_type=F32)
            image = image + lowest * term
        if i >= count - ZB:
            z = i - (count - ZB)
            term = jnp.dot(couplings[ZB + z], above[z], preferred_element_type=F32)
            image = image + highest * term
        g = column(gains, i, width)
        gain[i] = g
        rest[i] = warmth[i].astype(F32) - g * image


def early_kernel(shifts, heat, gain, *refs):
    maps, soon = refs[:shifts], refs[shifts : 2 * shifts]
    rest, field, out = refs[2 * shifts + 2 : 2 * shifts + 5]
    spots, sem = refs[2 * shifts + 5 : -1], refs[-1]
    tiles, points = rest.shape[:2]
    sent = tiles - spots[0].shape[0]
    for i in range(tiles):
        rest[i] = rest[i] + gain[i] * heat[i]
    for g in range(shifts):
        for p in range(sent):
            j = maps[g][p]
            rest[j] = rest[j] + gain[j] * soon[g][p * points : (p + 1) * points].astype(F32)
    whole = pltpu.make_async_copy(rest, out, sem)
    whole.start()
    for g in range(shifts):
        for p in range(spots[g].shape[0]):
            spots[g][p] = maps[g][tiles - spots[g].shape[0] + p]
    whole.wait()


def late_kernel(shifts, gain, *refs):
    maps, late = refs[:shifts], refs[shifts : 2 * shifts]
    rest, out, sems = refs[2 * shifts], refs[2 * shifts + 2], refs[2 * shifts + 3]
    spots = late[0].shape[0]
    for g in range(shifts):
        for p in range(spots):
            j = maps[g][p]
            rest[j] = rest[j] + gain[j] * late[g][p].astype(F32)
    copies = []
    for g in range(shifts):
        for p in range(spots):
            j = maps[g][p]
            copies.append(pltpu.make_async_copy(rest.at[j], out.at[j], sems.at[g * spots + p]))
    for c in copies:
        c.start()
    for c in copies:
        c.wait()


def body(
    injected_amperage,
    voltage_self_admittance,
    voltage_coupling_tiles,
    voltage_partner_tile_ids,
    interface_tiles_per_level,
    interface_admittance,
    warmth_receiver_layer,
    warmth_receiver_tile,
    warmth_values,
    warmth_self_coefficient,
    warmth_coupling_tiles,
    warmth_partner_tile_ids,
    layer_boundary_couplings,
    substance_kind,
    reference_material_kappas,
    warmth_storage_per_point,
):
    blocks, points, regimes = injected_amperage.shape
    tiles = warmth_values.shape[0]
    levels, width = interface_tiles_per_level.shape
    links = voltage_partner_tile_ids.shape[1]
    groups = lax.axis_size("therm")
    shifts = groups - 1
    whole = (blocks, points, regimes)
    warm = (tiles, points, regimes)
    face = (width * points, regimes)
    late_spots = min(levels * width, tiles)
    early_spots = tiles - late_spots
    sent_rows = early_spots * points
    near_flops = 2 * blocks * links * points * points * regimes
    terms = pltpu.VMEM((levels * width, points, regimes), F32)
    dma = pltpu.SemaphoreType.DMA

    def exchange(faces, order):
        return [from_partner(faces[b], "elec", b) for b in order]

    far_first = list(range(levels))[::-1]
    near, *middle, far = range(levels)
    first_order, last_order = [far] + middle + [near], [near] + middle[::-1] + [far]

    amps, diag, face_ids, ids, layer, tile, *faces = call(
        functools.partial(start_kernel, levels),
        [
            (whole, BF16, VM),
            (voltage_self_admittance.shape, F32, VM),
            ((width, levels), I32, SM),
            ((links, blocks), I32, SM),
            ((1, blocks), I32, SM),
            ((blocks,), I32, SM),
        ]
        + [(face, BF16, VM)] * levels,
        on(
            HB,
            injected_amperage,
            voltage_self_admittance,
            interface_tiles_per_level.T,
            voltage_partner_tile_ids.T,
            warmth_receiver_layer.T,
            warmth_receiver_tile,
        ),
        "start",
        scratch=[dma((6,))],
    )
    order = first_order
    incoming = exchange(faces, order)

    packed, state, field, scale, warmth, kind, slot, rows = call(
        functools.partial(first_kernel, groups),
        [
            ((blocks, points, links * points), BF16, VM),
            (whole, F32, VM),
            (whole, BF16, VM),
            (whole, F32, VM),
            (warm, BF16, VM),
            (substance_kind.shape, I32, VM),
            ((blocks,), I32, SM),
            ((shifts, 16, regimes), BF16, VM),
        ],
        on(SM, ids, layer, tile, face_ids)
        + on(HB, voltage_coupling_tiles, warmth_values, substance_kind)
        + on(VM, amps, diag),
        "first",
        scratch=[
            pltpu.VMEM(voltage_coupling_tiles.shape, BF16),
            pltpu.VMEM(whole, BF16),
            pltpu.SMEM((tiles,), I32),
            pltpu.SMEM((tiles,), I32),
            dma((4,)),
            dma((2,)),
        ],
        flops=near_flops,
        limit=8 << 20,
    )
    for sweep_index in range(SWEEPS - 1):
        if sweep_index:
            last = sweep_index == SWEEPS - 2
            state, field, *for_heat = call(
                near_kernel,
                [(whole, F32, VM), (whole, BF16, VM)]
                + [((groups * tiles, points, regimes), F32, VM), (whole, F32, VM)] * last,
                on(SM, ids) + on(VM, packed, field, state, amps, scale),
                "near",
                flops=near_flops,
            )
        token = scale
        if sweep_index == 1:
            flux, *edges = call(
                flux_kernel,
                [(warm, BF16, VM)] + [((ZB, points, regimes), BF16, VM)] * min(2, shifts),
                on(ANY, field) + on(SM, reference_material_kappas) + on(VM, kind, warmth),
                "flux",
            )
            token = edges[0]
        if sweep_index < SWEEPS - 2:
            state, field, *faces = call(
                functools.partial(face_kernel, order),
                [(whole, F32, VM), (whole, BF16, VM)] + [(face, BF16, VM)] * levels,
                on(ANY, token)
                + on(SM, face_ids)
                + on(VM, interface_admittance, scale, *incoming, state, field),
                "face",
                aliases={levels + 4: 0, levels + 5: 1},
                scratch=[terms],
            )
            order = far_first
            incoming = exchange(faces, order)

    if groups == 2:
        below = above = lax.ppermute(edges[0], "therm", [(0, 1), (1, 0)])
    else:
        up = [(i, i + 1) for i in range(groups - 1)]
        above = lax.ppermute(edges[0], "therm", [(j, i) for i, j in up])
        below = lax.ppermute(edges[1], "therm", up)
    heat, diag = for_heat
    _, field, heat, soon, *faces = call(
        functools.partial(heat_kernel, order, early_spots),
        [
            (whole, F32, VM),
            (whole, BF16, VM),
            (heat.shape, F32, VM),
            ((shifts, sent_rows + rows.shape[1], regimes), BF16, VM),
        ]
        + [(face, BF16, VM)] * levels,
        on(ANY, above)
        + on(SM, slot, ids, face_ids)
        + on(VM, interface_admittance, scale, packed, diag, rows, *incoming)
        + on(VM, state, field, heat),
        "heat",
        aliases={9 + levels + n: n for n in range(3)},
        scratch=[terms],
        flops=near_flops,
    )
    routes = [[(i, (i + s) % groups) for i in range(groups)] for s in range(1, groups)]
    soon = [lax.ppermute(soon[s], "therm", routes[s]) for s in range(shifts)]
    maps = [x[sent_rows, :tiles].astype(I32) for x in soon]
    order = last_order
    incoming = exchange(faces, order)

    rest, gain = call(
        functools.partial(conduction_kernel, groups),
        [(warm, F32, VM), (warm, F32, VM)],
        on(SM, warmth_partner_tile_ids.T)
        + on(
            VM,
            warmth_coupling_tiles,
            warmth_self_coefficient,
            warmth_storage_per_point,
            layer_boundary_couplings,
            warmth,
            flux,
            below,
            above,
        )
        + on(ANY, heat),
        "conduction",
        flops=near_flops,
    )
    heat, field, late = call(
        functools.partial(heat_face_kernel, order),
        [
            ((groups * tiles, points, regimes), F32, VM),
            (whole, BF16, VM),
            ((shifts, late_spots, points, regimes), BF16, VM),
        ],
        on(SM, slot, face_ids) + on(VM, interface_admittance, *incoming, heat, field),
        "heat_face",
        aliases={levels + 3: 0, levels + 4: 1},
        scratch=[terms],
    )
    late = [lax.ppermute(late[s], "therm", routes[s]) for s in range(shifts)]
    rest, voltage_solution, out, *maps = call(
        functools.partial(early_kernel, shifts),
        [(warm, F32, VM), (whole, BF16, VM), (warm, F32, HB)] + [((late_spots,), I32, SM)] * shifts,
        on(VM, heat, gain) + on(SM, *maps) + on(VM, *soon, rest, field),
        "early",
        aliases={2 + 2 * shifts: 0, 3 + 2 * shifts: 1},
        scratch=[dma],
    )
    (advanced_warmth_values,) = call(
        functools.partial(late_kernel, shifts),
        [(warm, F32, HB)],
        on(VM, gain) + on(SM, *maps) + on(VM, *late, rest) + on(HB, out),
        "late",
        aliases={2 + 2 * shifts: 0},
        scratch=[dma((shifts * late_spots,))],
    )
    return (voltage_solution, advanced_warmth_values)


def solution(mesh):
    split = P(("elec", "therm"))
    return jax.shard_map(
        body,
        mesh=mesh,
        in_specs=(split,) * 14 + (P(), split),
        out_specs=(split, split),
        check_vma=False,
    )
```

```python
import functools

import jax
import jax.numpy as jnp
from jax import lax
from jax.experimental import pallas as pl
from jax.experimental.pallas import tpu as pltpu
from jax.sharding import PartitionSpec as P

SWEEPS = 5
ZB = 2

relax_factor = 0.8
time_increment = 0.5

F32 = jnp.float32
BF16 = jnp.bfloat16
I32 = jnp.int32
VM = pl.BlockSpec(memory_space=pltpu.VMEM)
SM = pl.BlockSpec(memory_space=pltpu.SMEM)
HB = pl.BlockSpec(memory_space=pltpu.HBM)
ANY = pl.BlockSpec(memory_space=pl.ANY)
SPACES = {id(VM): pltpu.VMEM, id(HB): pltpu.HBM, id(SM): pltpu.SMEM}
LIMIT = 4 << 20


def call(kernel, outs, ins, name, aliases={}, scratch=(), flops=0, limit=LIMIT):
    args = []
    for x, spec in ins:
        if spec is VM or spec is HB:
            x = pltpu.with_memory_space_constraint(x, SPACES[id(spec)])
        args.append(x)
    return pl.pallas_call(
        kernel,
        out_shape=[SPACES[id(spec)](shape, dtype) for shape, dtype, spec in outs],
        in_specs=[spec for _, spec in ins],
        out_specs=[spec for _, _, spec in outs],
        input_output_aliases=aliases,
        scratch_shapes=scratch,
        compiler_params=pltpu.CompilerParams(vmem_limit_bytes=limit),
        cost_estimate=pl.CostEstimate(flops=flops, bytes_accessed=0, transcendentals=0),
        name=name,
    )(*args)


def on(spec, *arrays):
    return [(x, spec) for x in arrays]


def from_partner(block, axis, bit):
    count = lax.axis_size(axis)
    route = []
    for low in range(count):
        high = low | 1 << bit
        if high != low and high < count:
            route += [(low, high), (high, low)]
    return lax.ppermute(block, axis, route)


def column(table, row, width):
    return jnp.broadcast_to(table[:, row : row + 1], (table.shape[0], width))


def joined(tiles_ref, row):
    return jnp.concatenate([tiles_ref[row, k] for k in range(tiles_ref.shape[1])], axis=1)


def picked(field_ref, ids_ref, row):
    return jnp.concatenate([field_ref[ids_ref[k, row]] for k in range(ids_ref.shape[0])], axis=0)


def start_kernel(levels, amps, diag, face_ids, *refs):
    small = refs[:3]
    amps_v, diag_v, face_ids_s = refs[3:6]
    small_s, faces, sems = refs[6:9], refs[9 : 9 + levels], refs[-1]
    pairs = [(face_ids, face_ids_s), (diag, diag_v), (amps, amps_v)]
    copies = [
        pltpu.make_async_copy(a, b, sems.at[n])
        for n, (a, b) in enumerate(pairs + list(zip(small, small_s)))
    ]
    for c in copies:
        c.start()
    copies[0].wait()
    copies[1].wait()
    chosen = [
        diag_v[pl.ds(face_ids_s[f, b], 1), :]
        for b in range(levels)
        for f in range(face_ids.shape[0])
    ]
    turned = (relax_factor / jnp.concatenate(chosen, axis=0)).T
    copies[2].wait()
    for b in range(levels):
        for f in range(face_ids.shape[0]):
            s = column(turned, b * face_ids.shape[0] + f, amps.shape[2])
            points = amps.shape[1]
            block = s * amps_v[face_ids_s[f, b]].astype(F32)
            faces[b][f * points : (f + 1) * points] = block.astype(BF16)
    for c in copies[3:]:
        c.wait()


def route(groups, layer, tile, face_ids, slot, rows, flag, place):
    own = lax.axis_index("therm")
    blocks, tiles = slot.shape[0], flag.shape[0]
    levels, width = face_ids.shape[1], face_ids.shape[0]
    early_slots = max(tiles - levels * width, 0)
    lane = lax.broadcasted_iota(I32, rows.shape[1:], 1)

    def away(i):
        a = layer[0, i] - own
        return jnp.where(a < 0, a + groups, a)

    def home(i, c):
        slot[i] = tile[i]
        return c

    lax.fori_loop(0, blocks, home, 0)
    for g in range(1, groups):

        def clear(j, c):
            flag[j] = 0
            return c

        def mark(i, c):
            j = tile[i]
            flag[j] = jnp.where(away(i) == g, 1, flag[j])
            return c

        def late(j, c):
            is_late = flag[j] == 2
            place[j] = jnp.where(is_late, c, 0)
            return c + is_late.astype(I32)

        def early(j, c):
            at, behind, row = c
            is_early = flag[j] == 1
            fits = at < early_slots
            pos = jnp.where(fits, at, behind)
            pos = jnp.where(is_early, pos, place[j])
            place[j] = pos
            used = flag[j] > 0
            row = jnp.where((lane == pos) & used, j, row)
            at = at + (is_early & fits).astype(I32)
            behind = behind + (is_early & jnp.logical_not(fits)).astype(I32)
            return at, behind, row

        def assign(i, c):
            slot[i] = jnp.where(away(i) == g, g * tiles + place[tile[i]], slot[i])
            return c

        lax.fori_loop(0, tiles, clear, 0)
        lax.fori_loop(0, blocks, mark, 0)
        for b in range(levels):
            for f in range(width):
                i = face_ids[f, b]
                j = tile[i]
                flag[j] = jnp.where(away(i) == g, 2, flag[j])
        behind = lax.fori_loop(0, tiles, late, early_slots)
        _, _, row = lax.fori_loop(
            0, tiles, early, (0, behind, jnp.zeros(rows.shape[1:], I32))
        )
        lax.fori_loop(0, blocks, assign, 0)
        rows[g - 1] = row.astype(F32).astype(BF16)


def first_kernel(groups, ids, layer, tile, face_ids, tiles, warmth, kind, amps, diag, *refs):
    packed, state_out, field_out, scale, warmth_v, kind_v, slot, rows = refs[:8]
    tiles_v, field, flag, place, sems, later_sems = refs[8:]
    blocks = packed.shape[0]
    step = blocks // sems.shape[0]
    copies = []
    later = [
        pltpu.make_async_copy(warmth, warmth_v, later_sems.at[0]),
        pltpu.make_async_copy(kind, kind_v, later_sems.at[1]),
    ]
    for p in range(0, blocks, step):
        part = pl.ds(p, step)
        copies.append(
            pltpu.make_async_copy(tiles.at[part], tiles_v.at[part], sems.at[p // step])
        )
    for c in copies + later:
        c.start()
    route(groups, layer, tile, face_ids, slot, rows, flag, place)
    turned = (relax_factor / diag[...]).T
    for i in range(blocks):
        s = column(turned, i, scale.shape[2])
        scale[i] = s
        field[i] = (s * amps[i].astype(F32)).astype(BF16)
    for i in range(blocks):
        if i % step == 0:
            copies[i // step].wait()
        row = joined(tiles_v, i)
        packed[i] = row
        image = jnp.dot(row, picked(field, ids, i), preferred_element_type=F32)
        a = amps[i].astype(F32)
        s = scale[i]
        x = s * a - relax_factor * field[i].astype(F32) + s * (a - image)
        state_out[i] = x
        field_out[i] = x.astype(BF16)
    for c in later:
        c.wait()


def near_kernel(ids, packed, field, state, amps, scale, state_out, field_out, *for_heat):
    for i in range(packed.shape[0]):
        image = jnp.dot(packed[i], picked(field, ids, i), preferred_element_type=F32)
        x = state[i] - relax_factor * field[i].astype(F32)
        x = x + scale[i] * (amps[i].astype(F32) - image)
        state_out[i] = x
        field_out[i] = x.astype(BF16)
    if for_heat:
        heat, diag = for_heat
        heat[...] = jnp.zeros(heat.shape, F32)
        for i in range(packed.shape[0]):
            diag[i] = relax_factor / scale[i]


def face_terms(levels, face_ids, admittance, incoming, terms):
    width, points = face_ids.shape[0], terms.shape[1]
    for b in range(levels):
        for f in range(width):
            block = incoming[b][f * points : (f + 1) * points]
            terms[b * width + f] = jnp.dot(
                admittance[b * width + f], block, preferred_element_type=F32
            )


def in_level_order(refs, order):
    return [refs[order.index(b)] for b in range(len(order))]


def update_faces(face_ids, admittance, scale, incoming, state, field, faces, terms):
    levels, width, points = len(faces), face_ids.shape[0], terms.shape[1]
    face_terms(levels, face_ids, admittance, incoming, terms)
    for b in range(levels):
        for f in range(width):
            i = face_ids[f, b]
            state[i] = state[i] - scale[i] * terms[b * width + f]
    for b in range(levels):
        for f in range(width):
            i = face_ids[f, b]
            x = state[i].astype(BF16)
            field[i] = x
            faces[b][f * points : (f + 1) * points] = x


def face_kernel(order, token, face_ids, admittance, scale, *refs):
    levels = len(order)
    incoming = in_level_order(refs[:levels], order)
    state, field = refs[levels + 2 : levels + 4]
    faces, terms = refs[levels + 4 : 2 * levels + 4], refs[-1]
    update_faces(face_ids, admittance, scale, incoming, state, field, faces, terms)


def heat_kernel(
    order, spots, token, slot, ids, face_ids, admittance, scale, packed, diag, rows, *refs
):
    levels = len(order)
    incoming = in_level_order(refs[:levels], order)
    state, field, heat, soon = refs[levels + 3 : levels + 7]
    faces, terms = refs[levels + 7 : 2 * levels + 7], refs[-1]
    groups, points = soon.shape[0] + 1, heat.shape[1]
    tiles = heat.shape[0] // groups
    update_faces(face_ids, admittance, scale, incoming, state, field, faces, terms)
    for i in range(packed.shape[0]):
        image = jnp.dot(packed[i], picked(field, ids, i), preferred_element_type=F32)
        v = field[i].astype(F32)
        s = slot[i]
        heat[s] = heat[s] + v * (diag[i] * v + image)
    for g in range(1, groups):
        blocks = [heat[g * tiles + p].astype(BF16) for p in range(spots)]
        for p, block in enumerate(blocks):
            soon[g - 1, p * points : (p + 1) * points] = block
        soon[g - 1, len(blocks) * points :] = rows[g - 1]


def heat_face_kernel(order, slot, face_ids, admittance, *refs):
    levels = len(order)
    incoming = in_level_order(refs[:levels], order)
    heat, field, late, terms = refs[levels + 2 :]
    groups, spots = late.shape[0] + 1, late.shape[1]
    tiles = heat.shape[0] // groups
    width = face_ids.shape[0]
    face_terms(levels, face_ids, admittance, incoming, terms)
    for b in range(levels):
        for f in range(width):
            i = face_ids[f, b]
            s = slot[i]
            heat[s] = heat[s] + field[i].astype(F32) * terms[b * width + f]
    for g in range(1, groups):
        late[g - 1] = heat[(g + 1) * tiles - spots : (g + 1) * tiles].astype(BF16)


def kappa_columns(kappas, kind):
    kinds = kind[...]
    kappa = jnp.zeros(kinds.shape, F32)
    for m in range(kappas.shape[0]):
        kappa = jnp.where(kinds == m, kappas[m], kappa)
    return kappa.T


def block_flux(kappa, warmth):
    w = warmth.astype(F32)
    return (kappa * (1.0 + 0.4 * jnp.tanh(w)) * w).astype(BF16)


def flux_kernel(token, kappas, kind, warmth, flux, *edges):
    turned = kappa_columns(kappas, kind)
    tiles, points, width = warmth.shape
    for i in range(tiles):
        flux[i] = block_flux(column(turned, i, width), warmth[i])
    sends_top = lax.axis_index("therm") == 0
    for z in range(ZB):
        top = tiles - ZB + z
        if len(edges) == 1:
            edges[0][z] = flux[jnp.where(sends_top, top, z)]
        else:
            edges[0][z], edges[1][z] = flux[z], flux[top]


def conduction_kernel(
    groups,
    ids,
    tiles,
    coefficient,
    storage,
    couplings,
    warmth,
    flux,
    below,
    above,
    heat,
    rest,
    gain,
):
    count = tiles.shape[0]
    width = flux.shape[2]
    own = lax.axis_index("therm")
    lowest = (own > 0).astype(F32)
    highest = (own < groups - 1).astype(F32)
    diag = coefficient[...].T
    gains = (time_increment / storage[...]).T
    for i in range(count):
        image = jnp.dot(joined(tiles, i), picked(flux, ids, i), preferred_element_type=F32)
        image = image + column(diag, i, width) * flux[i].astype(F32)
        if i < ZB:
            term = jnp.dot(couplings[i], below[i], preferred_element_type=F32)
            image = image + lowest * term
        if i >= count - ZB:
            z = i - (count - ZB)
            term = jnp.dot(couplings[ZB + z], above[z], preferred_element_type=F32)
            image = image + highest * term
        g = column(gains, i, width)
        gain[i] = g
        rest[i] = warmth[i].astype(F32) - g * image


def early_kernel(shifts, heat, gain, *refs):
    maps, soon = refs[:shifts], refs[shifts : 2 * shifts]
    rest, field, out = refs[2 * shifts + 2 : 2 * shifts + 5]
    spots, sem = refs[2 * shifts + 5 : -1], refs[-1]
    tiles, points = rest.shape[:2]
    sent = tiles - spots[0].shape[0]
    for i in range(tiles):
        rest[i] = rest[i] + gain[i] * heat[i]
    for g in range(shifts):
        for p in range(sent):
            j = maps[g][p]
            rest[j] = rest[j] + gain[j] * soon[g][p * points : (p + 1) * points].astype(F32)
    whole = pltpu.make_async_copy(rest, out, sem)
    whole.start()
    for g in range(shifts):
        for p in range(spots[g].shape[0]):
            spots[g][p] = maps[g][tiles - spots[g].shape[0] + p]
    whole.wait()


def late_kernel(shifts, gain, *refs):
    maps, late = refs[:shifts], refs[shifts : 2 * shifts]
    rest, out, sems = refs[2 * shifts], refs[2 * shifts + 2], refs[2 * shifts + 3]
    spots = late[0].shape[0]
    for g in range(shifts):
        for p in range(spots):
            j = maps[g][p]
            rest[j] = rest[j] + gain[j] * late[g][p].astype(F32)
    copies = []
    for g in range(shifts):
        for p in range(spots):
            j = maps[g][p]
            copies.append(pltpu.make_async_copy(rest.at[j], out.at[j], sems.at[g * spots + p]))
    for c in copies:
        c.start()
    for c in copies:
        c.wait()


def body(
    injected_amperage,
    voltage_self_admittance,
    voltage_coupling_tiles,
    voltage_partner_tile_ids,
    interface_tiles_per_level,
    interface_admittance,
    warmth_receiver_layer,
    warmth_receiver_tile,
    warmth_values,
    warmth_self_coefficient,
    warmth_coupling_tiles,
    warmth_partner_tile_ids,
    layer_boundary_couplings,
    substance_kind,
    reference_material_kappas,
    warmth_storage_per_point,
):
    blocks, points, regimes = injected_amperage.shape
    tiles = warmth_values.shape[0]
    levels, width = interface_tiles_per_level.shape
    links = voltage_partner_tile_ids.shape[1]
    groups = lax.axis_size("therm")
    shifts = groups - 1
    whole = (blocks, points, regimes)
    warm = (tiles, points, regimes)
    face = (width * points, regimes)
    late_spots = min(levels * width, tiles)
    early_spots = tiles - late_spots
    sent_rows = early_spots * points
    near_flops = 2 * blocks * links * points * points * regimes
    terms = pltpu.VMEM((levels * width, points, regimes), F32)
    dma = pltpu.SemaphoreType.DMA

    def exchange(faces, order):
        return [from_partner(faces[b], "elec", b) for b in order]

    far_first = list(range(levels))[::-1]
    near, *middle, far = range(levels)
    first_order, last_order = [far] + middle + [near], [near] + middle[::-1] + [far]

    amps, diag, face_ids, ids, layer, tile, *faces = call(
        functools.partial(start_kernel, levels),
        [
            (whole, BF16, VM),
            (voltage_self_admittance.shape, F32, VM),
            ((width, levels), I32, SM),
            ((links, blocks), I32, SM),
            ((1, blocks), I32, SM),
            ((blocks,), I32, SM),
        ]
        + [(face, BF16, VM)] * levels,
        on(
            HB,
            injected_amperage,
            voltage_self_admittance,
            interface_tiles_per_level.T,
            voltage_partner_tile_ids.T,
            warmth_receiver_layer.T,
            warmth_receiver_tile,
        ),
        "start",
        scratch=[dma((6,))],
    )
    order = first_order
    incoming = exchange(faces, order)

    packed, state, field, scale, warmth, kind, slot, rows = call(
        functools.partial(first_kernel, groups),
        [
            ((blocks, points, links * points), BF16, VM),
            (whole, F32, VM),
            (whole, BF16, VM),
            (whole, F32, VM),
            (warm, BF16, VM),
            (substance_kind.shape, I32, VM),
            ((blocks,), I32, SM),
            ((shifts, 16, regimes), BF16, VM),
        ],
        on(SM, ids, layer, tile, face_ids)
        + on(HB, voltage_coupling_tiles, warmth_values, substance_kind)
        + on(VM, amps, diag),
        "first",
        scratch=[
            pltpu.VMEM(voltage_coupling_tiles.shape, BF16),
            pltpu.VMEM(whole, BF16),
            pltpu.SMEM((tiles,), I32),
            pltpu.SMEM((tiles,), I32),
            dma((4,)),
            dma((2,)),
        ],
        flops=near_flops,
        limit=8 << 20,
    )
    for sweep_index in range(SWEEPS - 1):
        if sweep_index:
            last = sweep_index == SWEEPS - 2
            state, field, *for_heat = call(
                near_kernel,
                [(whole, F32, VM), (whole, BF16, VM)]
                + [((groups * tiles, points, regimes), F32, VM), (whole, F32, VM)] * last,
                on(SM, ids) + on(VM, packed, field, state, amps, scale),
                "near",
                flops=near_flops,
            )
        token = scale
        if sweep_index == 1:
            flux, *edges = call(
                flux_kernel,
                [(warm, BF16, VM)] + [((ZB, points, regimes), BF16, VM)] * min(2, shifts),
                on(ANY, field) + on(SM, reference_material_kappas) + on(VM, kind, warmth),
                "flux",
            )
            token = edges[0]
        if sweep_index < SWEEPS - 2:
            state, field, *faces = call(
                functools.partial(face_kernel, order),
                [(whole, F32, VM), (whole, BF16, VM)] + [(face, BF16, VM)] * levels,
                on(ANY, token)
                + on(SM, face_ids)
                + on(VM, interface_admittance, scale, *incoming, state, field),
                "face",
                aliases={levels + 4: 0, levels + 5: 1},
                scratch=[terms],
            )
            order = far_first
            incoming = exchange(faces, order)

    if groups == 2:
        below = above = lax.ppermute(edges[0], "therm", [(0, 1), (1, 0)])
    else:
        up = [(i, i + 1) for i in range(groups - 1)]
        above = lax.ppermute(edges[0], "therm", [(j, i) for i, j in up])
        below = lax.ppermute(edges[1], "therm", up)
    heat, diag = for_heat
    _, field, heat, soon, *faces = call(
        functools.partial(heat_kernel, order, early_spots),
        [
            (whole, F32, VM),
            (whole, BF16, VM),
            (heat.shape, F32, VM),
            ((shifts, sent_rows + rows.shape[1], regimes), BF16, VM),
        ]
        + [(face, BF16, VM)] * levels,
        on(ANY, above)
        + on(SM, slot, ids, face_ids)
        + on(VM, interface_admittance, scale, packed, diag, rows, *incoming)
        + on(VM, state, field, heat),
        "heat",
        aliases={9 + levels + n: n for n in range(3)},
        scratch=[terms],
        flops=near_flops,
    )
    routes = [[(i, (i + s) % groups) for i in range(groups)] for s in range(1, groups)]
    soon = [lax.ppermute(soon[s], "therm", routes[s]) for s in range(shifts)]
    maps = [x[sent_rows, :tiles].astype(I32) for x in soon]
    order = last_order
    incoming = exchange(faces, order)

    rest, gain = call(
        functools.partial(conduction_kernel, groups),
        [(warm, F32, VM), (warm, F32, VM)],
        on(SM, warmth_partner_tile_ids.T)
        + on(
            VM,
            warmth_coupling_tiles,
            warmth_self_coefficient,
            warmth_storage_per_point,
            layer_boundary_couplings,
            warmth,
            flux,
            below,
            above,
        )
        + on(ANY, heat),
        "conduction",
        flops=near_flops,
    )
    heat, field, late = call(
        functools.partial(heat_face_kernel, order),
        [
            ((groups * tiles, points, regimes), F32, VM),
            (whole, BF16, VM),
            ((shifts, late_spots, points, regimes), BF16, VM),
        ],
        on(SM, slot, face_ids) + on(VM, interface_admittance, *incoming, heat, field),
        "heat_face",
        aliases={levels + 3: 0, levels + 4: 1},
        scratch=[terms],
    )
    late = [lax.ppermute(late[s], "therm", routes[s]) for s in range(shifts)]
    rest, voltage_solution, out, *maps = call(
        functools.partial(early_kernel, shifts),
        [(warm, F32, VM), (whole, BF16, VM), (warm, F32, HB)] + [((late_spots,), I32, SM)] * shifts,
        on(VM, heat, gain) + on(SM, *maps) + on(VM, *soon, rest, field),
        "early",
        aliases={2 + 2 * shifts: 0, 3 + 2 * shifts: 1},
        scratch=[dma],
    )
    (advanced_warmth_values,) = call(
        functools.partial(late_kernel, shifts),
        [(warm, F32, HB)],
        on(VM, gain) + on(SM, *maps) + on(VM, *late, rest) + on(HB, out),
        "late",
        aliases={2 + 2 * shifts: 0},
        scratch=[dma((shifts * late_spots,))],
    )
    return (voltage_solution, advanced_warmth_values)


def solution(mesh):
    split = P(("elec", "therm"))
    return jax.shard_map(
        body,
        mesh=mesh,
        in_specs=(split,) * 14 + (P(), split),
        out_specs=(split, split),
        check_vma=False,
    )
```

```python
import functools

import jax
import jax.numpy as jnp
from jax import lax
from jax.experimental import pallas as pl
from jax.experimental.pallas import tpu as pltpu
from jax.sharding import PartitionSpec as P

SWEEPS = 5
ZB = 2

relax_factor = 0.8
time_increment = 0.5

F32 = jnp.float32
BF16 = jnp.bfloat16
I32 = jnp.int32
VM = pl.BlockSpec(memory_space=pltpu.VMEM)
SM = pl.BlockSpec(memory_space=pltpu.SMEM)
HB = pl.BlockSpec(memory_space=pltpu.HBM)
ANY = pl.BlockSpec(memory_space=pl.ANY)
SPACES = {id(VM): pltpu.VMEM, id(HB): pltpu.HBM, id(SM): pltpu.SMEM}
LIMIT = 4 << 20


def call(kernel, outs, ins, name, aliases={}, scratch=(), flops=0, limit=LIMIT):
    args = []
    for x, spec in ins:
        if spec is VM or spec is HB:
            x = pltpu.with_memory_space_constraint(x, SPACES[id(spec)])
        args.append(x)
    return pl.pallas_call(
        kernel,
        out_shape=[SPACES[id(spec)](shape, dtype) for shape, dtype, spec in outs],
        in_specs=[spec for _, spec in ins],
        out_specs=[spec for _, _, spec in outs],
        input_output_aliases=aliases,
        scratch_shapes=scratch,
        compiler_params=pltpu.CompilerParams(vmem_limit_bytes=limit),
        cost_estimate=pl.CostEstimate(flops=flops, bytes_accessed=0, transcendentals=0),
        name=name,
    )(*args)


def on(spec, *arrays):
    return [(x, spec) for x in arrays]


def from_partner(block, axis, bit):
    count = lax.axis_size(axis)
    route = []
    for low in range(count):
        high = low | 1 << bit
        if high != low and high < count:
            route += [(low, high), (high, low)]
    return lax.ppermute(block, axis, route)


def column(table, row, width):
    return jnp.broadcast_to(table[:, row : row + 1], (table.shape[0], width))


def joined(tiles_ref, row):
    return jnp.concatenate([tiles_ref[row, k] for k in range(tiles_ref.shape[1])], axis=1)


def picked(field_ref, ids_ref, row):
    return jnp.concatenate([field_ref[ids_ref[k, row]] for k in range(ids_ref.shape[0])], axis=0)


def start_kernel(levels, amps, diag, face_ids, *refs):
    small = refs[:3]
    amps_v, diag_v, face_ids_s = refs[3:6]
    small_s, faces, sems = refs[6:9], refs[9 : 9 + levels], refs[-1]
    pairs = [(face_ids, face_ids_s), (diag, diag_v), (amps, amps_v)]
    copies = [
        pltpu.make_async_copy(a, b, sems.at[n])
        for n, (a, b) in enumerate(pairs + list(zip(small, small_s)))
    ]
    for c in copies:
        c.start()
    copies[0].wait()
    copies[1].wait()
    scale = relax_factor / diag_v[...]
    rows = lax.broadcasted_iota(I32, scale.shape, 0)
    chosen = []
    for b in range(levels):
        for f in range(face_ids.shape[0]):
            mine = jnp.where(rows == face_ids_s[f, b], scale, 0.0)
            chosen.append(jnp.sum(mine, axis=0, keepdims=True))
    turned = jnp.concatenate(chosen, axis=0).T
    copies[2].wait()
    for b in range(levels):
        for f in range(face_ids.shape[0]):
            s = column(turned, b * face_ids.shape[0] + f, amps.shape[2])
            points = amps.shape[1]
            block = s * amps_v[face_ids_s[f, b]].astype(F32)
            faces[b][f * points : (f + 1) * points] = block.astype(BF16)
    for c in copies[3:]:
        c.wait()


def route(groups, layer, tile, face_ids, slot, rows, flag, place):
    own = lax.axis_index("therm")
    blocks, tiles = slot.shape[0], flag.shape[0]
    levels, width = face_ids.shape[1], face_ids.shape[0]
    early_slots = max(tiles - levels * width, 0)
    lane = lax.broadcasted_iota(I32, rows.shape[1:], 1)

    def away(i):
        a = layer[0, i] - own
        return jnp.where(a < 0, a + groups, a)

    def home(i, c):
        slot[i] = tile[i]
        return c

    lax.fori_loop(0, blocks, home, 0)
    for g in range(1, groups):

        def clear(j, c):
            flag[j] = 0
            return c

        def mark(i, c):
            j = tile[i]
            flag[j] = jnp.where(away(i) == g, 1, flag[j])
            return c

        def late(j, c):
            is_late = flag[j] == 2
            place[j] = jnp.where(is_late, c, 0)
            return c + is_late.astype(I32)

        def early(j, c):
            at, behind, row = c
            is_early = flag[j] == 1
            fits = at < early_slots
            pos = jnp.where(fits, at, behind)
            pos = jnp.where(is_early, pos, place[j])
            place[j] = pos
            used = flag[j] > 0
            row = jnp.where((lane == pos) & used, j, row)
            at = at + (is_early & fits).astype(I32)
            behind = behind + (is_early & jnp.logical_not(fits)).astype(I32)
            return at, behind, row

        def assign(i, c):
            slot[i] = jnp.where(away(i) == g, g * tiles + place[tile[i]], slot[i])
            return c

        lax.fori_loop(0, tiles, clear, 0)
        lax.fori_loop(0, blocks, mark, 0)
        for b in range(levels):
            for f in range(width):
                i = face_ids[f, b]
                j = tile[i]
                flag[j] = jnp.where(away(i) == g, 2, flag[j])
        behind = lax.fori_loop(0, tiles, late, early_slots)
        _, _, row = lax.fori_loop(
            0, tiles, early, (0, behind, jnp.zeros(rows.shape[1:], I32))
        )
        lax.fori_loop(0, blocks, assign, 0)
        rows[g - 1] = row.astype(F32).astype(BF16)


def first_kernel(groups, ids, layer, tile, face_ids, tiles, warmth, kind, amps, diag, *refs):
    packed, state_out, field_out, scale, warmth_v, kind_v, slot, rows = refs[:8]
    tiles_v, field, flag, place, sems, later_sems = refs[8:]
    blocks = packed.shape[0]
    step = blocks // sems.shape[0]
    copies = []
    later = [
        pltpu.make_async_copy(warmth, warmth_v, later_sems.at[0]),
        pltpu.make_async_copy(kind, kind_v, later_sems.at[1]),
    ]
    for p in range(0, blocks, step):
        part = pl.ds(p, step)
        copies.append(
            pltpu.make_async_copy(tiles.at[part], tiles_v.at[part], sems.at[p // step])
        )
    for c in copies + later:
        c.start()
    route(groups, layer, tile, face_ids, slot, rows, flag, place)
    turned = (relax_factor / diag[...]).T
    for i in range(blocks):
        s = column(turned, i, scale.shape[2])
        scale[i] = s
        field[i] = (s * amps[i].astype(F32)).astype(BF16)
    for i in range(blocks):
        if i % step == 0:
            copies[i // step].wait()
        row = joined(tiles_v, i)
        packed[i] = row
        image = jnp.dot(row, picked(field, ids, i), preferred_element_type=F32)
        a = amps[i].astype(F32)
        s = scale[i]
        x = s * a - relax_factor * field[i].astype(F32) + s * (a - image)
        state_out[i] = x
        field_out[i] = x.astype(BF16)
    for c in later:
        c.wait()


def near_kernel(ids, packed, field, state, amps, scale, state_out, field_out, *for_heat):
    for i in range(packed.shape[0]):
        image = jnp.dot(packed[i], picked(field, ids, i), preferred_element_type=F32)
        x = state[i] - relax_factor * field[i].astype(F32)
        x = x + scale[i] * (amps[i].astype(F32) - image)
        state_out[i] = x
        field_out[i] = x.astype(BF16)
    if for_heat:
        heat, diag = for_heat
        heat[...] = jnp.zeros(heat.shape, F32)
        for i in range(packed.shape[0]):
            diag[i] = relax_factor / scale[i]


def face_terms(levels, face_ids, admittance, incoming, terms):
    width, points = face_ids.shape[0], terms.shape[1]
    for b in range(levels):
        for f in range(width):
            block = incoming[b][f * points : (f + 1) * points]
            terms[b * width + f] = jnp.dot(
                admittance[b * width + f], block, preferred_element_type=F32
            )


def in_level_order(refs, order):
    return [refs[order.index(b)] for b in range(len(order))]


def update_faces(face_ids, admittance, scale, incoming, state, field, faces, terms):
    levels, width, points = len(faces), face_ids.shape[0], terms.shape[1]
    face_terms(levels, face_ids, admittance, incoming, terms)
    for b in range(levels):
        for f in range(width):
            i = face_ids[f, b]
            state[i] = state[i] - scale[i] * terms[b * width + f]
    for b in range(levels):
        for f in range(width):
            i = face_ids[f, b]
            x = state[i].astype(BF16)
            field[i] = x
            faces[b][f * points : (f + 1) * points] = x


def face_kernel(order, token, face_ids, admittance, scale, *refs):
    levels = len(order)
    incoming = in_level_order(refs[:levels], order)
    state, field = refs[levels + 2 : levels + 4]
    faces, terms = refs[levels + 4 : 2 * levels + 4], refs[-1]
    update_faces(face_ids, admittance, scale, incoming, state, field, faces, terms)


def heat_kernel(
    order, spots, token, slot, ids, face_ids, admittance, scale, packed, diag, rows, *refs
):
    levels = len(order)
    incoming = in_level_order(refs[:levels], order)
    state, field, heat, soon = refs[levels + 3 : levels + 7]
    faces, terms, made = refs[levels + 7 : 2 * levels + 7], refs[-2], refs[-1]
    groups, points = soon.shape[0] + 1, heat.shape[1]
    tiles = heat.shape[0] // groups
    update_faces(face_ids, admittance, scale, incoming, state, field, faces, terms)
    for i in range(packed.shape[0]):
        image = jnp.dot(packed[i], picked(field, ids, i), preferred_element_type=F32)
        v = field[i].astype(F32)
        made[i] = v * (diag[i] * v + image)
    for i in range(packed.shape[0]):
        s = slot[i]
        heat[s] = heat[s] + made[i]
    for g in range(1, groups):
        blocks = [heat[g * tiles + p].astype(BF16) for p in range(spots)]
        for p, block in enumerate(blocks):
            soon[g - 1, p * points : (p + 1) * points] = block
        soon[g - 1, len(blocks) * points :] = rows[g - 1]


def heat_face_kernel(order, slot, face_ids, admittance, *refs):
    levels = len(order)
    incoming = in_level_order(refs[:levels], order)
    heat, field, late, terms = refs[levels + 2 :]
    groups, spots = late.shape[0] + 1, late.shape[1]
    tiles = heat.shape[0] // groups
    width = face_ids.shape[0]
    face_terms(levels, face_ids, admittance, incoming, terms)
    for b in range(levels):
        for f in range(width):
            i = face_ids[f, b]
            s = slot[i]
            heat[s] = heat[s] + field[i].astype(F32) * terms[b * width + f]
    for g in range(1, groups):
        late[g - 1] = heat[(g + 1) * tiles - spots : (g + 1) * tiles].astype(BF16)


def kappa_columns(kappas, kind):
    kinds = kind[...]
    kappa = jnp.zeros(kinds.shape, F32)
    for m in range(kappas.shape[0]):
        kappa = jnp.where(kinds == m, kappas[m], kappa)
    return kappa.T


def block_flux(kappa, warmth):
    w = warmth.astype(F32)
    return (kappa * (1.0 + 0.4 * jnp.tanh(w)) * w).astype(BF16)


def flux_kernel(token, kappas, kind, warmth, flux, *edges):
    turned = kappa_columns(kappas, kind)
    tiles, points, width = warmth.shape
    for i in range(tiles):
        flux[i] = block_flux(column(turned, i, width), warmth[i])
    sends_top = lax.axis_index("therm") == 0
    for z in range(ZB):
        top = tiles - ZB + z
        if len(edges) == 1:
            edges[0][z] = flux[jnp.where(sends_top, top, z)]
        else:
            edges[0][z], edges[1][z] = flux[z], flux[top]


def conduction_kernel(
    groups,
    ids,
    tiles,
    coefficient,
    storage,
    couplings,
    warmth,
    flux,
    below,
    above,
    heat,
    rest,
    gain,
):
    count = tiles.shape[0]
    width = flux.shape[2]
    own = lax.axis_index("therm")
    lowest = (own > 0).astype(F32)
    highest = (own < groups - 1).astype(F32)
    diag = coefficient[...].T
    gains = (time_increment / storage[...]).T
    for i in range(count):
        image = jnp.dot(joined(tiles, i), picked(flux, ids, i), preferred_element_type=F32)
        image = image + column(diag, i, width) * flux[i].astype(F32)
        if i < ZB:
            term = jnp.dot(couplings[i], below[i], preferred_element_type=F32)
            image = image + lowest * term
        if i >= count - ZB:
            z = i - (count - ZB)
            term = jnp.dot(couplings[ZB + z], above[z], preferred_element_type=F32)
            image = image + highest * term
        g = column(gains, i, width)
        gain[i] = g
        rest[i] = warmth[i].astype(F32) - g * image


def early_kernel(shifts, heat, gain, *refs):
    maps, soon = refs[:shifts], refs[shifts : 2 * shifts]
    rest, field, out = refs[2 * shifts + 2 : 2 * shifts + 5]
    spots, sem = refs[2 * shifts + 5 : -1], refs[-1]
    tiles, points = rest.shape[:2]
    sent = tiles - spots[0].shape[0]
    for i in range(tiles):
        rest[i] = rest[i] + gain[i] * heat[i]
    for g in range(shifts):
        for p in range(sent):
            j = maps[g][p]
            rest[j] = rest[j] + gain[j] * soon[g][p * points : (p + 1) * points].astype(F32)
    whole = pltpu.make_async_copy(rest, out, sem)
    whole.start()
    for g in range(shifts):
        for p in range(spots[g].shape[0]):
            spots[g][p] = maps[g][tiles - spots[g].shape[0] + p]
    whole.wait()


def late_kernel(shifts, gain, *refs):
    maps, late = refs[:shifts], refs[shifts : 2 * shifts]
    rest, out, sems = refs[2 * shifts], refs[2 * shifts + 2], refs[2 * shifts + 3]
    spots = late[0].shape[0]
    for g in range(shifts):
        for p in range(spots):
            j = maps[g][p]
            rest[j] = rest[j] + gain[j] * late[g][p].astype(F32)
    copies = []
    for g in range(shifts):
        for p in range(spots):
            j = maps[g][p]
            copies.append(pltpu.make_async_copy(rest.at[j], out.at[j], sems.at[g * spots + p]))
    for c in copies:
        c.start()
    for c in copies:
        c.wait()


def body(
    injected_amperage,
    voltage_self_admittance,
    voltage_coupling_tiles,
    voltage_partner_tile_ids,
    interface_tiles_per_level,
    interface_admittance,
    warmth_receiver_layer,
    warmth_receiver_tile,
    warmth_values,
    warmth_self_coefficient,
    warmth_coupling_tiles,
    warmth_partner_tile_ids,
    layer_boundary_couplings,
    substance_kind,
    reference_material_kappas,
    warmth_storage_per_point,
):
    blocks, points, regimes = injected_amperage.shape
    tiles = warmth_values.shape[0]
    levels, width = interface_tiles_per_level.shape
    links = voltage_partner_tile_ids.shape[1]
    groups = lax.axis_size("therm")
    shifts = groups - 1
    whole = (blocks, points, regimes)
    warm = (tiles, points, regimes)
    face = (width * points, regimes)
    late_spots = min(levels * width, tiles)
    early_spots = tiles - late_spots
    sent_rows = early_spots * points
    near_flops = 2 * blocks * links * points * points * regimes
    terms = pltpu.VMEM((levels * width, points, regimes), F32)
    dma = pltpu.SemaphoreType.DMA

    def exchange(faces, order):
        return [from_partner(faces[b], "elec", b) for b in order]

    far_first = list(range(levels))[::-1]
    near, *middle, far = range(levels)
    first_order, last_order = [far] + middle + [near], [near] + middle[::-1] + [far]

    amps, diag, face_ids, ids, layer, tile, *faces = call(
        functools.partial(start_kernel, levels),
        [
            (whole, BF16, VM),
            (voltage_self_admittance.shape, F32, VM),
            ((width, levels), I32, SM),
            ((links, blocks), I32, SM),
            ((1, blocks), I32, SM),
            ((blocks,), I32, SM),
        ]
        + [(face, BF16, VM)] * levels,
        on(
            HB,
            injected_amperage,
            voltage_self_admittance,
            interface_tiles_per_level.T,
            voltage_partner_tile_ids.T,
            warmth_receiver_layer.T,
            warmth_receiver_tile,
        ),
        "start",
        scratch=[dma((6,))],
    )
    order = first_order
    incoming = exchange(faces, order)

    packed, state, field, scale, warmth, kind, slot, rows = call(
        functools.partial(first_kernel, groups),
        [
            ((blocks, points, links * points), BF16, VM),
            (whole, F32, VM),
            (whole, BF16, VM),
            (whole, F32, VM),
            (warm, BF16, VM),
            (substance_kind.shape, I32, VM),
            ((blocks,), I32, SM),
            ((shifts, 16, regimes), BF16, VM),
        ],
        on(SM, ids, layer, tile, face_ids)
        + on(HB, voltage_coupling_tiles, warmth_values, substance_kind)
        + on(VM, amps, diag),
        "first",
        scratch=[
            pltpu.VMEM(voltage_coupling_tiles.shape, BF16),
            pltpu.VMEM(whole, BF16),
            pltpu.SMEM((tiles,), I32),
            pltpu.SMEM((tiles,), I32),
            dma((4,)),
            dma((2,)),
        ],
        flops=near_flops,
        limit=8 << 20,
    )
    for sweep_index in range(SWEEPS - 1):
        if sweep_index:
            last = sweep_index == SWEEPS - 2
            state, field, *for_heat = call(
                near_kernel,
                [(whole, F32, VM), (whole, BF16, VM)]
                + [((groups * tiles, points, regimes), F32, VM), (whole, F32, VM)] * last,
                on(SM, ids) + on(VM, packed, field, state, amps, scale),
                "near",
                flops=near_flops,
            )
        token = scale
        if sweep_index == 1:
            flux, *edges = call(
                flux_kernel,
                [(warm, BF16, VM)] + [((ZB, points, regimes), BF16, VM)] * min(2, shifts),
                on(ANY, field) + on(SM, reference_material_kappas) + on(VM, kind, warmth),
                "flux",
            )
            token = edges[0]
        if sweep_index < SWEEPS - 2:
            state, field, *faces = call(
                functools.partial(face_kernel, order),
                [(whole, F32, VM), (whole, BF16, VM)] + [(face, BF16, VM)] * levels,
                on(ANY, token)
                + on(SM, face_ids)
                + on(VM, interface_admittance, scale, *incoming, state, field),
                "face",
                aliases={levels + 4: 0, levels + 5: 1},
                scratch=[terms],
            )
            order = far_first
            incoming = exchange(faces, order)

    if groups == 2:
        below = above = lax.ppermute(edges[0], "therm", [(0, 1), (1, 0)])
    else:
        up = [(i, i + 1) for i in range(groups - 1)]
        above = lax.ppermute(edges[0], "therm", [(j, i) for i, j in up])
        below = lax.ppermute(edges[1], "therm", up)
    heat, diag = for_heat
    _, field, heat, soon, *faces = call(
        functools.partial(heat_kernel, order, early_spots),
        [
            (whole, F32, VM),
            (whole, BF16, VM),
            (heat.shape, F32, VM),
            ((shifts, sent_rows + rows.shape[1], regimes), BF16, VM),
        ]
        + [(face, BF16, VM)] * levels,
        on(ANY, above)
        + on(SM, slot, ids, face_ids)
        + on(VM, interface_admittance, scale, packed, diag, rows, *incoming)
        + on(VM, state, field, heat),
        "heat",
        aliases={9 + levels + n: n for n in range(3)},
        scratch=[terms, pltpu.VMEM(whole, F32)],
        flops=near_flops,
    )
    routes = [[(i, (i + s) % groups) for i in range(groups)] for s in range(1, groups)]
    soon = [lax.ppermute(soon[s], "therm", routes[s]) for s in range(shifts)]
    maps = [x[sent_rows, :tiles].astype(I32) for x in soon]
    order = last_order
    incoming = exchange(faces, order)

    rest, gain = call(
        functools.partial(conduction_kernel, groups),
        [(warm, F32, VM), (warm, F32, VM)],
        on(SM, warmth_partner_tile_ids.T)
        + on(
            VM,
            warmth_coupling_tiles,
            warmth_self_coefficient,
            warmth_storage_per_point,
            layer_boundary_couplings,
            warmth,
            flux,
            below,
            above,
        )
        + on(ANY, heat),
        "conduction",
        flops=near_flops,
    )
    heat, field, late = call(
        functools.partial(heat_face_kernel, order),
        [
            ((groups * tiles, points, regimes), F32, VM),
            (whole, BF16, VM),
            ((shifts, late_spots, points, regimes), BF16, VM),
        ],
        on(SM, slot, face_ids) + on(VM, interface_admittance, *incoming, heat, field),
        "heat_face",
        aliases={levels + 3: 0, levels + 4: 1},
        scratch=[terms],
    )
    late = [lax.ppermute(late[s], "therm", routes[s]) for s in range(shifts)]
    rest, voltage_solution, out, *maps = call(
        functools.partial(early_kernel, shifts),
        [(warm, F32, VM), (whole, BF16, VM), (warm, F32, HB)] + [((late_spots,), I32, SM)] * shifts,
        on(VM, heat, gain) + on(SM, *maps) + on(VM, *soon, rest, field),
        "early",
        aliases={2 + 2 * shifts: 0, 3 + 2 * shifts: 1},
        scratch=[dma],
    )
    (advanced_warmth_values,) = call(
        functools.partial(late_kernel, shifts),
        [(warm, F32, HB)],
        on(VM, gain) + on(SM, *maps) + on(VM, *late, rest) + on(HB, out),
        "late",
        aliases={2 + 2 * shifts: 0},
        scratch=[dma((shifts * late_spots,))],
    )
    return (voltage_solution, advanced_warmth_values)


def solution(mesh):
    split = P(("elec", "therm"))
    return jax.shard_map(
        body,
        mesh=mesh,
        in_specs=(split,) * 14 + (P(), split),
        out_specs=(split, split),
        check_vma=False,
    )
```
